256 devices in a mesh: ctx: 128 (over z, y_hi, x, core), head: 2 (over y_lo).
Axes of the slice: x: 4, y: 4 (y_hi: 2, y_lo: 2; y = y_hi * 2 + y_lo), z: 8, core: 2. Of those that a mesh axis runs over, the one named last changes fastest.
Arguments:
- teacher_queries: bfloat16 [65536, 4096], P('ctx', 'head'), may hold values from -13.5 to 13.5
- teacher_keys: bfloat16 [65536, 1024], P('ctx', 'head'), may hold values from -6 to 6
- query_projection: float32 [32, 128, 128], P('head'), may hold values from -0.5 to 0.5
- key_projection: float32 [8, 384, 128], P('head'), may hold values from -0.3125 to 0.3125
- block_offsets: int32 [1024, 24], P('ctx'), may hold values from 0 to 24, as said below
- valid_counts: int32 [1024], P('ctx'), may hold values from 1 to 24, as said below
Outputs:
- query_gradient: float32 [32, 128, 128], P('head')
- key_gradient: float32 [8, 384, 128], P('head')
- mean_divergence: float32 [], replicated
The draws below stay inside these ranges and needn't reach their ends.
Inputs may be any that keep to these rules, and one draw needn't show every extreme that they name: `block_offsets`: each row holds distinct offsets, the first of them 0 (a block's own diagonal block); the largest offset is reached in every draw. `valid_counts`: both ends are reached in every draw.
All inputs are finite; a program needn't handle non-finite values.
Results may differ from the reference program's by a relative error of at most 0.0003.
Values may be sent and summed in bfloat16 or wider, within the bound.
No kernel may reach another device: no remote copies, remote signals or barrier semaphores. Data moves between devices by JAX's collectives and lax.ppermute only.
A program may use at most 64 MiB of HBM per device.

```python
import math
import jax
import jax.numpy as jnp
from jax import lax

HEADS = 32
KV_HEADS = 8
HEAD_DIM = 128
GATE_WIDTH = 128
BLOCK = 64
CAND = 24
REACH = 4
QB_DEV = 8
TOKENS = 65536
QBLOCKS = 1024
N_CTX = 128


def paired_draw(key):
    base = jax.random.fold_in(key, 11)
    group_size = HEADS // KV_HEADS
    keys_float = jax.random.normal(jax.random.fold_in(base, 1), (TOKENS, KV_HEADS, HEAD_DIM), jnp.float32)
    queries_float = jax.random.normal(jax.random.fold_in(base, 2), (TOKENS, KV_HEADS, group_size, HEAD_DIM), jnp.float32)
    keys_float = jnp.clip(keys_float, -6.0, 6.0)
    queries_float = jnp.clip(queries_float, -6.0, 6.0)
    return (queries_float.reshape(TOKENS, HEADS * HEAD_DIM), keys_float.reshape(TOKENS, KV_HEADS * HEAD_DIM))


def draw_teacher_queries(key, part):
    return paired_draw(key)[0].astype(jnp.bfloat16)


def draw_teacher_keys(key, part):
    return paired_draw(key)[1].astype(jnp.bfloat16)


def draw_block_offsets(key, part):
    span_max = (REACH - 1) * QB_DEV
    row_keys = jax.random.split(jax.random.fold_in(key, 21), QBLOCKS)
    orders = jax.vmap(lambda one_key: jax.random.permutation(one_key, span_max) + 1)(row_keys)
    picked = orders[:, :CAND - 1].astype(jnp.int32)
    row_index = jnp.arange(QBLOCKS)
    needed = (row_index % QB_DEV == 0) & jnp.logical_not(jnp.any(picked == span_max, axis=1))
    last_slot = jnp.where(needed, span_max, picked[:, CAND - 2]).astype(jnp.int32)
    zeros_col = jnp.zeros((QBLOCKS, 1), jnp.int32)
    return jnp.concatenate([zeros_col, picked[:, :CAND - 2], last_slot[:, None]], axis=1).astype(jnp.int32)


def draw_valid_counts(key, part):
    counts = jax.random.randint(jax.random.fold_in(key, 31), (QBLOCKS,), 1, CAND + 1)
    row_index = jnp.arange(QBLOCKS)
    counts = jnp.where(row_index % QB_DEV == 0, CAND, counts)
    counts = jnp.where(row_index % QB_DEV == 1, 1, counts)
    return counts.astype(jnp.int32)


def block_levels(rng, dims, pieces, low, high):
    loudness = 1.0
    for dim, shards_of in pieces:
        steps = jax.random.uniform(jax.random.fold_in(jax.random.fold_in(rng, 6), dim), (shards_of,), jnp.float32, low / len(pieces), high / len(pieces))
        loudness = loudness * jnp.repeat(jnp.exp(steps), dims[dim] // shards_of).reshape((-1,) + (1,) * (len(dims) - 1 - dim))
    return loudness


def gaussian(key, shape, scale, bound, pieces=(), kind=jnp.bfloat16):
    array = scale * jax.random.normal(key, shape, jnp.float32)
    if pieces:
        array = array * block_levels(key, shape, pieces, -0.22, 0.18)
    return jnp.clip(array, -bound, bound).astype(kind)


def setup_inputs(seed: int = 0) -> dict:
    arg_keys = jax.random.split(jax.random.key(seed), 7)
    teacher_queries = draw_teacher_queries(jax.random.fold_in(arg_keys[6], 71), 0)
    teacher_keys = draw_teacher_keys(jax.random.fold_in(arg_keys[6], 71), 0)
    query_projection = gaussian(arg_keys[2], (HEADS, HEAD_DIM, GATE_WIDTH), HEAD_DIM ** -0.5, 0.5, ((0, 2),), jnp.float32)
    key_projection = gaussian(arg_keys[3], (KV_HEADS, 3 * HEAD_DIM, GATE_WIDTH), (3 * HEAD_DIM) ** -0.5, 0.3125, ((0, 2),), jnp.float32)
    block_offsets = draw_block_offsets(jax.random.fold_in(arg_keys[6], 71), 0)
    valid_counts = draw_valid_counts(jax.random.fold_in(arg_keys[6], 71), 0)
    return dict(teacher_queries=teacher_queries, teacher_keys=teacher_keys, query_projection=query_projection, key_projection=key_projection, block_offsets=block_offsets, valid_counts=valid_counts)


def block_map(query_block, cand_keys, offsets, usable):
    scores = jnp.einsum('tgrd,cugd->grtcu', query_block, cand_keys, preferred_element_type=jnp.float32) / math.sqrt(query_block.shape[-1])
    width = query_block.shape[0]
    query_pos = jnp.arange(width)[:, None, None]
    key_pos = jnp.arange(width)[None, None, :]
    allowed = ((offsets[None, :, None] != 0) | (key_pos <= query_pos)) & usable[None, :, None]
    scores = jnp.where(allowed, scores, -jnp.inf)
    top_score = lax.optimization_barrier(jnp.max(scores, axis=(3, 4), keepdims=True))
    weights = jnp.exp(scores - top_score)
    per_block = lax.optimization_barrier(jnp.sum(weights, axis=4))
    shares = per_block / lax.optimization_barrier(jnp.sum(per_block, axis=3, keepdims=True))
    return lax.optimization_barrier(jnp.mean(shares, axis=2))

def gate_terms(gate_query, cand_gate, teacher_map, usable):
    logits = jnp.einsum('bgre,bcge->bgrc', gate_query, cand_gate, precision=lax.Precision.HIGHEST) / math.sqrt(gate_query.shape[-1])
    mask = usable[:, None, None, :]
    logits = jnp.where(mask, logits, -jnp.inf)
    log_gate = logits - jax.nn.logsumexp(logits, axis=3, keepdims=True)
    log_gate = jnp.where(mask, log_gate, 0.0)
    terms = jnp.where(mask, jax.scipy.special.xlogy(teacher_map, teacher_map) - teacher_map * log_gate, 0.0)
    return jnp.sum(terms)

def reference(teacher_queries, teacher_keys, query_projection, key_projection, block_offsets, valid_counts):
    group_size = HEADS // KV_HEADS
    query_blocks = teacher_queries.reshape(QBLOCKS, BLOCK, KV_HEADS, group_size, HEAD_DIM)
    key_blocks = teacher_keys.reshape(QBLOCKS, BLOCK, KV_HEADS, HEAD_DIM)
    row_index = jnp.arange(QBLOCKS, dtype=jnp.int32)
    key_block = row_index[:, None] - block_offsets
    slot_index = jnp.arange(CAND, dtype=jnp.int32)
    usable = (slot_index[None, :] < valid_counts[:, None]) & (key_block >= 0)
    cand_index = jnp.maximum(key_block, 0).astype(jnp.int32)

    def one_block(inputs):
        query_block, index_row, offsets, usable_row = inputs
        cand_keys = key_blocks[index_row]
        return block_map(query_block.astype(jnp.float32), cand_keys.astype(jnp.float32), offsets, usable_row)
    teacher_map = lax.map(one_block, (query_blocks, cand_index, block_offsets, usable))
    pooled_query = lax.optimization_barrier(jnp.mean(query_blocks.astype(jnp.float32), axis=1))
    keys_float = key_blocks.astype(jnp.float32)
    pooled_key = jnp.concatenate([lax.optimization_barrier(jnp.max(keys_float, axis=1)), lax.optimization_barrier(jnp.min(keys_float, axis=1)), lax.optimization_barrier(jnp.mean(keys_float, axis=1))], axis=-1)

    def total_loss(query_weights, key_weights):
        gate_query = jnp.einsum('bgrd,grde->bgre', pooled_query, query_weights.reshape(KV_HEADS, group_size, HEAD_DIM, GATE_WIDTH), precision=lax.Precision.HIGHEST)
        gate_key = jnp.einsum('ngf,gfe->nge', pooled_key, key_weights, precision=lax.Precision.HIGHEST)
        shaped = (N_CTX, QB_DEV)

        def one_shard(inputs):
            shard_query, shard_index, shard_map, shard_usable = inputs
            return gate_terms(shard_query, gate_key[shard_index], shard_map, shard_usable)
        parts = lax.map(one_shard, (gate_query.reshape(shaped + gate_query.shape[1:]), cand_index.reshape(shaped + (CAND,)), teacher_map.reshape(shaped + teacher_map.shape[1:]), usable.reshape(shaped + (CAND,))))
        return jnp.sum(parts)
    kl_total, grads = jax.value_and_grad(total_loss, argnums=(0, 1))(query_projection, key_projection)
    grad_scale = 1.0 / math.sqrt(QBLOCKS)
    return (grads[0] * grad_scale, grads[1] * grad_scale, kl_total / (QBLOCKS * HEADS))
```

```python
import math

import jax
import jax.numpy as jnp
from jax import lax
from jax.experimental import pallas as pl
from jax.experimental.pallas import tpu as pltpu
from jax.sharding import Mesh, PartitionSpec as P

HEADS = 32
KV_HEADS = 8
HEAD_DIM = 128
BLOCK = 64
CAND = 24
REACH = 4

ROWS = 8
SPAN = 24
CHIP_BLOCKS = 2 * ROWS
WINDOW = SPAN + CHIP_BLOCKS
PADDED = 48
KV_HERE = 2
GROUP = HEADS // KV_HEADS
Q_COLS = KV_HERE * GROUP * HEAD_DIM
K_COLS = KV_HERE * HEAD_DIM
DUMMY = 31
SLOT_ROWS = 32
LANES = GROUP * CHIP_BLOCKS
SHARES = 8
GRAD_ROWS = KV_HERE * GROUP * HEAD_DIM + KV_HERE * 3 * HEAD_DIM
SHARE_ROWS = GRAD_ROWS // SHARES
LOW = -1e30
EXP_SCALE = math.log2(math.e) / math.sqrt(HEAD_DIM)
HIGH = lax.Precision.HIGHEST


def dot_f32(a, b, dims):
    return lax.dot_general(
        a, b, (dims, ((), ())), precision=HIGH, preferred_element_type=jnp.float32
    )


def kernel(
    core_ref, rho_ref, groups_ref,
    q_own_ref, q_other_ref, k_own_ref, k_other_ref, k_prev_ref, k_far_ref,
    usable_ref, wq_ref, wk_ref,
    out_ref,
    keys, pooled_key, pooled_query, slot_max, slot_sum, shares,
):
    core = core_ref[0]
    half = ROWS * BLOCK
    own_at = pl.multiple_of((SPAN + ROWS * core) * BLOCK, half)
    other_at = pl.multiple_of((SPAN + ROWS * (1 - core)) * BLOCK, half)
    prev_own_at = pl.multiple_of((ROWS + ROWS * core) * BLOCK, half)
    prev_other_at = pl.multiple_of((ROWS + ROWS * (1 - core)) * BLOCK, half)
    places = (
        (0, k_far_ref, 0),
        (prev_own_at, k_prev_ref, 0),
        (prev_other_at, k_prev_ref, half),
        (own_at, k_own_ref, 0),
        (other_at, k_other_ref, 0),
    )
    for at, source, first in places:
        tile = source[first:first + half, :]
        keys[pl.ds(at, half), :] = tile
        wide = tile.astype(jnp.float32).reshape(ROWS, BLOCK, K_COLS)
        row = at // BLOCK if isinstance(at, int) else pl.multiple_of(lax.div(at, BLOCK), ROWS)
        top = jnp.max(wide, axis=1)
        low = jnp.min(wide, axis=1)
        mean = jnp.sum(wide, axis=1) * (1.0 / BLOCK)
        for g in range(KV_HERE):
            cols = slice(g * HEAD_DIM, (g + 1) * HEAD_DIM)
            for part, value in enumerate((top, low, mean)):
                pooled_key[g, pl.ds(row, ROWS), part * HEAD_DIM:(part + 1) * HEAD_DIM] = (
                    value[:, cols]
                )
    for g in range(KV_HERE):
        pooled_key[g, WINDOW:PADDED, :] = jnp.zeros((PADDED - WINDOW, 3 * HEAD_DIM), jnp.float32)
    shares[...] = jnp.zeros_like(shares)

    width = GROUP * BLOCK
    lane = lax.broadcasted_iota(jnp.int32, (BLOCK, width), 1) % BLOCK
    causal = lax.broadcasted_iota(jnp.int32, (BLOCK, width), 0) <= lane
    slot_row = lax.broadcasted_iota(jnp.int32, (SLOT_ROWS, width), 0)
    live = slot_row <= SPAN
    spread = jnp.where(
        lax.broadcasted_iota(jnp.int32, (width, LANES), 0) // BLOCK
        == lax.broadcasted_iota(jnp.int32, (width, LANES), 1) // CHIP_BLOCKS,
        1.0 / BLOCK, 0.0,
    ).astype(jnp.bfloat16)
    lane_block = lax.broadcasted_iota(jnp.int32, (SLOT_ROWS, LANES), 1) % CHIP_BLOCKS

    def one_group(s, block, g, queries, first_slot, diagonal):
        rows = [rho_ref[s * CAND + first_slot + i] for i in range(4)]
        tiles = []
        for row in rows:
            n = block + jnp.minimum(row, SPAN)
            tiles.append(
                keys[pl.ds(pl.multiple_of(n * BLOCK, BLOCK), BLOCK),
                     g * HEAD_DIM:(g + 1) * HEAD_DIM]
            )
        scores = lax.dot_general(
            jnp.concatenate(tiles, axis=0), queries, (((1,), (1,)), ((), ())),
            preferred_element_type=jnp.float32,
        )
        for i, row in enumerate(rows):
            part = scores[i * BLOCK:(i + 1) * BLOCK, :]
            if diagonal and i == 0:
                part = jnp.where(causal, part, LOW)
            top = jnp.max(part, axis=0, keepdims=True)
            total = jnp.sum(jnp.exp2((part - top) * EXP_SCALE), axis=0, keepdims=True)
            slot_max[pl.ds(row, 1), :] = top
            slot_sum[pl.ds(row, 1), :] = total

    def one_block(s, q_ref, at, block):
        for g in range(KV_HERE):
            queries = jnp.concatenate(
                [
                    q_ref[pl.ds(at, BLOCK), (g * GROUP + r) * HEAD_DIM:(g * GROUP + r + 1) * HEAD_DIM]
                    for r in range(GROUP)
                ],
                axis=0,
            )
            for r in range(GROUP):
                pooled_query[g, pl.ds(r * CHIP_BLOCKS + s, 1), :] = jnp.sum(
                    queries[r * BLOCK:(r + 1) * BLOCK, :].astype(jnp.float32), axis=0, keepdims=True
                ) * (1.0 / BLOCK)
            slot_max[...] = jnp.full_like(slot_max, LOW)
            slot_sum[...] = jnp.zeros_like(slot_sum)
            one_group(s, block, g, queries, 0, True)

            @pl.loop(1, groups_ref[s])
            def _(i):
                one_group(s, block, g, queries, i * 4, False)

            tops = jnp.where(live, slot_max[...], LOW)
            top = jnp.max(tops, axis=0, keepdims=True)
            weight = jnp.where(live, slot_sum[...] * jnp.exp2((tops - top) * EXP_SCALE), 0.0)
            share = weight / jnp.sum(weight, axis=0, keepdims=True)
            coarse = share.astype(jnp.bfloat16)
            fine = (share - coarse.astype(jnp.float32)).astype(jnp.bfloat16)
            mean = (
                jnp.dot(coarse, spread, preferred_element_type=jnp.float32)
                + jnp.dot(fine, spread, preferred_element_type=jnp.float32)
            )
            mine = jnp.where(lane_block == s, mean, 0.0)
            shares[g, pl.ds(block, SLOT_ROWS), :] += mine

    for source in range(2):
        q_ref = (q_own_ref, q_other_ref)[source]
        first = ROWS * core if source == 0 else ROWS * (1 - core)

        @pl.loop(0, ROWS)
        def _(j):
            one_block(source * ROWS + j, q_ref, pl.multiple_of(j * BLOCK, BLOCK), first + j)

    scale = 1.0 / math.sqrt(HEAD_DIM)
    usable = usable_ref[...] > 0.0
    divergence = jnp.zeros((1, LANES), jnp.float32)

    def put(row, value):
        done = 0
        while done < value.shape[0]:
            share_index, inside = divmod(row + done, SHARE_ROWS)
            count = min(value.shape[0] - done, SHARE_ROWS - inside)
            out_ref[share_index, inside:inside + count, :] = value[done:done + count, :]
            done += count

    for g in range(KV_HERE):
        gate_key = dot_f32(pooled_key[g], wk_ref[g], ((1,), (0,)))
        gate_query = jnp.concatenate(
            [
                dot_f32(
                    pooled_query[g, r * CHIP_BLOCKS:(r + 1) * CHIP_BLOCKS, :],
                    wq_ref[g * GROUP + r], ((1,), (0,)),
                )
                for r in range(GROUP)
            ],
            axis=0,
        )
        logits = dot_f32(gate_key, gate_query, ((1,), (1,))) * scale
        logits = jnp.where(usable, logits, LOW)
        top = jnp.max(logits, axis=0, keepdims=True)
        weight = jnp.where(usable, jnp.exp(logits - top), 0.0)
        mass = jnp.sum(weight, axis=0, keepdims=True)
        log_gate = jnp.where(usable, logits - top - jnp.log(mass), 0.0)
        target = shares[g]
        positive = target > 0.0
        log_target = jnp.log(jnp.where(positive, target, 1.0))
        terms = jnp.where(usable, target * (log_target - log_gate), 0.0)
        divergence += jnp.sum(terms, axis=0, keepdims=True)
        target = jnp.where(usable, target, 0.0)
        slope = (weight / mass) * jnp.sum(target, axis=0, keepdims=True) - target
        slope = slope * (scale / 32.0)
        d_query = dot_f32(slope, gate_key, ((0,), (0,)))
        d_key = dot_f32(slope, gate_query, ((1,), (0,)))
        for r in range(GROUP):
            picked = slice(r * CHIP_BLOCKS, (r + 1) * CHIP_BLOCKS)
            put(
                (g * GROUP + r) * HEAD_DIM,
                dot_f32(pooled_query[g, picked, :], d_query[picked, :], ((0,), (0,))),
            )
        put(
            KV_HERE * GROUP * HEAD_DIM + g * 3 * HEAD_DIM,
            dot_f32(pooled_key[g], d_key, ((0,), (0,))),
        )
    total = jnp.sum(divergence)
    for i in range(SHARES):
        out_ref[i, SHARE_ROWS:SHARE_ROWS + 8, :] = jnp.full((8, HEAD_DIM), total, jnp.float32)


def swap(x, axis):
    return lax.ppermute(x, axis, [(0, 1), (1, 0)])


def body(
    teacher_queries, teacher_keys, query_projection, key_projection, block_offsets, valid_counts
):
    chips = ("z", "yh", "x")
    places = ("z", "yh", "x", "core")
    count = lax.axis_size(places)
    core = lax.axis_index("core")
    chip = lax.axis_index(chips)
    half = ROWS * BLOCK

    note = jnp.concatenate(
        [block_offsets, valid_counts[:, None], jnp.zeros((ROWS, K_COLS - CAND - 1), jnp.int32)], axis=1
    ).astype(jnp.bfloat16)
    note = jnp.concatenate([note, jnp.zeros_like(note)], axis=0)
    k_mine = lax.dynamic_slice_in_dim(teacher_keys, core * K_COLS, K_COLS, 1)
    k_give = lax.dynamic_slice_in_dim(teacher_keys, (1 - core) * K_COLS, K_COLS, 1)
    k_other = swap(jnp.concatenate([k_give, note], axis=0), "core")
    note_other = k_other[half:half + ROWS, :CAND + 1].astype(jnp.int32)
    k_other = k_other[:half]
    k_prev = lax.ppermute(
        jnp.concatenate([k_mine, k_other], axis=0), places,
        [(i, i + 2) for i in range(count - 2)],
    )
    k_far = lax.ppermute(
        jnp.where(core == 1, k_mine, k_other), places, [(i, i + 4) for i in range(count - 4)]
    )
    q_other = swap(
        lax.dynamic_slice_in_dim(teacher_queries, (1 - core) * Q_COLS, Q_COLS, 1), "core"
    )

    offsets = jnp.concatenate([block_offsets, note_other[:, :CAND]], axis=0)
    counts = jnp.concatenate([valid_counts, note_other[:, CAND]], axis=0)
    step = jnp.arange(CHIP_BLOCKS, dtype=jnp.int32)
    block = jnp.where(step < ROWS, core * ROWS + step, (1 - core) * ROWS + step - ROWS)
    key_block = chip * CHIP_BLOCKS + block[:, None] - offsets
    usable = (jnp.arange(CAND, dtype=jnp.int32)[None, :] < counts[:, None]) & (key_block >= 0)
    rho = jnp.where(usable, SPAN - offsets, DUMMY)
    place = jnp.where(usable, block[:, None] + rho, -1)
    hit = jnp.any(
        place[None, :, :] == jnp.arange(PADDED, dtype=jnp.int32)[:, None, None], axis=2
    )
    hit = jnp.tile(hit.astype(jnp.float32), (1, GROUP))
    groups = (counts + 3) // 4

    wq = lax.dynamic_slice_in_dim(query_projection, core * KV_HERE * GROUP, KV_HERE * GROUP, 0)
    wk = lax.dynamic_slice_in_dim(key_projection, core * KV_HERE, KV_HERE, 0)

    whole = lambda *shape: pl.BlockSpec(shape, lambda i, c, r, n: (0,) * len(shape))
    parts = pl.pallas_call(
        kernel,
        grid_spec=pltpu.PrefetchScalarGridSpec(
            num_scalar_prefetch=3,
            grid=(1,),
            in_specs=[
                pl.BlockSpec((half, Q_COLS), lambda i, c, r, n: (0, c[0])),
                whole(half, Q_COLS),
                whole(half, K_COLS),
                whole(half, K_COLS),
                whole(2 * half, K_COLS),
                whole(half, K_COLS),
                whole(PADDED, LANES),
                whole(KV_HERE * GROUP, HEAD_DIM, HEAD_DIM),
                whole(KV_HERE, 3 * HEAD_DIM, HEAD_DIM),
            ],
            out_specs=whole(SHARES, SHARE_ROWS + 8, HEAD_DIM),
            scratch_shapes=[
                pltpu.VMEM((WINDOW * BLOCK, K_COLS), jnp.bfloat16),
                pltpu.VMEM((KV_HERE, PADDED, 3 * HEAD_DIM), jnp.float32),
                pltpu.VMEM((KV_HERE, LANES, HEAD_DIM), jnp.float32),
                pltpu.VMEM((SLOT_ROWS, GROUP * BLOCK), jnp.float32),
                pltpu.VMEM((SLOT_ROWS, GROUP * BLOCK), jnp.float32),
                pltpu.VMEM((KV_HERE, PADDED, LANES), jnp.float32),
            ],
        ),
        out_shape=jax.ShapeDtypeStruct((SHARES, SHARE_ROWS + 8, HEAD_DIM), jnp.float32),
        compiler_params=pltpu.CompilerParams(vmem_limit_bytes=40 * 1024 * 1024),
        name="gate",
    )(
        core.reshape(1).astype(jnp.int32), rho.reshape(-1), groups,
        teacher_queries, q_other, k_mine, k_other, k_prev, k_far, hit, wq, wk,
    )

    got = lax.all_to_all(parts, ("yh", "x"), 0, 0)
    got = jnp.sum(got, axis=0)
    for far in (1, 2, 4):
        got = got + lax.ppermute(got, "z", [(i, i ^ far) for i in range(8)])
    total = got[SHARE_ROWS:SHARE_ROWS + 1, :]
    total = total + swap(total, "head")
    total = total + swap(total, "core")
    spread = jnp.broadcast_to(got[:SHARE_ROWS], (SHARES, SHARE_ROWS, HEAD_DIM))
    mine = lax.all_to_all(spread, ("yh", "x"), 0, 0).reshape(GRAD_ROWS, HEAD_DIM)
    other = swap(mine, "core")
    first = jnp.where(core == 0, mine, other)
    second = jnp.where(core == 0, other, mine)
    cut = KV_HERE * GROUP * HEAD_DIM
    query_gradient = jnp.concatenate([first[:cut], second[:cut]], axis=0)
    key_gradient = jnp.concatenate([first[cut:], second[cut:]], axis=0)
    return (
        query_gradient.reshape(2 * KV_HERE * GROUP, HEAD_DIM, HEAD_DIM),
        key_gradient.reshape(2 * KV_HERE, 3 * HEAD_DIM, HEAD_DIM),
        total[0, 0] / (1024 * HEADS),
    )


def solution(mesh):
    split = Mesh(mesh.devices.reshape(8, 2, 4, 2, 2), ("z", "yh", "x", "core", "head"))
    ctx = ("z", "yh", "x", "core")
    placed = (
        P(ctx, "head"),
        P(ctx, "head"),
        P("head", None, None),
        P("head", None, None),
        P(ctx, None),
        P(ctx),
    )
    return jax.shard_map(
        body,
        mesh=split,
        in_specs=placed,
        out_specs=(P("head", None, None), P("head", None, None), P()),
        check_vma=False,
    )
```

```python
import math

import jax
import jax.numpy as jnp
from jax import lax
from jax.experimental import pallas as pl
from jax.experimental.pallas import tpu as pltpu
from jax.sharding import Mesh, PartitionSpec as P

HEADS = 32
KV_HEADS = 8
HEAD_DIM = 128
BLOCK = 64
CAND = 24
REACH = 4

ROWS = 8
SPAN = 24
CHIP_BLOCKS = 2 * ROWS
PADDED = 48
KV_HERE = 2
GROUP = HEADS // KV_HEADS
HEADS_HERE = KV_HERE * GROUP
Q_COLS = HEADS_HERE * HEAD_DIM
K_COLS = KV_HERE * HEAD_DIM
POOL = 3 * HEAD_DIM
WIDTH = GROUP * BLOCK
DUMMY = 31
SLOT_ROWS = 32
LANES = GROUP * CHIP_BLOCKS
SHARES = 8
KEY_ROWS = KV_HERE * POOL // SHARES
PART_ROWS = 2 * CHIP_BLOCKS + KEY_ROWS + 8
SUM_ROWS = HEAD_DIM + KEY_ROWS
UNROLL = 3
LOW = -1e30
EXP_SCALE = math.log2(math.e) / math.sqrt(HEAD_DIM)
HIGH = lax.Precision.HIGHEST


def dot_f32(a, b, dims):
    return lax.dot_general(
        a, b, (dims, ((), ())), precision=HIGH, preferred_element_type=jnp.float32
    )


def pool_keys(tile):
    wide = tile.astype(jnp.float32).reshape(ROWS, BLOCK, K_COLS)
    top = jnp.max(wide, axis=1)
    low = jnp.min(wide, axis=1)
    mean = jnp.sum(wide, axis=1) * (1.0 / BLOCK)
    return [
        jnp.concatenate(
            [v[:, g * HEAD_DIM:(g + 1) * HEAD_DIM] for v in (top, low, mean)], axis=1
        )
        for g in range(KV_HERE)
    ]


def enlist(groups_ref, work):
    def per_block(s, filled):
        def one(i, filled):
            work[filled] = s * CAND + i * 4
            return filled + 1
        return lax.fori_loop(0, groups_ref[s], one, filled)

    filled = lax.fori_loop(0, CHIP_BLOCKS, per_block, 0)
    spare = work[jnp.maximum(filled - 1, 0)]
    for extra in range(UNROLL - 1):
        work[filled + extra] = spare
    return filled


def position(core, s):
    return jnp.where(s < ROWS, ROWS * core + s, ROWS * (1 - core) + s - ROWS)


def slot_loop(filled, work, list_ref, tile_start, keys, queries, slot_max, slot_sum, diagonal):
    lane = lax.broadcasted_iota(jnp.int32, (BLOCK, WIDTH), 1) % BLOCK
    key_row = lax.broadcasted_iota(jnp.int32, (BLOCK, WIDTH), 0)

    @pl.loop(0, (filled + UNROLL - 1) // UNROLL)
    def _(step):
        found = []
        for e in range(UNROLL):
            first = work[step * UNROLL + e]
            s = first // CAND
            rows = [list_ref[first + i] for i in range(4)]
            starts = [pl.multiple_of(tile_start(s, row) * BLOCK, BLOCK) for row in rows]
            if diagonal:
                keep = key_row <= lane + jnp.where(first == s * CAND, 0, BLOCK)
            for g in range(KV_HERE):
                tiles = [
                    keys[pl.ds(start, BLOCK), g * HEAD_DIM:(g + 1) * HEAD_DIM] for start in starts
                ]
                scores = lax.dot_general(
                    jnp.concatenate(tiles, axis=0), queries[s * KV_HERE + g],
                    (((1,), (1,)), ((), ())), preferred_element_type=jnp.float32,
                )
                for i, row in enumerate(rows):
                    part = scores[i * BLOCK:(i + 1) * BLOCK, :]
                    if diagonal and i == 0:
                        part = jnp.where(keep, part, LOW)
                    top = jnp.max(part, axis=0, keepdims=True)
                    total = jnp.sum(
                        jnp.exp2((part - top) * EXP_SCALE), axis=0, keepdims=True
                    )
                    found.append((s * KV_HERE + g, row, top, total))
        for index, row, top, total in found:
            slot_max[index, pl.ds(row, 1), :] = top
            slot_sum[index, pl.ds(row, 1), :] = total


def near_kernel(
    core_ref, list_ref, groups_ref,
    q_own_ref, q_other_ref, k_own_ref, k_other_ref, wq_ref, wk_ref,
    queries, slot_max, slot_sum, pooled_query, gate_query, pooled_key, gate_key,
    keys, work,
):
    core = core_ref[0]
    half = ROWS * BLOCK
    for source, ref in ((core, k_own_ref), (1 - core, k_other_ref)):
        tile = ref[...]
        keys[pl.ds(pl.multiple_of(source * half, half), half), :] = tile
        for g, pooled in enumerate(pool_keys(tile)):
            pooled_key[g, pl.ds(pl.multiple_of(source * ROWS, ROWS), ROWS), :] = pooled

    def prepare(s, q_ref, at):
        for g in range(KV_HERE):
            for r in range(GROUP):
                head = g * GROUP + r
                tile = q_ref[pl.ds(at, BLOCK), head * HEAD_DIM:(head + 1) * HEAD_DIM]
                queries[s * KV_HERE + g, r * BLOCK:(r + 1) * BLOCK, :] = tile
                pooled_query[g, pl.ds(r * CHIP_BLOCKS + s, 1), :] = jnp.sum(
                    tile.astype(jnp.float32), axis=0, keepdims=True
                ) * (1.0 / BLOCK)

    for source in range(2):
        q_ref = (q_own_ref, q_other_ref)[source]

        @pl.loop(0, ROWS)
        def _(j):
            prepare(source * ROWS + j, q_ref, pl.multiple_of(j * BLOCK, BLOCK))

    slot_max[...] = jnp.full_like(slot_max, LOW)
    slot_sum[...] = jnp.zeros_like(slot_sum)
    filled = enlist(groups_ref, work)
    slot_loop(
        filled, work, list_ref,
        lambda s, row: position(core, s) + jnp.minimum(row, SPAN) - SPAN,
        keys, queries, slot_max, slot_sum, True,
    )
    for g in range(KV_HERE):
        gate_key[g] = dot_f32(pooled_key[g], wk_ref[g], ((1,), (0,)))
        for r in range(GROUP):
            picked = slice(r * CHIP_BLOCKS, (r + 1) * CHIP_BLOCKS)
            gate_query[g, picked, :] = dot_f32(
                pooled_query[g, picked, :], wq_ref[g * GROUP + r], ((1,), (0,))
            )


def far_kernel(
    core_ref, list_ref, groups_ref,
    k_prev_own_ref, k_prev_other_ref, k_far_ref, queries,
    max_ref, sum_ref, pooled_query, gate_query, near_key, near_gate_key, usable_ref, wk_ref,
    out_ref,
    keys, slot_max, slot_sum, pooled_key, shares, work,
):
    core = core_ref[0]
    half = ROWS * BLOCK
    for place, ref in ((0, k_far_ref), (1 + core, k_prev_own_ref), (2 - core, k_prev_other_ref)):
        tile = ref[...]
        at = place * half if isinstance(place, int) else pl.multiple_of(place * half, half)
        row = place * ROWS if isinstance(place, int) else pl.multiple_of(place * ROWS, ROWS)
        keys[pl.ds(at, half), :] = tile
        for g, pooled in enumerate(pool_keys(tile)):
            pooled_key[g, pl.ds(row, ROWS), :] = pooled
    for g in range(KV_HERE):
        pooled_key[g, SPAN:SPAN + CHIP_BLOCKS, :] = near_key[g]
    slot_max[...] = max_ref[...]
    slot_sum[...] = sum_ref[...]
    shares[...] = jnp.zeros_like(shares)

    filled = enlist(groups_ref, work)
    slot_loop(
        filled, work, list_ref,
        lambda s, row: jnp.where(row <= SPAN, position(core, s) + row, 0),
        keys, queries, slot_max, slot_sum, False,
    )

    live = lax.broadcasted_iota(jnp.int32, (SLOT_ROWS, WIDTH), 0) <= SPAN
    spread = jnp.where(
        lax.broadcasted_iota(jnp.int32, (WIDTH, LANES), 0) // BLOCK
        == lax.broadcasted_iota(jnp.int32, (WIDTH, LANES), 1) // CHIP_BLOCKS,
        1.0 / BLOCK, 0.0,
    ).astype(jnp.bfloat16)
    lane_block = lax.broadcasted_iota(jnp.int32, (SLOT_ROWS, LANES), 1) % CHIP_BLOCKS

    @pl.loop(0, CHIP_BLOCKS // 4)
    def _(step):
        found = []
        for e in range(4):
            s = step * 4 + e
            for g in range(KV_HERE):
                tops = jnp.where(live, slot_max[s * KV_HERE + g], LOW)
                top = jnp.max(tops, axis=0, keepdims=True)
                weight = jnp.where(
                    live, slot_sum[s * KV_HERE + g] * jnp.exp2((tops - top) * EXP_SCALE), 0.0
                )
                share = weight / jnp.sum(weight, axis=0, keepdims=True)
                coarse = share.astype(jnp.bfloat16)
                fine = (share - coarse.astype(jnp.float32)).astype(jnp.bfloat16)
                mean = (
                    jnp.dot(coarse, spread, preferred_element_type=jnp.float32)
                    + jnp.dot(fine, spread, preferred_element_type=jnp.float32)
                )
                found.append((g, position(core, s), jnp.where(lane_block == s, mean, 0.0)))
        for g, block, mine in found:
            shares[g, pl.ds(block, SLOT_ROWS), :] += mine

    scale = 1.0 / math.sqrt(HEAD_DIM)
    window = SPAN + CHIP_BLOCKS
    usable = usable_ref[...] > 0.0
    divergence = jnp.zeros((1, LANES), jnp.float32)
    key_base = 2 * CHIP_BLOCKS
    for g in range(KV_HERE):
        far_gate_key = dot_f32(pooled_key[g, 0:SPAN, :], wk_ref[g], ((1,), (0,)))
        gate_key = jnp.concatenate([far_gate_key, near_gate_key[g]], axis=0)
        logits = dot_f32(gate_key, gate_query[g], ((1,), (1,))) * scale
        logits = jnp.where(usable, logits, LOW)
        top = jnp.max(logits, axis=0, keepdims=True)
        weight = jnp.where(usable, jnp.exp(logits - top), 0.0)
        mass = jnp.sum(weight, axis=0, keepdims=True)
        log_gate = jnp.where(usable, logits - top - jnp.log(mass), 0.0)
        target = shares[g, 0:window, :]
        log_target = jnp.log(jnp.where(target > 0.0, target, 1.0))
        terms = jnp.where(usable, target * (log_target - log_gate), 0.0)
        divergence += jnp.sum(terms, axis=0, keepdims=True)
        target = jnp.where(usable, target, 0.0)
        slope = (weight / mass) * jnp.sum(target, axis=0, keepdims=True) - target
        slope = slope * (scale / 32.0)
        d_query = dot_f32(slope, gate_key, ((0,), (0,)))
        d_key = dot_f32(slope, gate_query[g], ((1,), (0,)))
        for r in range(GROUP):
            picked = slice(r * CHIP_BLOCKS, (r + 1) * CHIP_BLOCKS)
            out_ref[g * GROUP + r, 0:CHIP_BLOCKS, :] = pooled_query[g, picked, :]
            out_ref[g * GROUP + r, CHIP_BLOCKS:key_base, :] = d_query[picked, :]
        key_part = dot_f32(pooled_key[g], d_key, ((0,), (0,)))
        for i in range(SHARES // KV_HERE):
            out_ref[g * (SHARES // KV_HERE) + i, key_base:key_base + KEY_ROWS, :] = (
                key_part[i * KEY_ROWS:(i + 1) * KEY_ROWS, :]
            )
    total = jnp.sum(divergence)
    for i in range(SHARES):
        out_ref[i, PART_ROWS - 8:PART_ROWS, :] = jnp.full((8, HEAD_DIM), total, jnp.float32)


def sum_kernel(parts_ref, out_ref):
    parts = parts_ref[...]
    pooled = parts[:, 0:CHIP_BLOCKS, :].reshape(SHARES * CHIP_BLOCKS, HEAD_DIM)
    slope = parts[:, CHIP_BLOCKS:2 * CHIP_BLOCKS, :].reshape(SHARES * CHIP_BLOCKS, HEAD_DIM)
    out_ref[0:HEAD_DIM, :] = dot_f32(pooled, slope, ((0,), (0,)))
    out_ref[HEAD_DIM:, :] = jnp.sum(parts[:, 2 * CHIP_BLOCKS:, :], axis=0)


def swap(x, axis):
    return lax.ppermute(x, axis, [(0, 1), (1, 0)])


def whole(*shape):
    return pl.BlockSpec(shape, lambda i, *_: (0,) * len(shape))


def shaped(shape, dtype=jnp.float32):
    return jax.ShapeDtypeStruct(shape, dtype)


def near_call(core, slots, groups, q_own, q_other, k_own, k_other, wq, wk):
    half = ROWS * BLOCK
    outs = [
        shaped((CHIP_BLOCKS * KV_HERE, WIDTH, HEAD_DIM), jnp.bfloat16),
        shaped((CHIP_BLOCKS * KV_HERE, SLOT_ROWS, WIDTH)),
        shaped((CHIP_BLOCKS * KV_HERE, SLOT_ROWS, WIDTH)),
        shaped((KV_HERE, LANES, HEAD_DIM)),
        shaped((KV_HERE, LANES, HEAD_DIM)),
        shaped((KV_HERE, CHIP_BLOCKS, POOL)),
        shaped((KV_HERE, CHIP_BLOCKS, HEAD_DIM)),
    ]
    return pl.pallas_call(
        near_kernel,
        grid_spec=pltpu.PrefetchScalarGridSpec(
            num_scalar_prefetch=3,
            grid=(1,),
            in_specs=[
                pl.BlockSpec((half, Q_COLS), lambda i, c, *_: (0, c[0])),
                whole(half, Q_COLS),
                pl.BlockSpec((half, K_COLS), lambda i, c, *_: (0, c[0])),
                whole(half, K_COLS),
                whole(HEADS_HERE, HEAD_DIM, HEAD_DIM),
                whole(KV_HERE, POOL, HEAD_DIM),
            ],
            out_specs=[whole(*o.shape) for o in outs],
            scratch_shapes=[
                pltpu.VMEM((CHIP_BLOCKS * BLOCK, K_COLS), jnp.bfloat16),
                pltpu.SMEM((CHIP_BLOCKS * 6 + 8,), jnp.int32),
            ],
        ),
        out_shape=outs,
        compiler_params=pltpu.CompilerParams(vmem_limit_bytes=40 * 1024 * 1024),
        cost_estimate=pl.CostEstimate(
            flops=2_000_000_000, bytes_accessed=8_000_000, transcendentals=8_000_000
        ),
        name="near",
    )(core, slots, groups, q_own, q_other, k_own, k_other, wq, wk)


def far_call(core, slots, groups, k_prev_own, k_prev_other, k_far, near, hit, wk):
    half = ROWS * BLOCK
    queries, slot_max, slot_sum, pooled_query, gate_query, near_key, near_gate_key = near
    args = (
        k_prev_own, k_prev_other, k_far, queries, slot_max, slot_sum, pooled_query, gate_query,
        near_key, near_gate_key, hit, wk,
    )
    return pl.pallas_call(
        far_kernel,
        grid_spec=pltpu.PrefetchScalarGridSpec(
            num_scalar_prefetch=3,
            grid=(1,),
            in_specs=[whole(*a.shape) for a in args],
            out_specs=whole(SHARES, PART_ROWS, HEAD_DIM),
            scratch_shapes=[
                pltpu.VMEM((SPAN * BLOCK, K_COLS), jnp.bfloat16),
                pltpu.VMEM((CHIP_BLOCKS * KV_HERE, SLOT_ROWS, WIDTH), jnp.float32),
                pltpu.VMEM((CHIP_BLOCKS * KV_HERE, SLOT_ROWS, WIDTH), jnp.float32),
                pltpu.VMEM((KV_HERE, SPAN + CHIP_BLOCKS, POOL), jnp.float32),
                pltpu.VMEM((KV_HERE, PADDED, LANES), jnp.float32),
                pltpu.SMEM((CHIP_BLOCKS * 6 + 8,), jnp.int32),
            ],
        ),
        out_shape=shaped((SHARES, PART_ROWS, HEAD_DIM)),
        compiler_params=pltpu.CompilerParams(vmem_limit_bytes=40 * 1024 * 1024),
        cost_estimate=pl.CostEstimate(
            flops=2_000_000_000, bytes_accessed=8_000_000, transcendentals=8_000_000
        ),
        name="far",
    )(core, slots, groups, *args)


def pack_slots(picked, rho):
    slot = jnp.arange(CAND, dtype=jnp.int32)
    before = jnp.sum(
        jnp.where(picked[:, None, :] & (slot[None, None, :] < slot[None, :, None]), 1, 0), axis=2
    )
    here = picked[:, None, :] & (before[:, None, :] == slot[None, :, None])
    count = jnp.sum(picked.astype(jnp.int32), axis=1)
    packed = jnp.sum(jnp.where(here, rho[:, None, :], 0), axis=2)
    packed = jnp.where(slot[None, :] < count[:, None], packed, DUMMY)
    return packed.reshape(-1), (count + 3) // 4


def plan(core, chip, offsets, counts):
    step = jnp.arange(CHIP_BLOCKS, dtype=jnp.int32)
    block = jnp.where(step < ROWS, core * ROWS + step, (1 - core) * ROWS + step - ROWS)[:, None]
    key_block = chip * CHIP_BLOCKS + block - offsets
    usable = (jnp.arange(CAND, dtype=jnp.int32)[None, :] < counts[:, None]) & (key_block >= 0)
    rho = SPAN - offsets
    near = pack_slots(usable & (offsets <= block), rho)
    far = pack_slots(usable & (offsets > block), rho)
    place = jnp.where(usable, block + rho, -1)
    row = jnp.arange(SPAN + CHIP_BLOCKS, dtype=jnp.int32)[:, None, None]
    hit = jnp.any(place[None, :, :] == row, axis=2)
    return near, far, jnp.tile(hit.astype(jnp.float32), (1, GROUP))


def body(
    teacher_queries, teacher_keys, query_projection, key_projection, block_offsets, valid_counts
):
    chips = ("z", "yh", "x")
    places = ("z", "yh", "x", "core")
    count = lax.axis_size(places)
    core = lax.axis_index("core")
    chip = lax.axis_index(chips)
    half = ROWS * BLOCK

    k_mine = lax.dynamic_slice_in_dim(teacher_keys, core * K_COLS, K_COLS, 1)
    k_prev_own = lax.ppermute(k_mine, places, [(i, i + 2) for i in range(count - 2)])
    k_give = lax.dynamic_slice_in_dim(teacher_keys, (1 - core) * K_COLS, K_COLS, 1)
    k_prev_other = lax.ppermute(
        k_give, places, [(i, (i ^ 1) + 2) for i in range(count - 2)]
    )
    note = jnp.concatenate(
        [block_offsets, valid_counts[:, None], jnp.zeros((ROWS, K_COLS - CAND - 1), jnp.int32)], axis=1
    ).astype(jnp.bfloat16)
    note = jnp.concatenate([note, jnp.zeros_like(note)], axis=0)
    k_other = swap(jnp.concatenate([k_give, note], axis=0), "core")
    note_other = k_other[half:half + ROWS, :CAND + 1].astype(jnp.int32)
    k_other = k_other[:half]
    k_far = lax.ppermute(
        jnp.where(core == 1, k_mine, k_other), places, [(i, i + 4) for i in range(count - 4)]
    )
    q_other = swap(
        lax.dynamic_slice_in_dim(teacher_queries, (1 - core) * Q_COLS, Q_COLS, 1), "core"
    )

    offsets = jnp.concatenate([block_offsets, note_other[:, :CAND]], axis=0)
    counts = jnp.concatenate([valid_counts, note_other[:, CAND]], axis=0)
    near, far, hit = plan(core, chip, offsets, counts)
    wq = lax.dynamic_slice_in_dim(query_projection, core * HEADS_HERE, HEADS_HERE, 0)
    wk = lax.dynamic_slice_in_dim(key_projection, core * KV_HERE, KV_HERE, 0)
    index = core.reshape(1).astype(jnp.int32)
    near_out = near_call(index, *near, teacher_queries, q_other, teacher_keys, k_other, wq, wk)
    parts = far_call(index, *far, k_prev_own, k_prev_other, k_far, near_out, hit, wk)

    got = lax.all_to_all(parts, ("yh", "x"), 0, 0)
    got = pl.pallas_call(sum_kernel, out_shape=shaped((SUM_ROWS + 8, HEAD_DIM)), name="sum")(got)
    for step in (1, 2, 4):
        got = got + lax.ppermute(got, "z", [(i, i ^ step) for i in range(8)])
    total = got[SUM_ROWS:SUM_ROWS + 1, :]
    total = total + swap(total, "head")
    total = total + swap(total, "core")
    spread = jnp.broadcast_to(got[:SUM_ROWS], (SHARES, SUM_ROWS, HEAD_DIM))
    mine = lax.all_to_all(spread, ("yh", "x"), 0, 0)
    other = swap(mine, "core")
    first = jnp.where(core == 0, mine, other)
    second = jnp.where(core == 0, other, mine)
    both = jnp.concatenate([first, second], axis=0)
    query_gradient = both[:, :HEAD_DIM]
    key_gradient = both[:, HEAD_DIM:].reshape(2 * KV_HERE, POOL, HEAD_DIM)
    return query_gradient, key_gradient, total[0, 0] / (1024 * HEADS)


def solution(mesh):
    split = Mesh(mesh.devices.reshape(8, 2, 4, 2, 2), ("z", "yh", "x", "core", "head"))
    ctx = ("z", "yh", "x", "core")
    placed = (
        P(ctx, "head"),
        P(ctx, "head"),
        P("head", None, None),
        P("head", None, None),
        P(ctx, None),
        P(ctx),
    )
    return jax.shard_map(
        body,
        mesh=split,
        in_specs=placed,
        out_specs=(P("head", None, None), P("head", None, None), P()),
        check_vma=False,
    )
```

```python
import math

import jax
import jax.numpy as jnp
from jax import lax
from jax.experimental import pallas as pl
from jax.experimental.pallas import tpu as pltpu
from jax.sharding import Mesh, PartitionSpec as P

HEADS = 32
KV_HEADS = 8
HEAD_DIM = 128
BLOCK = 64
CAND = 24
REACH = 4

ROWS = 8
SPAN = 24
CHIP_BLOCKS = 2 * ROWS
PADDED = 48
KV_HERE = 2
GROUP = HEADS // KV_HEADS
HEADS_HERE = KV_HERE * GROUP
Q_COLS = HEADS_HERE * HEAD_DIM
K_COLS = KV_HERE * HEAD_DIM
POOL = 3 * HEAD_DIM
WIDTH = GROUP * BLOCK
DUMMY = 31
SLOT_ROWS = 32
LANES = GROUP * CHIP_BLOCKS
SHARES = 16
KEY_ROWS = KV_HERE * POOL // SHARES
HALF_HEAD = HEAD_DIM // 2
PART_ROWS = CHIP_BLOCKS + ROWS + KEY_ROWS + 8
SUM_ROWS = HALF_HEAD + KEY_ROWS
VMEM_BYTES = 56 * 1024 * 1024
UNROLL = 3
LIST_SIZE = CHIP_BLOCKS * CAND + 8
WORK_SIZE = CHIP_BLOCKS * CAND // 4 + 8
LOW = -1e30
EXP_SCALE = math.log2(math.e) / math.sqrt(HEAD_DIM)
HIGH = lax.Precision.HIGHEST


def dot_f32(a, b, dims):
    return lax.dot_general(
        a, b, (dims, ((), ())), precision=HIGH, preferred_element_type=jnp.float32
    )


def pool_keys(tile):
    wide = tile.astype(jnp.float32).reshape(ROWS, BLOCK, K_COLS)
    top = jnp.max(wide, axis=1)
    low = jnp.min(wide, axis=1)
    mean = jnp.sum(wide, axis=1) * (1.0 / BLOCK)
    return [
        jnp.concatenate(
            [v[:, g * HEAD_DIM:(g + 1) * HEAD_DIM] for v in (top, low, mean)], axis=1
        )
        for g in range(KV_HERE)
    ]


def make_lists(core, chip, tables, near_list, near_work, far_list, far_work):
    limit_base = chip * CHIP_BLOCKS
    filled = (jnp.int32(0), jnp.int32(0))
    for source, (offsets_ref, counts_ref) in enumerate(tables):
        first = ROWS * core if source == 0 else ROWS * (1 - core)

        def per_block(j, filled):
            block = first + j
            base = (source * ROWS + j) * CAND

            def per_slot(c, ends):
                near_end, far_end = ends
                offset = offsets_ref[j, c]
                near = offset <= block
                far = (offset > block) & (offset <= limit_base + block)
                near_list[near_end] = SPAN - offset
                far_list[far_end] = SPAN - offset
                return near_end + near.astype(jnp.int32), far_end + far.astype(jnp.int32)

            ends = lax.fori_loop(0, counts_ref[j], per_slot, (base, base))
            out = []
            for end, slots, work, total in zip(
                ends, (near_list, far_list), (near_work, far_work), filled
            ):
                for extra in range(3):
                    slots[end + extra] = DUMMY

                def add(i, total):
                    work[total] = base + i * 4
                    return total + 1

                out.append(lax.fori_loop(0, (end - base + 3) // 4, add, total))
            return tuple(out)

        filled = lax.fori_loop(0, ROWS, per_block, filled)
    for work, total in zip((near_work, far_work), filled):
        spare = work[jnp.maximum(total - 1, 0)]
        for extra in range(UNROLL - 1):
            work[total + extra] = spare
    return filled


def position(core, s):
    return jnp.where(s < ROWS, ROWS * core + s, ROWS * (1 - core) + s - ROWS)


def slot_loop(filled, work, list_ref, tile_start, keys, queries, slot_max, slot_sum, diagonal):
    lane = lax.broadcasted_iota(jnp.int32, (BLOCK, WIDTH), 1) % BLOCK
    key_row = lax.broadcasted_iota(jnp.int32, (BLOCK, WIDTH), 0)

    @pl.loop(0, (filled + UNROLL - 1) // UNROLL)
    def _(step):
        found = []
        for e in range(UNROLL):
            first = work[step * UNROLL + e]
            s = first // CAND
            rows = [list_ref[first + i] for i in range(4)]
            starts = [pl.multiple_of(tile_start(s, row) * BLOCK, BLOCK) for row in rows]
            if diagonal:
                keep = key_row <= lane + jnp.where(first == s * CAND, 0, BLOCK)
            for g in range(KV_HERE):
                tiles = [
                    keys[pl.ds(start, BLOCK), g * HEAD_DIM:(g + 1) * HEAD_DIM] for start in starts
                ]
                scores = lax.dot_general(
                    jnp.concatenate(tiles, axis=0), queries[s * KV_HERE + g],
                    (((1,), (1,)), ((), ())), preferred_element_type=jnp.float32,
                )
                for i, row in enumerate(rows):
                    part = scores[i * BLOCK:(i + 1) * BLOCK, :]
                    if diagonal and i == 0:
                        part = jnp.where(keep, part, LOW)
                    top = jnp.max(part, axis=0, keepdims=True)
                    total = jnp.sum(
                        jnp.exp2((part - top) * EXP_SCALE), axis=0, keepdims=True
                    )
                    found.append((s * KV_HERE + g, row, top, total))
        for index, row, top, total in found:
            slot_max[index, pl.ds(row, 1), :] = top
            slot_sum[index, pl.ds(row, 1), :] = total


def near_kernel(
    place_ref, offsets_own_ref, counts_own_ref, offsets_other_ref, counts_other_ref,
    q_own_ref, q_other_ref, k_own_ref, k_other_ref, wq_ref, wk_ref,
    queries, slot_max, slot_sum, pooled_query, gate_query, pooled_key, gate_key,
    far_list, far_work, far_filled,
    keys, near_list, near_work,
):
    core_ref = place_ref
    core = core_ref[0]
    half = ROWS * BLOCK
    for source, ref in ((core, k_own_ref), (1 - core, k_other_ref)):
        tile = ref[...]
        keys[pl.ds(pl.multiple_of(source * half, half), half), :] = tile
        for g, pooled in enumerate(pool_keys(tile)):
            pooled_key[g, pl.ds(pl.multiple_of(source * ROWS, ROWS), ROWS), :] = pooled

    def prepare(s, q_ref, at):
        for g in range(KV_HERE):
            for r in range(GROUP):
                head = g * GROUP + r
                tile = q_ref[pl.ds(at, BLOCK), head * HEAD_DIM:(head + 1) * HEAD_DIM]
                queries[s * KV_HERE + g, r * BLOCK:(r + 1) * BLOCK, :] = tile
                pooled_query[g, pl.ds(r * CHIP_BLOCKS + s, 1), :] = jnp.sum(
                    tile.astype(jnp.float32), axis=0, keepdims=True
                ) * (1.0 / BLOCK)

    for source in range(2):
        q_ref = (q_own_ref, q_other_ref)[source]

        @pl.loop(0, ROWS)
        def _(j):
            prepare(source * ROWS + j, q_ref, pl.multiple_of(j * BLOCK, BLOCK))

    slot_max[...] = jnp.full_like(slot_max, LOW)
    slot_sum[...] = jnp.zeros_like(slot_sum)
    filled, filled_far = make_lists(
        core, place_ref[1],
        ((offsets_own_ref, counts_own_ref), (offsets_other_ref, counts_other_ref)),
        near_list, near_work, far_list, far_work,
    )
    far_filled[0] = filled_far
    slot_loop(
        filled, near_work, near_list,
        lambda s, row: position(core, s) + jnp.minimum(row, SPAN) - SPAN,
        keys, queries, slot_max, slot_sum, True,
    )
    for g in range(KV_HERE):
        gate_key[g] = dot_f32(pooled_key[g], wk_ref[g], ((1,), (0,)))
        for r in range(GROUP):
            picked = slice(r * CHIP_BLOCKS, (r + 1) * CHIP_BLOCKS)
            gate_query[g, picked, :] = dot_f32(
                pooled_query[g, picked, :], wq_ref[g * GROUP + r], ((1,), (0,))
            )


def far_kernel(
    core_ref, far_list, far_work, far_filled,
    k_prev_own_ref, k_prev_other_ref, k_far_ref, queries,
    max_ref, sum_ref, pooled_query, gate_query, near_key, near_gate_key, wk_ref,
    out_ref,
    keys, slot_max, slot_sum, pooled_key, shares, hits,
):
    core = core_ref[0]
    half = ROWS * BLOCK
    for place, ref in ((0, k_far_ref), (1 + core, k_prev_own_ref), (2 - core, k_prev_other_ref)):
        tile = ref[...]
        at = place * half if isinstance(place, int) else pl.multiple_of(place * half, half)
        row = place * ROWS if isinstance(place, int) else pl.multiple_of(place * ROWS, ROWS)
        keys[pl.ds(at, half), :] = tile
        for g, pooled in enumerate(pool_keys(tile)):
            pooled_key[g, pl.ds(row, ROWS), :] = pooled
    for g in range(KV_HERE):
        pooled_key[g, SPAN:SPAN + CHIP_BLOCKS, :] = near_key[g]
    slot_max[...] = max_ref[...]
    slot_sum[...] = sum_ref[...]
    shares[...] = jnp.zeros_like(shares)
    hits[...] = jnp.zeros_like(hits)
    slot_loop(
        far_filled[0], far_work, far_list,
        lambda s, row: jnp.where(row <= SPAN, position(core, s) + row, 0),
        keys, queries, slot_max, slot_sum, False,
    )

    live = lax.broadcasted_iota(jnp.int32, (SLOT_ROWS, WIDTH), 0) <= SPAN
    spread = jnp.where(
        lax.broadcasted_iota(jnp.int32, (WIDTH, LANES), 0) // BLOCK
        == lax.broadcasted_iota(jnp.int32, (WIDTH, LANES), 1) // CHIP_BLOCKS,
        1.0 / BLOCK, 0.0,
    ).astype(jnp.bfloat16)
    lane_block = lax.broadcasted_iota(jnp.int32, (SLOT_ROWS, LANES), 1) % CHIP_BLOCKS

    @pl.loop(0, CHIP_BLOCKS // 4)
    def _(step):
        found = []
        for e in range(4):
            s = step * 4 + e
            for g in range(KV_HERE):
                tops = jnp.where(live, slot_max[s * KV_HERE + g], LOW)
                top = jnp.max(tops, axis=0, keepdims=True)
                weight = jnp.where(
                    live, slot_sum[s * KV_HERE + g] * jnp.exp2((tops - top) * EXP_SCALE), 0.0
                )
                share = weight / jnp.sum(weight, axis=0, keepdims=True)
                coarse = share.astype(jnp.bfloat16)
                fine = (share - coarse.astype(jnp.float32)).astype(jnp.bfloat16)
                mean = (
                    jnp.dot(coarse, spread, preferred_element_type=jnp.float32)
                    + jnp.dot(fine, spread, preferred_element_type=jnp.float32)
                )
                found.append((shares.at[g], position(core, s), jnp.where(lane_block == s, mean, 0.0)))
                if g == 0:
                    filled = jnp.where(tops > 0.5 * LOW, 1.0, 0.0).astype(jnp.bfloat16)
                    hit = jnp.dot(filled, spread, preferred_element_type=jnp.float32)
                    found.append((hits, position(core, s), jnp.where(lane_block == s, hit, 0.0)))
        for table, block, mine in found:
            table[pl.ds(block, SLOT_ROWS), :] += mine

    scale = 1.0 / math.sqrt(HEAD_DIM)
    window = SPAN + CHIP_BLOCKS
    usable = hits[0:window, :] > 0.5
    divergence = jnp.zeros((1, LANES), jnp.float32)
    key_base = CHIP_BLOCKS + ROWS
    for g in range(KV_HERE):
        far_gate_key = dot_f32(pooled_key[g, 0:SPAN, :], wk_ref[g], ((1,), (0,)))
        gate_key = jnp.concatenate([far_gate_key, near_gate_key[g]], axis=0)
        logits = dot_f32(gate_key, gate_query[g], ((1,), (1,))) * scale
        logits = jnp.where(usable, logits, LOW)
        top = jnp.max(logits, axis=0, keepdims=True)
        weight = jnp.where(usable, jnp.exp(logits - top), 0.0)
        mass = jnp.sum(weight, axis=0, keepdims=True)
        log_gate = jnp.where(usable, logits - top - jnp.log(mass), 0.0)
        target = shares[g, 0:window, :]
        log_target = jnp.log(jnp.where(target > 0.0, target, 1.0))
        terms = jnp.where(usable, target * (log_target - log_gate), 0.0)
        divergence += jnp.sum(terms, axis=0, keepdims=True)
        target = jnp.where(usable, target, 0.0)
        slope = (weight / mass) * jnp.sum(target, axis=0, keepdims=True) - target
        slope = slope * (scale / 32.0)
        d_query = dot_f32(slope, gate_key, ((0,), (0,)))
        d_key = dot_f32(slope, gate_query[g], ((1,), (0,)))
        for r in range(GROUP):
            at = r * CHIP_BLOCKS
            pooled = pooled_query[g, at:at + CHIP_BLOCKS, :]
            for part in range(2):
                share = (g * GROUP + r) * 2 + part
                cols = slice(part * HALF_HEAD, (part + 1) * HALF_HEAD)
                out_ref[share, 0:CHIP_BLOCKS, :] = d_query[at:at + CHIP_BLOCKS, :]
                out_ref[share, CHIP_BLOCKS:key_base, :] = jnp.concatenate(
                    [pooled[0:ROWS, cols], pooled[ROWS:CHIP_BLOCKS, cols]], axis=1
                )
        key_part = dot_f32(pooled_key[g], d_key, ((0,), (0,)))
        for i in range(SHARES // KV_HERE):
            out_ref[g * (SHARES // KV_HERE) + i, key_base:key_base + KEY_ROWS, :] = (
                key_part[i * KEY_ROWS:(i + 1) * KEY_ROWS, :]
            )
    total = jnp.sum(divergence)
    for i in range(SHARES):
        out_ref[i, PART_ROWS - 8:PART_ROWS, :] = jnp.full((8, HEAD_DIM), total, jnp.float32)


def sum_kernel(parts_ref, out_ref):
    parts = parts_ref[...]
    pooled = parts[:, CHIP_BLOCKS:CHIP_BLOCKS + ROWS, :].reshape(SHARES * ROWS, HEAD_DIM)
    early = parts[:, 0:ROWS, :].reshape(SHARES * ROWS, HEAD_DIM)
    late = parts[:, ROWS:CHIP_BLOCKS, :].reshape(SHARES * ROWS, HEAD_DIM)
    out_ref[0:HALF_HEAD, :] = (
        dot_f32(pooled[:, :HALF_HEAD], early, ((0,), (0,)))
        + dot_f32(pooled[:, HALF_HEAD:], late, ((0,), (0,)))
    )
    out_ref[HALF_HEAD:, :] = jnp.sum(parts[:, CHIP_BLOCKS + ROWS:, :], axis=0)


def cut_keys_kernel(core_ref, keys_ref, mine_ref, give_ref, sems):
    at = pl.multiple_of(core_ref[0] * K_COLS, K_COLS)
    other = pl.multiple_of((1 - core_ref[0]) * K_COLS, K_COLS)
    mine = pltpu.make_async_copy(keys_ref.at[:, pl.ds(at, K_COLS)], mine_ref, sems.at[0])
    give = pltpu.make_async_copy(keys_ref.at[:, pl.ds(other, K_COLS)], give_ref, sems.at[1])
    mine.start()
    give.start()
    mine.wait()
    give.wait()


def cut_queries_kernel(core_ref, queries_ref, give_ref, sems):
    other = pl.multiple_of((1 - core_ref[0]) * Q_COLS, Q_COLS)
    give = pltpu.make_async_copy(queries_ref.at[:, pl.ds(other, Q_COLS)], give_ref, sems.at[0])
    give.start()
    give.wait()


def cut(kernel, core, whole_array, outs, name):
    return pl.pallas_call(
        kernel,
        grid_spec=pltpu.PrefetchScalarGridSpec(
            num_scalar_prefetch=1,
            grid=(1,),
            in_specs=[pl.BlockSpec(memory_space=pl.ANY)],
            out_specs=[pl.BlockSpec(memory_space=pl.ANY)] * len(outs),
            scratch_shapes=[pltpu.SemaphoreType.DMA((2,))],
        ),
        out_shape=outs,
        name=name,
    )(core, whole_array)


def swap(x, axis):
    return lax.ppermute(x, axis, [(0, 1), (1, 0)])


def whole(*shape):
    return pl.BlockSpec(shape, lambda i, *_: (0,) * len(shape))


def shaped(shape, dtype=jnp.float32):
    return jax.ShapeDtypeStruct(shape, dtype)


def smem():
    return pl.BlockSpec(memory_space=pltpu.SMEM)


def near_call(place, tables, q_own, q_other, k_mine, k_other, wq, wk):
    half = ROWS * BLOCK
    outs = [
        shaped((CHIP_BLOCKS * KV_HERE, WIDTH, HEAD_DIM), jnp.bfloat16),
        shaped((CHIP_BLOCKS * KV_HERE, SLOT_ROWS, WIDTH)),
        shaped((CHIP_BLOCKS * KV_HERE, SLOT_ROWS, WIDTH)),
        shaped((KV_HERE, LANES, HEAD_DIM)),
        shaped((KV_HERE, LANES, HEAD_DIM)),
        shaped((KV_HERE, CHIP_BLOCKS, POOL)),
        shaped((KV_HERE, CHIP_BLOCKS, HEAD_DIM)),
    ]
    lists = [LIST_SIZE, WORK_SIZE, 1]
    return pl.pallas_call(
        near_kernel,
        grid_spec=pltpu.PrefetchScalarGridSpec(
            num_scalar_prefetch=1,
            grid=(1,),
            in_specs=[smem()] * 4 + [
                pl.BlockSpec((half, Q_COLS), lambda i, c: (0, c[0])),
                whole(half, Q_COLS),
                whole(half, K_COLS),
                whole(half, K_COLS),
                pl.BlockSpec((HEADS_HERE, HEAD_DIM, HEAD_DIM), lambda i, c: (c[0], 0, 0)),
                pl.BlockSpec((KV_HERE, POOL, HEAD_DIM), lambda i, c: (c[0], 0, 0)),
            ],
            out_specs=[whole(*o.shape) for o in outs] + [smem()] * 3,
            scratch_shapes=[
                pltpu.VMEM((CHIP_BLOCKS * BLOCK, K_COLS), jnp.bfloat16),
                pltpu.SMEM((LIST_SIZE,), jnp.int32),
                pltpu.SMEM((WORK_SIZE,), jnp.int32),
            ],
        ),
        out_shape=outs + [shaped((n,), jnp.int32) for n in lists],
        compiler_params=pltpu.CompilerParams(vmem_limit_bytes=VMEM_BYTES),
        cost_estimate=pl.CostEstimate(
            flops=2_000_000_000, bytes_accessed=8_000_000, transcendentals=8_000_000
        ),
        name="near",
    )(place, *tables, q_own, q_other, k_mine, k_other, wq, wk)


def far_call(place, k_prev_own, k_prev_other, k_far, near, wk):
    args = (k_prev_own, k_prev_other, k_far, *near[:-3])
    return pl.pallas_call(
        far_kernel,
        grid_spec=pltpu.PrefetchScalarGridSpec(
            num_scalar_prefetch=1,
            grid=(1,),
            in_specs=[smem()] * 3 + [whole(*a.shape) for a in args] + [
                pl.BlockSpec((KV_HERE, POOL, HEAD_DIM), lambda i, c: (c[0], 0, 0)),
            ],
            out_specs=whole(SHARES, PART_ROWS, HEAD_DIM),
            scratch_shapes=[
                pltpu.VMEM((SPAN * BLOCK, K_COLS), jnp.bfloat16),
                pltpu.VMEM((CHIP_BLOCKS * KV_HERE, SLOT_ROWS, WIDTH), jnp.float32),
                pltpu.VMEM((CHIP_BLOCKS * KV_HERE, SLOT_ROWS, WIDTH), jnp.float32),
                pltpu.VMEM((KV_HERE, SPAN + CHIP_BLOCKS, POOL), jnp.float32),
                pltpu.VMEM((KV_HERE, PADDED, LANES), jnp.float32),
                pltpu.VMEM((PADDED, LANES), jnp.float32),
            ],
        ),
        out_shape=shaped((SHARES, PART_ROWS, HEAD_DIM)),
        compiler_params=pltpu.CompilerParams(vmem_limit_bytes=VMEM_BYTES),
        cost_estimate=pl.CostEstimate(
            flops=2_000_000_000, bytes_accessed=8_000_000, transcendentals=8_000_000
        ),
        name="far",
    )(place, *near[-3:], *args, wk)


def body(
    teacher_queries, teacher_keys, query_projection, key_projection, block_offsets, valid_counts
):
    chips = ("za", "zb", "yh", "x")
    places = chips + ("core",)
    count = lax.axis_size(places)
    core = lax.axis_index("core")
    place = jnp.stack([core, lax.axis_index(chips)]).astype(jnp.int32)
    half = ROWS * BLOCK

    k_mine, k_give = cut(
        cut_keys_kernel, place, teacher_keys, [shaped((half, K_COLS), jnp.bfloat16)] * 2, "cut_keys"
    )
    k_prev_own = lax.ppermute(k_mine, places, [(i, i + 2) for i in range(count - 2)])
    k_prev_other = lax.ppermute(
        k_give, places, [(i, (i ^ 1) + 2) for i in range(count - 2)]
    )
    k_other = swap(k_give, "core")
    (q_give,) = cut(
        cut_queries_kernel, place, teacher_queries, [shaped((half, Q_COLS), jnp.bfloat16)], "cut_queries"
    )
    q_other = swap(q_give, "core")
    tables = (block_offsets, valid_counts, swap(block_offsets, "core"), swap(valid_counts, "core"))
    k_far = lax.ppermute(
        jnp.where(core == 1, k_mine, k_other), places, [(i, i + 4) for i in range(count - 4)]
    )
    near = near_call(
        place, tables, teacher_queries, q_other, k_mine, k_other, query_projection, key_projection
    )
    parts = far_call(place, k_prev_own, k_prev_other, k_far, near, key_projection)

    group = ("zb", "yh", "x")
    got = lax.all_to_all(parts, group, 0, 0)
    got = pl.pallas_call(sum_kernel, out_shape=shaped((SUM_ROWS + 8, HEAD_DIM)), name="sum")(got)
    one, two, three = (
        lax.ppermute(got, "za", [(i, i ^ step) for i in range(4)]) for step in (1, 2, 3)
    )
    got = (got + one) + (two + three)
    total = got[SUM_ROWS:SUM_ROWS + 1, :]
    total = total + swap(total, "head")
    total = total + swap(total, "core")
    spread = jnp.broadcast_to(got[:SUM_ROWS], (SHARES, SUM_ROWS, HEAD_DIM))
    mine = lax.all_to_all(spread, group, 0, 0)
    other = swap(mine, "core")
    first = jnp.where(core == 0, mine, other)
    second = jnp.where(core == 0, other, mine)
    both = jnp.concatenate([first, second], axis=0)
    query_gradient = both[:, :HALF_HEAD].reshape(2 * HEADS_HERE, HEAD_DIM, HEAD_DIM)
    key_gradient = both[:, HALF_HEAD:].reshape(2 * KV_HERE, POOL, HEAD_DIM)
    return query_gradient, key_gradient, total[0, 0] / (1024 * HEADS)


def solution(mesh):
    split = Mesh(mesh.devices.reshape(4, 2, 2, 4, 2, 2), ("za", "zb", "yh", "x", "core", "head"))
    ctx = ("za", "zb", "yh", "x", "core")
    placed = (
        P(ctx, "head"),
        P(ctx, "head"),
        P("head", None, None),
        P("head", None, None),
        P(ctx, None),
        P(ctx),
    )
    return jax.shard_map(
        body,
        mesh=split,
        in_specs=placed,
        out_specs=(P("head", None, None), P("head", None, None), P()),
        check_vma=False,
    )
```

```python
import math

import jax
import jax.numpy as jnp
from jax import lax
from jax.experimental import pallas as pl
from jax.experimental.pallas import tpu as pltpu
from jax.sharding import Mesh, PartitionSpec as P

HEADS = 32
KV_HEADS = 8
HEAD_DIM = 128
BLOCK = 64
CAND = 24
REACH = 4

ROWS = 8
SPAN = 24
CHIP_BLOCKS = 2 * ROWS
PADDED = 48
KV_HERE = 2
GROUP = HEADS // KV_HEADS
HEADS_HERE = KV_HERE * GROUP
Q_COLS = HEADS_HERE * HEAD_DIM
K_COLS = KV_HERE * HEAD_DIM
POOL = 3 * HEAD_DIM
WIDTH = GROUP * BLOCK
DUMMY = 31
SLOT_ROWS = 32
LANES = GROUP * CHIP_BLOCKS
SHARES = 16
KEY_ROWS = KV_HERE * POOL // SHARES
HALF_HEAD = HEAD_DIM // 2
PART_ROWS = CHIP_BLOCKS + ROWS + KEY_ROWS + 8
SUM_ROWS = HALF_HEAD + KEY_ROWS
VMEM_BYTES = 40 * 1024 * 1024
UNROLL = 3
NOTE_ROWS = 16
LIST_SIZE = CHIP_BLOCKS * CAND + 8
WORK_SIZE = CHIP_BLOCKS * CAND // 4 + 8
LOW = -1e30
EXP_SCALE = math.log2(math.e) / math.sqrt(HEAD_DIM)
HIGH = lax.Precision.HIGHEST


def dot_f32(a, b, dims):
    return lax.dot_general(
        a, b, (dims, ((), ())), precision=HIGH, preferred_element_type=jnp.float32
    )


def pool_keys(tile):
    wide = tile.astype(jnp.float32).reshape(ROWS, BLOCK, K_COLS)
    top = jnp.max(wide, axis=1)
    low = jnp.min(wide, axis=1)
    mean = jnp.sum(wide, axis=1) * (1.0 / BLOCK)
    return [
        jnp.concatenate(
            [v[:, g * HEAD_DIM:(g + 1) * HEAD_DIM] for v in (top, low, mean)], axis=1
        )
        for g in range(KV_HERE)
    ]


def make_lists(core, chip, tables, near_list, near_work, far_list, far_work):
    filled = (jnp.int32(0), jnp.int32(0))
    for source, table in enumerate(tables):
        first = ROWS * core if source == 0 else ROWS * (1 - core)

        def per_block(j, filled):
            block = first + j
            limit = chip * CHIP_BLOCKS + block
            count = table(j, CAND)
            base = (source * ROWS + j) * CAND
            near_end = far_end = base
            for c in range(CAND):
                offset = table(j, c)
                here = (c < count) & (offset <= limit)
                near = jnp.where(here & (offset <= block), 1, 0)
                far = jnp.where(here & (offset > block), 1, 0)
                near_list[near_end] = SPAN - offset
                far_list[far_end] = SPAN - offset
                near_end += near
                far_end += far
            out = []
            for end, slots, work, total in zip(
                (near_end, far_end), (near_list, far_list), (near_work, far_work), filled
            ):
                for extra in range(3):
                    slots[end + extra] = DUMMY
                for i in range(CAND // 4):
                    work[total] = base + i * 4
                    total += jnp.where(i * 4 < end - base, 1, 0)
                out.append(total)
            return tuple(out)

        filled = lax.fori_loop(0, ROWS, per_block, filled)
    for work, total in zip((near_work, far_work), filled):
        spare = jnp.where(total > 0, work[jnp.maximum(total - 1, 0)], 0)
        for extra in range(UNROLL - 1):
            work[total + extra] = spare
    return filled


def position(core, s):
    return jnp.where(s < ROWS, ROWS * core + s, ROWS * (1 - core) + s - ROWS)


def slot_loop(filled, work, list_ref, tile_start, keys, queries, slot_max, slot_sum, diagonal):
    lane = lax.broadcasted_iota(jnp.int32, (BLOCK, WIDTH), 1) % BLOCK
    key_row = lax.broadcasted_iota(jnp.int32, (BLOCK, WIDTH), 0)

    @pl.loop(0, (filled + UNROLL - 1) // UNROLL)
    def _(step):
        found = []
        for e in range(UNROLL):
            first = work[step * UNROLL + e]
            s = first // CAND
            rows = [list_ref[first + i] for i in range(4)]
            starts = [pl.multiple_of(tile_start(s, row) * BLOCK, BLOCK) for row in rows]
            if diagonal:
                keep = key_row <= lane + jnp.where(first == s * CAND, 0, BLOCK)
            for g in range(KV_HERE):
                tiles = [
                    keys[pl.ds(start, BLOCK), g * HEAD_DIM:(g + 1) * HEAD_DIM] for start in starts
                ]
                scores = lax.dot_general(
                    jnp.concatenate(tiles, axis=0), queries[s * KV_HERE + g],
                    (((1,), (1,)), ((), ())), preferred_element_type=jnp.float32,
                )
                for i, row in enumerate(rows):
                    part = scores[i * BLOCK:(i + 1) * BLOCK, :]
                    if diagonal and i == 0:
                        part = jnp.where(keep, part, LOW)
                    top = jnp.max(part, axis=0, keepdims=True)
                    total = jnp.sum(
                        jnp.exp2((part - top) * EXP_SCALE), axis=0, keepdims=True
                    )
                    found.append((s * KV_HERE + g, row, top, total))
        for index, row, top, total in found:
            slot_max[index, pl.ds(row, 1), :] = top
            slot_sum[index, pl.ds(row, 1), :] = total


def near_kernel(
    place_ref, offsets_ref, counts_ref,
    q_own_ref, q_other_ref, k_own_ref, k_other_ref, wq_ref, wk_ref,
    queries, slot_max, slot_sum, pooled_query, gate_query, pooled_key, gate_key,
    far_list, far_work, far_filled,
    keys, near_list, near_work, note_vector, note_scalar, sems,
):
    core_ref = place_ref
    note_vector[...] = q_other_ref[ROWS * BLOCK:, 0:HEAD_DIM].astype(jnp.float32).astype(jnp.int32)
    note_copy = pltpu.make_async_copy(note_vector, note_scalar, sems.at[0])
    note_copy.start()
    core = core_ref[0]
    half = ROWS * BLOCK
    for source, ref in ((core, k_own_ref), (1 - core, k_other_ref)):
        tile = ref[...]
        keys[pl.ds(pl.multiple_of(source * half, half), half), :] = tile
        for g, pooled in enumerate(pool_keys(tile)):
            pooled_key[g, pl.ds(pl.multiple_of(source * ROWS, ROWS), ROWS), :] = pooled

    def prepare(s, q_ref, at):
        for g in range(KV_HERE):
            for r in range(GROUP):
                head = g * GROUP + r
                tile = q_ref[pl.ds(at, BLOCK), head * HEAD_DIM:(head + 1) * HEAD_DIM]
                queries[s * KV_HERE + g, r * BLOCK:(r + 1) * BLOCK, :] = tile
                pooled_query[g, pl.ds(r * CHIP_BLOCKS + s, 1), :] = jnp.sum(
                    tile.astype(jnp.float32), axis=0, keepdims=True
                ) * (1.0 / BLOCK)

    for source in range(2):
        q_ref = (q_own_ref, q_other_ref)[source]

        @pl.loop(0, ROWS)
        def _(j):
            prepare(source * ROWS + j, q_ref, pl.multiple_of(j * BLOCK, BLOCK))

    slot_max[...] = jnp.full_like(slot_max, LOW)
    slot_sum[...] = jnp.zeros_like(slot_sum)
    note_copy.wait()
    filled, filled_far = make_lists(
        core, place_ref[1],
        (
            lambda j, c: counts_ref[j] if c == CAND else offsets_ref[j, c],
            lambda j, c: note_scalar[j, c],
        ),
        near_list, near_work, far_list, far_work,
    )
    far_filled[0] = filled_far
    slot_loop(
        filled, near_work, near_list,
        lambda s, row: position(core, s) + jnp.minimum(row, SPAN) - SPAN,
        keys, queries, slot_max, slot_sum, True,
    )
    for g in range(KV_HERE):
        gate_key[g] = dot_f32(pooled_key[g], wk_ref[g], ((1,), (0,)))
        for r in range(GROUP):
            picked = slice(r * CHIP_BLOCKS, (r + 1) * CHIP_BLOCKS)
            gate_query[g, picked, :] = dot_f32(
                pooled_query[g, picked, :], wq_ref[g * GROUP + r], ((1,), (0,))
            )


def far_kernel(
    core_ref, far_list, far_work, far_filled,
    k_prev_own_ref, k_prev_other_ref, k_far_ref, queries,
    max_ref, sum_ref, pooled_query, gate_query, near_key, near_gate_key, wk_ref,
    out_ref,
    keys, slot_max, slot_sum, pooled_key, shares, hits,
):
    core = core_ref[0]
    half = ROWS * BLOCK
    for place, ref in ((0, k_far_ref), (1 + core, k_prev_own_ref), (2 - core, k_prev_other_ref)):
        tile = ref[...]
        at = place * half if isinstance(place, int) else pl.multiple_of(place * half, half)
        row = place * ROWS if isinstance(place, int) else pl.multiple_of(place * ROWS, ROWS)
        keys[pl.ds(at, half), :] = tile
        for g, pooled in enumerate(pool_keys(tile)):
            pooled_key[g, pl.ds(row, ROWS), :] = pooled
    for g in range(KV_HERE):
        pooled_key[g, SPAN:SPAN + CHIP_BLOCKS, :] = near_key[g]
    slot_max[...] = max_ref[...]
    slot_sum[...] = sum_ref[...]
    shares[...] = jnp.zeros_like(shares)
    hits[...] = jnp.zeros_like(hits)
    slot_loop(
        far_filled[0], far_work, far_list,
        lambda s, row: jnp.where(row <= SPAN, position(core, s) + row, 0),
        keys, queries, slot_max, slot_sum, False,
    )

    live = lax.broadcasted_iota(jnp.int32, (SLOT_ROWS, WIDTH), 0) <= SPAN
    spread = jnp.where(
        lax.broadcasted_iota(jnp.int32, (WIDTH, LANES), 0) // BLOCK
        == lax.broadcasted_iota(jnp.int32, (WIDTH, LANES), 1) // CHIP_BLOCKS,
        1.0 / BLOCK, 0.0,
    ).astype(jnp.bfloat16)
    lane_block = lax.broadcasted_iota(jnp.int32, (SLOT_ROWS, LANES), 1) % CHIP_BLOCKS

    @pl.loop(0, CHIP_BLOCKS // 4)
    def _(step):
        found = []
        for e in range(4):
            s = step * 4 + e
            for g in range(KV_HERE):
                tops = jnp.where(live, slot_max[s * KV_HERE + g], LOW)
                top = jnp.max(tops, axis=0, keepdims=True)
                weight = jnp.where(
                    live, slot_sum[s * KV_HERE + g] * jnp.exp2((tops - top) * EXP_SCALE), 0.0
                )
                share = weight / jnp.sum(weight, axis=0, keepdims=True)
                coarse = share.astype(jnp.bfloat16)
                fine = (share - coarse.astype(jnp.float32)).astype(jnp.bfloat16)
                mean = (
                    jnp.dot(coarse, spread, preferred_element_type=jnp.float32)
                    + jnp.dot(fine, spread, preferred_element_type=jnp.float32)
                )
                found.append((shares.at[g], position(core, s), jnp.where(lane_block == s, mean, 0.0)))
                if g == 0:
                    filled = jnp.where(tops > 0.5 * LOW, 1.0, 0.0).astype(jnp.bfloat16)
                    hit = jnp.dot(filled, spread, preferred_element_type=jnp.float32)
                    found.append((hits, position(core, s), jnp.where(lane_block == s, hit, 0.0)))
        for table, block, mine in found:
            table[pl.ds(block, SLOT_ROWS), :] += mine

    scale = 1.0 / math.sqrt(HEAD_DIM)
    window = SPAN + CHIP_BLOCKS
    usable = hits[0:window, :] > 0.5
    divergence = jnp.zeros((1, LANES), jnp.float32)
    key_base = CHIP_BLOCKS + ROWS
    for g in range(KV_HERE):
        far_gate_key = dot_f32(pooled_key[g, 0:SPAN, :], wk_ref[g], ((1,), (0,)))
        gate_key = jnp.concatenate([far_gate_key, near_gate_key[g]], axis=0)
        logits = dot_f32(gate_key, gate_query[g], ((1,), (1,))) * scale
        logits = jnp.where(usable, logits, LOW)
        top = jnp.max(logits, axis=0, keepdims=True)
        weight = jnp.where(usable, jnp.exp(logits - top), 0.0)
        mass = jnp.sum(weight, axis=0, keepdims=True)
        log_gate = jnp.where(usable, logits - top - jnp.log(mass), 0.0)
        target = shares[g, 0:window, :]
        log_target = jnp.log(jnp.where(target > 0.0, target, 1.0))
        terms = jnp.where(usable, target * (log_target - log_gate), 0.0)
        divergence += jnp.sum(terms, axis=0, keepdims=True)
        target = jnp.where(usable, target, 0.0)
        slope = (weight / mass) * jnp.sum(target, axis=0, keepdims=True) - target
        slope = slope * (scale / 32.0)
        d_query = dot_f32(slope, gate_key, ((0,), (0,)))
        d_key = dot_f32(slope, gate_query[g], ((1,), (0,)))
        for r in range(GROUP):
            at = r * CHIP_BLOCKS
            pooled = pooled_query[g, at:at + CHIP_BLOCKS, :]
            for part in range(2):
                share = (g * GROUP + r) * 2 + part
                cols = slice(part * HALF_HEAD, (part + 1) * HALF_HEAD)
                out_ref[share, 0:CHIP_BLOCKS, :] = d_query[at:at + CHIP_BLOCKS, :]
                out_ref[share, CHIP_BLOCKS:key_base, :] = jnp.concatenate(
                    [pooled[0:ROWS, cols], pooled[ROWS:CHIP_BLOCKS, cols]], axis=1
                )
        key_part = dot_f32(pooled_key[g], d_key, ((0,), (0,)))
        for i in range(SHARES // KV_HERE):
            out_ref[g * (SHARES // KV_HERE) + i, key_base:key_base + KEY_ROWS, :] = (
                key_part[i * KEY_ROWS:(i + 1) * KEY_ROWS, :]
            )
    total = jnp.sum(divergence)
    for i in range(SHARES):
        out_ref[i, PART_ROWS - 8:PART_ROWS, :] = jnp.full((8, HEAD_DIM), total, jnp.float32)


def sum_kernel(parts_ref, out_ref):
    parts = parts_ref[...]
    pooled = parts[:, CHIP_BLOCKS:CHIP_BLOCKS + ROWS, :].reshape(SHARES * ROWS, HEAD_DIM)
    early = parts[:, 0:ROWS, :].reshape(SHARES * ROWS, HEAD_DIM)
    late = parts[:, ROWS:CHIP_BLOCKS, :].reshape(SHARES * ROWS, HEAD_DIM)
    out_ref[0:HALF_HEAD, :] = (
        dot_f32(pooled[:, :HALF_HEAD], early, ((0,), (0,)))
        + dot_f32(pooled[:, HALF_HEAD:], late, ((0,), (0,)))
    )
    out_ref[HALF_HEAD:, :] = jnp.sum(parts[:, CHIP_BLOCKS + ROWS:, :], axis=0)


def cut_keys_kernel(place_ref, mine_in, give_in, mine_ref, give_ref):
    mine_ref[...] = mine_in[...]
    give_ref[...] = give_in[...]


def cut_queries_kernel(place_ref, counts_ref, offsets_ref, give_in, give_ref):
    half = ROWS * BLOCK
    give_ref[0:half, :] = give_in[...]
    row = lax.broadcasted_iota(jnp.int32, (ROWS, HEAD_DIM), 0)
    lane = lax.broadcasted_iota(jnp.int32, (ROWS, HEAD_DIM), 1)
    note = jnp.concatenate(
        [offsets_ref[...], jnp.zeros((ROWS, HEAD_DIM - CAND), jnp.int32)], axis=1
    )
    for j in range(ROWS):
        note = jnp.where((lane == CAND) & (row == j), counts_ref[j], note)
    note = note.astype(jnp.float32).astype(jnp.bfloat16)
    give_ref[half:, :] = jnp.zeros((NOTE_ROWS, Q_COLS), jnp.bfloat16)
    give_ref[half:, 0:HEAD_DIM] = jnp.concatenate([note, jnp.zeros_like(note)], axis=0)


def swap(x, axis):
    return lax.ppermute(x, axis, [(0, 1), (1, 0)])


def whole(*shape):
    return pl.BlockSpec(shape, lambda i, *_: (0,) * len(shape))


def shaped(shape, dtype=jnp.float32):
    return jax.ShapeDtypeStruct(shape, dtype)


def smem():
    return pl.BlockSpec(memory_space=pltpu.SMEM)


def cut_keys(place, keys):
    half = ROWS * BLOCK
    return pl.pallas_call(
        cut_keys_kernel,
        grid_spec=pltpu.PrefetchScalarGridSpec(
            num_scalar_prefetch=1,
            grid=(1,),
            in_specs=[
                pl.BlockSpec((half, K_COLS), lambda i, c: (0, c[0])),
                pl.BlockSpec((half, K_COLS), lambda i, c: (0, 1 - c[0])),
            ],
            out_specs=[whole(half, K_COLS)] * 2,
        ),
        out_shape=[shaped((half, K_COLS), jnp.bfloat16)] * 2,
        name="cut_keys",
    )(place, keys, keys)


def cut_queries(place, queries, offsets, counts):
    half = ROWS * BLOCK
    return pl.pallas_call(
        cut_queries_kernel,
        grid_spec=pltpu.PrefetchScalarGridSpec(
            num_scalar_prefetch=1,
            grid=(1,),
            in_specs=[
                smem(),
                whole(ROWS, CAND),
                pl.BlockSpec((half, Q_COLS), lambda i, c: (0, 1 - c[0])),
            ],
            out_specs=whole(half + NOTE_ROWS, Q_COLS),
        ),
        out_shape=shaped((half + NOTE_ROWS, Q_COLS), jnp.bfloat16),
        name="cut_queries",
    )(place, counts, offsets, queries)


def near_call(place, tables, q_own, q_other, k_mine, k_other, wq, wk):
    half = ROWS * BLOCK
    outs = [
        shaped((CHIP_BLOCKS * KV_HERE, WIDTH, HEAD_DIM), jnp.bfloat16),
        shaped((CHIP_BLOCKS * KV_HERE, SLOT_ROWS, WIDTH)),
        shaped((CHIP_BLOCKS * KV_HERE, SLOT_ROWS, WIDTH)),
        shaped((KV_HERE, LANES, HEAD_DIM)),
        shaped((KV_HERE, LANES, HEAD_DIM)),
        shaped((KV_HERE, CHIP_BLOCKS, POOL)),
        shaped((KV_HERE, CHIP_BLOCKS, HEAD_DIM)),
    ]
    lists = [LIST_SIZE, WORK_SIZE, 1]
    return pl.pallas_call(
        near_kernel,
        grid_spec=pltpu.PrefetchScalarGridSpec(
            num_scalar_prefetch=1,
            grid=(1,),
            in_specs=[smem()] * 2 + [
                pl.BlockSpec((half, Q_COLS), lambda i, c: (0, c[0])),
                whole(half + NOTE_ROWS, Q_COLS),
                whole(half, K_COLS),
                whole(half, K_COLS),
                pl.BlockSpec((HEADS_HERE, HEAD_DIM, HEAD_DIM), lambda i, c: (c[0], 0, 0)),
                pl.BlockSpec((KV_HERE, POOL, HEAD_DIM), lambda i, c: (c[0], 0, 0)),
            ],
            out_specs=[whole(*o.shape) for o in outs] + [smem()] * 3,
            scratch_shapes=[
                pltpu.VMEM((CHIP_BLOCKS * BLOCK, K_COLS), jnp.bfloat16),
                pltpu.SMEM((LIST_SIZE,), jnp.int32),
                pltpu.SMEM((WORK_SIZE,), jnp.int32),
                pltpu.VMEM((NOTE_ROWS, HEAD_DIM), jnp.int32),
                pltpu.SMEM((NOTE_ROWS, HEAD_DIM), jnp.int32),
                pltpu.SemaphoreType.DMA((1,)),
            ],
        ),
        out_shape=outs + [shaped((n,), jnp.int32) for n in lists],
        compiler_params=pltpu.CompilerParams(vmem_limit_bytes=VMEM_BYTES),
        cost_estimate=pl.CostEstimate(
            flops=2_000_000_000, bytes_accessed=8_000_000, transcendentals=8_000_000
        ),
        name="near",
    )(place, *tables, q_own, q_other, k_mine, k_other, wq, wk)


def far_call(place, k_prev_own, k_prev_other, k_far, near, wk):
    args = (k_prev_own, k_prev_other, k_far, *near[:-3])
    return pl.pallas_call(
        far_kernel,
        grid_spec=pltpu.PrefetchScalarGridSpec(
            num_scalar_prefetch=1,
            grid=(1,),
            in_specs=[smem()] * 3 + [whole(*a.shape) for a in args] + [
                pl.BlockSpec((KV_HERE, POOL, HEAD_DIM), lambda i, c: (c[0], 0, 0)),
            ],
            out_specs=whole(SHARES, PART_ROWS, HEAD_DIM),
            scratch_shapes=[
                pltpu.VMEM((SPAN * BLOCK, K_COLS), jnp.bfloat16),
                pltpu.VMEM((CHIP_BLOCKS * KV_HERE, SLOT_ROWS, WIDTH), jnp.float32),
                pltpu.VMEM((CHIP_BLOCKS * KV_HERE, SLOT_ROWS, WIDTH), jnp.float32),
                pltpu.VMEM((KV_HERE, SPAN + CHIP_BLOCKS, POOL), jnp.float32),
                pltpu.VMEM((KV_HERE, PADDED, LANES), jnp.float32),
                pltpu.VMEM((PADDED, LANES), jnp.float32),
            ],
        ),
        out_shape=shaped((SHARES, PART_ROWS, HEAD_DIM)),
        compiler_params=pltpu.CompilerParams(vmem_limit_bytes=VMEM_BYTES),
        cost_estimate=pl.CostEstimate(
            flops=2_000_000_000, bytes_accessed=8_000_000, transcendentals=8_000_000
        ),
        name="far",
    )(place, *near[-3:], *args, wk)


def body(
    teacher_queries, teacher_keys, query_projection, key_projection, block_offsets, valid_counts
):
    chips = ("za", "zb", "yh", "x")
    places = chips + ("core",)
    count = lax.axis_size(places)
    core = lax.axis_index("core")
    place = jnp.stack([core, lax.axis_index(chips)]).astype(jnp.int32)

    k_mine, k_give = cut_keys(place, teacher_keys)
    k_prev_own = lax.ppermute(k_mine, places, [(i, i + 2) for i in range(count - 2)])
    k_prev_other = lax.ppermute(
        k_give, places, [(i, (i ^ 1) + 2) for i in range(count - 2)]
    )
    k_other = swap(k_give, "core")
    q_other = swap(cut_queries(place, teacher_queries, block_offsets, valid_counts), "core")
    k_far = lax.ppermute(
        jnp.where(core == 1, k_mine, k_other), places, [(i, i + 4) for i in range(count - 4)]
    )
    near = near_call(
        place, (block_offsets, valid_counts), teacher_queries, q_other, k_mine, k_other, query_projection, key_projection
    )
    parts = far_call(place, k_prev_own, k_prev_other, k_far, near, key_projection)

    group = ("zb", "yh", "x")
    got = lax.all_to_all(parts, group, 0, 0)
    got = pl.pallas_call(sum_kernel, out_shape=shaped((SUM_ROWS + 8, HEAD_DIM)), name="sum")(got)
    one, two, three = (
        lax.ppermute(got, "za", [(i, i ^ step) for i in range(4)]) for step in (1, 2, 3)
    )
    got = (got + one) + (two + three)
    total = got[SUM_ROWS:SUM_ROWS + 1, :]
    total = total + swap(total, "head")
    total = total + swap(total, "core")
    spread = jnp.broadcast_to(got[:SUM_ROWS], (SHARES, SUM_ROWS, HEAD_DIM))
    mine = lax.all_to_all(spread, group, 0, 0)
    other = swap(mine, "core")
    first = jnp.where(core == 0, mine, other)
    second = jnp.where(core == 0, other, mine)
    both = jnp.concatenate([first, second], axis=0)
    query_gradient = both[:, :HALF_HEAD].reshape(2 * HEADS_HERE, HEAD_DIM, HEAD_DIM)
    key_gradient = both[:, HALF_HEAD:].reshape(2 * KV_HERE, POOL, HEAD_DIM)
    return query_gradient, key_gradient, total[0, 0] / (1024 * HEADS)


def solution(mesh):
    split = Mesh(mesh.devices.reshape(4, 2, 2, 4, 2, 2), ("za", "zb", "yh", "x", "core", "head"))
    ctx = ("za", "zb", "yh", "x", "core")
    placed = (
        P(ctx, "head"),
        P(ctx, "head"),
        P("head", None, None),
        P("head", None, None),
        P(ctx, None),
        P(ctx),
    )
    return jax.shard_map(
        body,
        mesh=split,
        in_specs=placed,
        out_specs=(P("head", None, None), P("head", None, None), P()),
        check_vma=False,
    )
```

```python
import math

import jax
import jax.numpy as jnp
from jax import lax
from jax.experimental import pallas as pl
from jax.experimental.pallas import tpu as pltpu
from jax.sharding import Mesh, PartitionSpec as P

HEADS = 32
KV_HEADS = 8
HEAD_DIM = 128
BLOCK = 64
CAND = 24
REACH = 4

ROWS = 8
SPAN = 24
CHIP_BLOCKS = 2 * ROWS
PADDED = 48
KV_HERE = 2
GROUP = HEADS // KV_HEADS
HEADS_HERE = KV_HERE * GROUP
Q_COLS = HEADS_HERE * HEAD_DIM
K_COLS = KV_HERE * HEAD_DIM
POOL = 3 * HEAD_DIM
WIDTH = GROUP * BLOCK
DUMMY = 31
SLOT_ROWS = 32
LANES = GROUP * CHIP_BLOCKS
SHARES = 16
KEY_ROWS = KV_HERE * POOL // SHARES
HALF_HEAD = HEAD_DIM // 2
PART_ROWS = CHIP_BLOCKS + ROWS + KEY_ROWS + 8
SUM_ROWS = HALF_HEAD + KEY_ROWS
VMEM_BYTES = 40 * 1024 * 1024
UNROLL = 3
NOTE_ROWS = 16
TILE = 16
LEVELS = 32760.0
LIST_SIZE = CHIP_BLOCKS * CAND + 8
WORK_SIZE = CHIP_BLOCKS * CAND // 4 + 8
LOW = -1e30
EXP_SCALE = math.log2(math.e) / math.sqrt(HEAD_DIM)
HIGH = lax.Precision.HIGHEST


def dot_f32(a, b, dims):
    return lax.dot_general(
        a, b, (dims, ((), ())), precision=HIGH, preferred_element_type=jnp.float32
    )


def pool_keys(tile):
    wide = tile.astype(jnp.float32).reshape(ROWS, BLOCK, K_COLS)
    top = jnp.max(wide, axis=1)
    low = jnp.min(wide, axis=1)
    mean = jnp.sum(wide, axis=1) * (1.0 / BLOCK)
    return [
        jnp.concatenate(
            [v[:, g * HEAD_DIM:(g + 1) * HEAD_DIM] for v in (top, low, mean)], axis=1
        )
        for g in range(KV_HERE)
    ]


def make_lists(core, chip, tables, near_list, near_work, far_list, far_work):
    filled = (jnp.int32(0), jnp.int32(0))
    for source, table in enumerate(tables):
        first = ROWS * core if source == 0 else ROWS * (1 - core)

        def per_block(j, filled):
            block = first + j
            limit = chip * CHIP_BLOCKS + block
            count = table(j, CAND)
            base = (source * ROWS + j) * CAND
            near_end = far_end = base
            for c in range(CAND):
                offset = table(j, c)
                here = (c < count) & (offset <= limit)
                near = jnp.where(here & (offset <= block), 1, 0)
                far = jnp.where(here & (offset > block), 1, 0)
                near_list[near_end] = SPAN - offset
                far_list[far_end] = SPAN - offset
                near_end += near
                far_end += far
            out = []
            for end, slots, work, total in zip(
                (near_end, far_end), (near_list, far_list), (near_work, far_work), filled
            ):
                for extra in range(3):
                    slots[end + extra] = DUMMY
                for i in range(CAND // 4):
                    work[total] = base + i * 4
                    total += jnp.where(i * 4 < end - base, 1, 0)
                out.append(total)
            return tuple(out)

        filled = lax.fori_loop(0, ROWS, per_block, filled)
    for work, total in zip((near_work, far_work), filled):
        spare = jnp.where(total > 0, work[jnp.maximum(total - 1, 0)], 0)
        for extra in range(UNROLL - 1):
            work[total + extra] = spare
    return filled


def position(core, s):
    return jnp.where(s < ROWS, ROWS * core + s, ROWS * (1 - core) + s - ROWS)


def slot_loop(filled, work, list_ref, tile_start, keys, queries, slot_max, slot_sum, diagonal):
    lane = lax.broadcasted_iota(jnp.int32, (BLOCK, WIDTH), 1) % BLOCK
    key_row = lax.broadcasted_iota(jnp.int32, (BLOCK, WIDTH), 0)

    @pl.loop(0, (filled + UNROLL - 1) // UNROLL)
    def _(step):
        found = []
        for e in range(UNROLL):
            first = work[step * UNROLL + e]
            s = first // CAND
            rows = [list_ref[first + i] for i in range(4)]
            starts = [pl.multiple_of(tile_start(s, row) * BLOCK, BLOCK) for row in rows]
            if diagonal:
                keep = key_row <= lane + jnp.where(first == s * CAND, 0, BLOCK)
            for g in range(KV_HERE):
                tiles = [
                    keys[pl.ds(start, BLOCK), g * HEAD_DIM:(g + 1) * HEAD_DIM] for start in starts
                ]
                scores = lax.dot_general(
                    jnp.concatenate(tiles, axis=0), queries[s * KV_HERE + g],
                    (((1,), (1,)), ((), ())), preferred_element_type=jnp.float32,
                )
                for i, row in enumerate(rows):
                    part = scores[i * BLOCK:(i + 1) * BLOCK, :]
                    if diagonal and i == 0:
                        part = jnp.where(keep, part, LOW)
                    top = jnp.max(part, axis=0, keepdims=True)
                    total = jnp.sum(
                        jnp.exp2((part - top) * EXP_SCALE), axis=0, keepdims=True
                    )
                    found.append((s * KV_HERE + g, row, top, total))
        for index, row, top, total in found:
            slot_max[index, pl.ds(row, 1), :] = top
            slot_sum[index, pl.ds(row, 1), :] = total


def near_kernel(
    place_ref, offsets_ref, counts_ref,
    q_own_hbm, q_other_ref, k_own_ref, k_other_ref, wq_hbm, wk_hbm,
    queries, slot_max, slot_sum, pooled_query, gate_query, pooled_key, gate_key,
    far_list, far_work, far_filled,
    keys, near_list, near_work, note_vector, note_scalar, q_own_ref, wq_ref, wk_ref, sems,
):
    core_ref = place_ref
    note_vector[...] = q_other_ref[ROWS * BLOCK:, 0:HEAD_DIM].astype(jnp.float32).astype(jnp.int32)
    note_copy = pltpu.make_async_copy(note_vector, note_scalar, sems.at[0])
    note_copy.start()
    core = core_ref[0]
    half = ROWS * BLOCK
    q_copy = pltpu.make_async_copy(
        q_own_hbm.at[:, pl.ds(pl.multiple_of(core * Q_COLS, Q_COLS), Q_COLS)], q_own_ref, sems.at[1]
    )
    wq_copy = pltpu.make_async_copy(
        wq_hbm.at[pl.ds(core * HEADS_HERE, HEADS_HERE)], wq_ref, sems.at[2]
    )
    wk_copy = pltpu.make_async_copy(
        wk_hbm.at[pl.ds(core * KV_HERE, KV_HERE)], wk_ref, sems.at[3]
    )
    q_copy.start()
    wq_copy.start()
    wk_copy.start()
    for source, ref in ((core, k_own_ref), (1 - core, k_other_ref)):
        tile = ref[...]
        keys[pl.ds(pl.multiple_of(source * half, half), half), :] = tile
        for g, pooled in enumerate(pool_keys(tile)):
            pooled_key[g, pl.ds(pl.multiple_of(source * ROWS, ROWS), ROWS), :] = pooled

    def prepare(s, q_ref, at):
        for g in range(KV_HERE):
            for r in range(GROUP):
                head = g * GROUP + r
                tile = q_ref[pl.ds(at, BLOCK), head * HEAD_DIM:(head + 1) * HEAD_DIM]
                queries[s * KV_HERE + g, r * BLOCK:(r + 1) * BLOCK, :] = tile
                pooled_query[g, pl.ds(r * CHIP_BLOCKS + s, 1), :] = jnp.sum(
                    tile.astype(jnp.float32), axis=0, keepdims=True
                ) * (1.0 / BLOCK)

    for source in (1, 0):
        q_ref = (q_own_ref, q_other_ref)[source]
        if source == 0:
            q_copy.wait()

        @pl.loop(0, ROWS)
        def _(j):
            prepare(source * ROWS + j, q_ref, pl.multiple_of(j * BLOCK, BLOCK))

    slot_max[...] = jnp.full_like(slot_max, LOW)
    slot_sum[...] = jnp.zeros_like(slot_sum)
    note_copy.wait()
    filled, filled_far = make_lists(
        core, place_ref[1],
        (
            lambda j, c: counts_ref[j] if c == CAND else offsets_ref[j, c],
            lambda j, c: note_scalar[j, c],
        ),
        near_list, near_work, far_list, far_work,
    )
    far_filled[0] = filled_far
    slot_loop(
        filled, near_work, near_list,
        lambda s, row: position(core, s) + jnp.minimum(row, SPAN) - SPAN,
        keys, queries, slot_max, slot_sum, True,
    )
    wq_copy.wait()
    wk_copy.wait()
    for g in range(KV_HERE):
        gate_key[g] = dot_f32(pooled_key[g], wk_ref[g], ((1,), (0,)))
        for r in range(GROUP):
            picked = slice(r * CHIP_BLOCKS, (r + 1) * CHIP_BLOCKS)
            gate_query[g, picked, :] = dot_f32(
                pooled_query[g, picked, :], wq_ref[g * GROUP + r], ((1,), (0,))
            )


def far_kernel(
    core_ref, far_list, far_work, far_filled,
    k_prev_own_ref, k_prev_other_ref, k_far_ref, queries,
    max_ref, sum_ref, pooled_query, gate_query, near_key, near_gate_key, wk_ref,
    out_ref,
    keys, slot_max, slot_sum, pooled_key, shares, hits,
):
    core = core_ref[0]
    half = ROWS * BLOCK
    for place, ref in ((0, k_far_ref), (1 + core, k_prev_own_ref), (2 - core, k_prev_other_ref)):
        tile = ref[...]
        at = place * half if isinstance(place, int) else pl.multiple_of(place * half, half)
        row = place * ROWS if isinstance(place, int) else pl.multiple_of(place * ROWS, ROWS)
        keys[pl.ds(at, half), :] = tile
        for g, pooled in enumerate(pool_keys(tile)):
            pooled_key[g, pl.ds(row, ROWS), :] = pooled
    for g in range(KV_HERE):
        pooled_key[g, SPAN:SPAN + CHIP_BLOCKS, :] = near_key[g]
    slot_max[...] = max_ref[...]
    slot_sum[...] = sum_ref[...]
    shares[...] = jnp.zeros_like(shares)
    hits[...] = jnp.zeros_like(hits)
    slot_loop(
        far_filled[0], far_work, far_list,
        lambda s, row: jnp.where(row <= SPAN, position(core, s) + row, 0),
        keys, queries, slot_max, slot_sum, False,
    )

    live = lax.broadcasted_iota(jnp.int32, (SLOT_ROWS, WIDTH), 0) <= SPAN
    spread = jnp.where(
        lax.broadcasted_iota(jnp.int32, (WIDTH, LANES), 0) // BLOCK
        == lax.broadcasted_iota(jnp.int32, (WIDTH, LANES), 1) // CHIP_BLOCKS,
        1.0 / BLOCK, 0.0,
    ).astype(jnp.bfloat16)
    lane_block = lax.broadcasted_iota(jnp.int32, (SLOT_ROWS, LANES), 1) % CHIP_BLOCKS

    @pl.loop(0, CHIP_BLOCKS // 4)
    def _(step):
        found = []
        for e in range(4):
            s = step * 4 + e
            for g in range(KV_HERE):
                tops = jnp.where(live, slot_max[s * KV_HERE + g], LOW)
                top = jnp.max(tops, axis=0, keepdims=True)
                weight = jnp.where(
                    live, slot_sum[s * KV_HERE + g] * jnp.exp2((tops - top) * EXP_SCALE), 0.0
                )
                share = weight / jnp.sum(weight, axis=0, keepdims=True)
                coarse = share.astype(jnp.bfloat16)
                fine = (share - coarse.astype(jnp.float32)).astype(jnp.bfloat16)
                mean = (
                    jnp.dot(coarse, spread, preferred_element_type=jnp.float32)
                    + jnp.dot(fine, spread, preferred_element_type=jnp.float32)
                )
                found.append((shares.at[g], position(core, s), jnp.where(lane_block == s, mean, 0.0)))
                if g == 0:
                    filled = jnp.where(tops > 0.5 * LOW, 1.0, 0.0).astype(jnp.bfloat16)
                    hit = jnp.dot(filled, spread, preferred_element_type=jnp.float32)
                    found.append((hits, position(core, s), jnp.where(lane_block == s, hit, 0.0)))
        for table, block, mine in found:
            table[pl.ds(block, SLOT_ROWS), :] += mine

    scale = 1.0 / math.sqrt(HEAD_DIM)
    window = SPAN + CHIP_BLOCKS
    usable = hits[0:window, :] > 0.5
    divergence = jnp.zeros((1, LANES), jnp.float32)
    key_base = CHIP_BLOCKS + ROWS
    for g in range(KV_HERE):
        far_gate_key = dot_f32(pooled_key[g, 0:SPAN, :], wk_ref[g], ((1,), (0,)))
        gate_key = jnp.concatenate([far_gate_key, near_gate_key[g]], axis=0)
        logits = dot_f32(gate_key, gate_query[g], ((1,), (1,))) * scale
        logits = jnp.where(usable, logits, LOW)
        top = jnp.max(logits, axis=0, keepdims=True)
        weight = jnp.where(usable, jnp.exp(logits - top), 0.0)
        mass = jnp.sum(weight, axis=0, keepdims=True)
        log_gate = jnp.where(usable, logits - top - jnp.log(mass), 0.0)
        target = shares[g, 0:window, :]
        log_target = jnp.log(jnp.where(target > 0.0, target, 1.0))
        terms = jnp.where(usable, target * (log_target - log_gate), 0.0)
        divergence += jnp.sum(terms, axis=0, keepdims=True)
        target = jnp.where(usable, target, 0.0)
        slope = (weight / mass) * jnp.sum(target, axis=0, keepdims=True) - target
        slope = slope * (scale / 32.0)
        d_query = dot_f32(slope, gate_key, ((0,), (0,)))
        d_key = dot_f32(slope, gate_query[g], ((1,), (0,)))
        for r in range(GROUP):
            at = r * CHIP_BLOCKS
            pooled = pooled_query[g, at:at + CHIP_BLOCKS, :]
            for part in range(2):
                share = (g * GROUP + r) * 2 + part
                cols = slice(part * HALF_HEAD, (part + 1) * HALF_HEAD)
                out_ref[share, 0:CHIP_BLOCKS, :] = d_query[at:at + CHIP_BLOCKS, :]
                out_ref[share, CHIP_BLOCKS:key_base, :] = jnp.concatenate(
                    [pooled[0:ROWS, cols], pooled[ROWS:CHIP_BLOCKS, cols]], axis=1
                )
        key_part = dot_f32(pooled_key[g], d_key, ((0,), (0,)))
        for i in range(SHARES // KV_HERE):
            out_ref[g * (SHARES // KV_HERE) + i, key_base:key_base + KEY_ROWS, :] = (
                key_part[i * KEY_ROWS:(i + 1) * KEY_ROWS, :]
            )
    total = jnp.sum(divergence)
    for i in range(SHARES):
        out_ref[i, PART_ROWS - 8:PART_ROWS, :] = jnp.full((8, HEAD_DIM), total, jnp.float32)


def sum_kernel(parts_ref, out_ref):
    parts = parts_ref[...]
    pooled = parts[:, CHIP_BLOCKS:CHIP_BLOCKS + ROWS, :].reshape(SHARES * ROWS, HEAD_DIM)
    early = parts[:, 0:ROWS, :].reshape(SHARES * ROWS, HEAD_DIM)
    late = parts[:, ROWS:CHIP_BLOCKS, :].reshape(SHARES * ROWS, HEAD_DIM)
    out_ref[0:HALF_HEAD, :] = (
        dot_f32(pooled[:, :HALF_HEAD], early, ((0,), (0,)))
        + dot_f32(pooled[:, HALF_HEAD:], late, ((0,), (0,)))
    )
    out_ref[HALF_HEAD:, :] = jnp.sum(parts[:, CHIP_BLOCKS + ROWS:, :], axis=0)


def pack_kernel(own_ref, one_ref, two_ref, three_ref, out_ref, total_ref):
    got = (own_ref[...] + one_ref[...]) + (two_ref[...] + three_ref[...])
    total_ref[...] = got[SUM_ROWS:, :]
    coded = []
    powers = jnp.zeros((TILE, HEAD_DIM), jnp.float32)
    row = lax.broadcasted_iota(jnp.int32, (TILE, HEAD_DIM), 0)
    for tile in range(SUM_ROWS // TILE):
        value = got[tile * TILE:(tile + 1) * TILE, :]
        top = jnp.max(jnp.abs(value), axis=0, keepdims=True)
        power = jnp.clip(jnp.ceil(jnp.log2(jnp.maximum(top, 1e-35))), -110.0, 110.0)
        level = jnp.clip(jnp.round(value * jnp.exp2(-power) * LEVELS), -32767.0, 32767.0)
        coded.append(level.astype(jnp.int32).astype(jnp.int16))
        powers = jnp.where(row == tile, power, powers)
    coded.append(powers.astype(jnp.int32).astype(jnp.int16))
    coded = jnp.concatenate(coded, axis=0)
    for i in range(SHARES):
        out_ref[i] = coded


def unpack_kernel(place_ref, mine_ref, other_ref, query_ref, key_ref):
    core = place_ref[0]
    for source, ref in ((core, mine_ref), (1 - core, other_ref)):

        @pl.loop(0, SHARES)
        def _(share):
            coded = ref[share].astype(jnp.int32).astype(jnp.float32)
            scale = jnp.exp2(coded[SUM_ROWS:, :]) * (1.0 / LEVELS)
            for tile in range(SUM_ROWS // TILE):
                value = coded[tile * TILE:(tile + 1) * TILE, :] * scale[tile:tile + 1, :]
                if tile < HALF_HEAD // TILE:
                    at = source * (SHARES * HALF_HEAD) + share * HALF_HEAD + tile * TILE
                    query_ref[pl.ds(pl.multiple_of(at, TILE), TILE), :] = value
                else:
                    at = source * (SHARES * KEY_ROWS) + share * KEY_ROWS + tile * TILE - HALF_HEAD
                    key_ref[pl.ds(pl.multiple_of(at, TILE), TILE), :] = value


def pack(*parts):
    return pl.pallas_call(
        pack_kernel,
        out_shape=[
            shaped((SHARES, SUM_ROWS + TILE, HEAD_DIM), jnp.int16), shaped((8, HEAD_DIM)),
        ],
        name="pack",
    )(*parts)


def unpack(place, mine, other):
    rows = 2 * SHARES * HALF_HEAD, 2 * SHARES * KEY_ROWS
    return pl.pallas_call(
        unpack_kernel,
        grid_spec=pltpu.PrefetchScalarGridSpec(
            num_scalar_prefetch=1,
            grid=(1,),
            in_specs=[whole(*mine.shape)] * 2,
            out_specs=[whole(n, HEAD_DIM) for n in rows],
        ),
        out_shape=[shaped((n, HEAD_DIM)) for n in rows],
        name="unpack",
    )(place, mine, other)


def cut_keys_kernel(place_ref, mine_in, give_in, mine_ref, give_ref):
    mine_ref[...] = mine_in[...]
    give_ref[...] = give_in[...]


def cut_queries_kernel(place_ref, counts_ref, offsets_ref, give_in, after_ref, give_ref):
    half = ROWS * BLOCK
    give_ref[0:half, :] = give_in[...]
    row = lax.broadcasted_iota(jnp.int32, (ROWS, HEAD_DIM), 0)
    lane = lax.broadcasted_iota(jnp.int32, (ROWS, HEAD_DIM), 1)
    note = jnp.concatenate(
        [offsets_ref[...], jnp.zeros((ROWS, HEAD_DIM - CAND), jnp.int32)], axis=1
    )
    for j in range(ROWS):
        note = jnp.where((lane == CAND) & (row == j), counts_ref[j], note)
    note = note.astype(jnp.float32).astype(jnp.bfloat16)
    give_ref[half:, :] = jnp.zeros((NOTE_ROWS, Q_COLS), jnp.bfloat16)
    give_ref[half:, 0:HEAD_DIM] = jnp.concatenate([note, jnp.zeros_like(note)], axis=0)


def swap(x, axis):
    return lax.ppermute(x, axis, [(0, 1), (1, 0)])


def whole(*shape):
    return pl.BlockSpec(shape, lambda i, *_: (0,) * len(shape))


def shaped(shape, dtype=jnp.float32):
    return jax.ShapeDtypeStruct(shape, dtype)


def smem():
    return pl.BlockSpec(memory_space=pltpu.SMEM)


def cut_keys(place, keys):
    half = ROWS * BLOCK
    return pl.pallas_call(
        cut_keys_kernel,
        grid_spec=pltpu.PrefetchScalarGridSpec(
            num_scalar_prefetch=1,
            grid=(1,),
            in_specs=[
                pl.BlockSpec((half, K_COLS), lambda i, c: (0, c[0])),
                pl.BlockSpec((half, K_COLS), lambda i, c: (0, 1 - c[0])),
            ],
            out_specs=[whole(half, K_COLS)] * 2,
        ),
        out_shape=[shaped((half, K_COLS), jnp.bfloat16)] * 2,
        name="cut_keys",
    )(place, keys, keys)


def cut_queries(place, queries, offsets, counts, after):
    half = ROWS * BLOCK
    return pl.pallas_call(
        cut_queries_kernel,
        grid_spec=pltpu.PrefetchScalarGridSpec(
            num_scalar_prefetch=1,
            grid=(1,),
            in_specs=[
                smem(),
                whole(ROWS, CAND),
                pl.BlockSpec((half, Q_COLS), lambda i, c: (0, 1 - c[0])),
                pl.BlockSpec(memory_space=pl.ANY),
            ],
            out_specs=whole(half + NOTE_ROWS, Q_COLS),
        ),
        out_shape=shaped((half + NOTE_ROWS, Q_COLS), jnp.bfloat16),
        name="cut_queries",
    )(place, counts, offsets, queries, after)


def near_call(place, tables, q_own, q_other, k_mine, k_other, wq, wk):
    half = ROWS * BLOCK
    outs = [
        shaped((CHIP_BLOCKS * KV_HERE, WIDTH, HEAD_DIM), jnp.bfloat16),
        shaped((CHIP_BLOCKS * KV_HERE, SLOT_ROWS, WIDTH)),
        shaped((CHIP_BLOCKS * KV_HERE, SLOT_ROWS, WIDTH)),
        shaped((KV_HERE, LANES, HEAD_DIM)),
        shaped((KV_HERE, LANES, HEAD_DIM)),
        shaped((KV_HERE, CHIP_BLOCKS, POOL)),
        shaped((KV_HERE, CHIP_BLOCKS, HEAD_DIM)),
    ]
    lists = [LIST_SIZE, WORK_SIZE, 1]
    return pl.pallas_call(
        near_kernel,
        grid_spec=pltpu.PrefetchScalarGridSpec(
            num_scalar_prefetch=1,
            grid=(1,),
            in_specs=[smem()] * 2 + [
                pl.BlockSpec(memory_space=pltpu.HBM),
                whole(half + NOTE_ROWS, Q_COLS),
                whole(half, K_COLS),
                whole(half, K_COLS),
                pl.BlockSpec(memory_space=pltpu.HBM),
                pl.BlockSpec(memory_space=pltpu.HBM),
            ],
            out_specs=[whole(*o.shape) for o in outs] + [smem()] * 3,
            scratch_shapes=[
                pltpu.VMEM((CHIP_BLOCKS * BLOCK, K_COLS), jnp.bfloat16),
                pltpu.SMEM((LIST_SIZE,), jnp.int32),
                pltpu.SMEM((WORK_SIZE,), jnp.int32),
                pltpu.VMEM((NOTE_ROWS, HEAD_DIM), jnp.int32),
                pltpu.SMEM((NOTE_ROWS, HEAD_DIM), jnp.int32),
                pltpu.VMEM((half, Q_COLS), jnp.bfloat16),
                pltpu.VMEM((HEADS_HERE, HEAD_DIM, HEAD_DIM), jnp.float32),
                pltpu.VMEM((KV_HERE, POOL, HEAD_DIM), jnp.float32),
                pltpu.SemaphoreType.DMA((4,)),
            ],
        ),
        out_shape=outs + [shaped((n,), jnp.int32) for n in lists],
        compiler_params=pltpu.CompilerParams(vmem_limit_bytes=VMEM_BYTES),
        cost_estimate=pl.CostEstimate(
            flops=2_000_000_000, bytes_accessed=8_000_000, transcendentals=8_000_000
        ),
        name="near",
    )(place, *tables, q_own, q_other, k_mine, k_other, wq, wk)


def far_call(place, k_prev_own, k_prev_other, k_far, near, wk):
    args = (k_prev_own, k_prev_other, k_far, *near[:-3])
    return pl.pallas_call(
        far_kernel,
        grid_spec=pltpu.PrefetchScalarGridSpec(
            num_scalar_prefetch=1,
            grid=(1,),
            in_specs=[smem()] * 3 + [whole(*a.shape) for a in args] + [
                pl.BlockSpec((KV_HERE, POOL, HEAD_DIM), lambda i, c: (c[0], 0, 0)),
            ],
            out_specs=whole(SHARES, PART_ROWS, HEAD_DIM),
            scratch_shapes=[
                pltpu.VMEM((SPAN * BLOCK, K_COLS), jnp.bfloat16),
                pltpu.VMEM((CHIP_BLOCKS * KV_HERE, SLOT_ROWS, WIDTH), jnp.float32),
                pltpu.VMEM((CHIP_BLOCKS * KV_HERE, SLOT_ROWS, WIDTH), jnp.float32),
                pltpu.VMEM((KV_HERE, SPAN + CHIP_BLOCKS, POOL), jnp.float32),
                pltpu.VMEM((KV_HERE, PADDED, LANES), jnp.float32),
                pltpu.VMEM((PADDED, LANES), jnp.float32),
            ],
        ),
        out_shape=shaped((SHARES, PART_ROWS, HEAD_DIM)),
        compiler_params=pltpu.CompilerParams(vmem_limit_bytes=VMEM_BYTES),
        cost_estimate=pl.CostEstimate(
            flops=2_000_000_000, bytes_accessed=8_000_000, transcendentals=8_000_000
        ),
        name="far",
    )(place, *near[-3:], *args, wk)


def body(
    teacher_queries, teacher_keys, query_projection, key_projection, block_offsets, valid_counts
):
    chips = ("za", "zb", "yh", "x")
    places = chips + ("core",)
    count = lax.axis_size(places)
    core = lax.axis_index("core")
    place = jnp.stack([core, lax.axis_index(chips)]).astype(jnp.int32)

    k_mine, k_give = cut_keys(place, teacher_keys)
    k_prev_own = lax.ppermute(k_mine, places, [(i, i + 2) for i in range(count - 2)])
    k_prev_other = lax.ppermute(
        k_give, places, [(i, (i ^ 1) + 2) for i in range(count - 2)]
    )
    k_other = swap(k_give, "core")
    q_other = swap(cut_queries(place, teacher_queries, block_offsets, valid_counts, k_mine), "core")
    k_far = lax.ppermute(
        jnp.where(core == 1, k_mine, k_other), places, [(i, i + 4) for i in range(count - 4)]
    )
    near = near_call(
        place, (block_offsets, valid_counts), teacher_queries, q_other, k_mine, k_other, query_projection, key_projection
    )
    parts = far_call(place, k_prev_own, k_prev_other, k_far, near, key_projection)

    group = ("zb", "yh", "x")
    got = lax.all_to_all(parts, group, 0, 0)
    got = pl.pallas_call(sum_kernel, out_shape=shaped((SUM_ROWS + 8, HEAD_DIM)), name="sum")(got)
    one, two, three = (
        lax.ppermute(got, "za", [(i, i ^ step) for i in range(4)]) for step in (1, 2, 3)
    )
    coded, total = pack(got, one, two, three)
    total = total[:1]
    total = total + swap(total, "head")
    total = total + swap(total, "core")
    mine = lax.all_to_all(coded, group, 0, 0)
    query_gradient, key_gradient = unpack(place, mine, swap(mine, "core"))
    return (
        query_gradient.reshape(2 * HEADS_HERE, HEAD_DIM, HEAD_DIM),
        key_gradient.reshape(2 * KV_HERE, POOL, HEAD_DIM),
        total[0, 0] / (1024 * HEADS),
    )


def solution(mesh):
    split = Mesh(mesh.devices.reshape(4, 2, 2, 4, 2, 2), ("za", "zb", "yh", "x", "core", "head"))
    ctx = ("za", "zb", "yh", "x", "core")
    placed = (
        P(ctx, "head"),
        P(ctx, "head"),
        P("head", None, None),
        P("head", None, None),
        P(ctx, None),
        P(ctx),
    )
    return jax.shard_map(
        body,
        mesh=split,
        in_specs=placed,
        out_specs=(P("head", None, None), P("head", None, None), P()),
        check_vma=False,
    )
```

```python
import math

import jax
import jax.numpy as jnp
from jax import lax
from jax.experimental import pallas as pl
from jax.experimental.pallas import tpu as pltpu
from jax.sharding import Mesh, PartitionSpec as P

HEADS = 32
KV_HEADS = 8
HEAD_DIM = 128
BLOCK = 64
CAND = 24
REACH = 4

ROWS = 8
SPAN = 24
CHIP_BLOCKS = 2 * ROWS
PADDED = 48
KV_HERE = 2
GROUP = HEADS // KV_HEADS
HEADS_HERE = KV_HERE * GROUP
Q_COLS = HEADS_HERE * HEAD_DIM
K_COLS = KV_HERE * HEAD_DIM
POOL = 3 * HEAD_DIM
WIDTH = GROUP * BLOCK
DUMMY = 31
SLOT_ROWS = 32
LANES = GROUP * CHIP_BLOCKS
SHARES = 16
KEY_ROWS = KV_HERE * POOL // SHARES
HALF_HEAD = HEAD_DIM // 2
PART_ROWS = CHIP_BLOCKS + ROWS + KEY_ROWS + 8
SUM_ROWS = HALF_HEAD + KEY_ROWS
VMEM_BYTES = 40 * 1024 * 1024
NEAR_UNROLL = 4
FAR_UNROLL = 6
NOTE_ROWS = 16
TILE = 16
LEVELS = 32760.0
WORK_SIZE = CHIP_BLOCKS * CAND // 4 + 16
LOW = -1e30
EXP_SCALE = math.log2(math.e) / math.sqrt(HEAD_DIM)


def dot_f32(a, b, dims):
    def one(x, y):
        return lax.dot_general(x, y, (dims, ((), ())), preferred_element_type=jnp.float32)

    a_top = a.astype(jnp.bfloat16)
    b_top = b.astype(jnp.bfloat16)
    a_low = (a - a_top.astype(jnp.float32)).astype(jnp.bfloat16)
    b_low = (b - b_top.astype(jnp.float32)).astype(jnp.bfloat16)
    return one(a_top, b_top) + (one(a_top, b_low) + one(a_low, b_top))


def pool_keys(tile):
    wide = tile.astype(jnp.float32).reshape(ROWS, BLOCK, K_COLS)
    top = jnp.max(wide, axis=1)
    low = jnp.min(wide, axis=1)
    mean = jnp.sum(wide, axis=1) * (1.0 / BLOCK)
    return [
        jnp.concatenate(
            [v[:, g * HEAD_DIM:(g + 1) * HEAD_DIM] for v in (top, low, mean)], axis=1
        )
        for g in range(KV_HERE)
    ]


def make_lists(core, chip, table):
    shape = (CHIP_BLOCKS, HEAD_DIM)
    lane = lax.broadcasted_iota(jnp.int32, shape, 1)
    row = lax.broadcasted_iota(jnp.int32, shape, 0)
    block = position(core, row)
    offset = table.astype(jnp.int32)
    count = jnp.sum(jnp.where(lane == CAND, table, 0.0), axis=1, keepdims=True).astype(jnp.int32)
    usable = (lane < count) & (offset <= chip * CHIP_BLOCKS + block)
    near = jnp.where(usable & (offset <= block), 1.0, 0.0)
    far = jnp.where(usable & (offset > block), 1.0, 0.0)
    picked = jnp.concatenate([near, far], axis=0)
    before = jnp.where(
        lax.broadcasted_iota(jnp.int32, (HEAD_DIM, HEAD_DIM), 0)
        < lax.broadcasted_iota(jnp.int32, (HEAD_DIM, HEAD_DIM), 1), 1.0, 0.0,
    ).astype(jnp.bfloat16)
    rank = jnp.dot(picked.astype(jnp.bfloat16), before, preferred_element_type=jnp.float32)
    rank = jnp.where(picked > 0.0, rank, -1.0)
    value = (SPAN - DUMMY) - jnp.concatenate([table, table], axis=0)
    lane = jnp.concatenate([lane, lane], axis=0)
    packed = jnp.where(lane == CAND, jnp.sum(picked, axis=1, keepdims=True), float(DUMMY))
    for slot in range(CAND):
        here = jnp.sum(jnp.where(rank == slot, value, 0.0), axis=1, keepdims=True)
        packed = jnp.where(lane == slot, here + DUMMY, packed)
    return packed.astype(jnp.int32)


def make_work(list_ref, work, unroll):
    def per_block(s, total):
        count = list_ref[s, CAND]
        for i in range(CAND // 4):
            work[total] = s * CAND + i * 4
            total += jnp.where(i * 4 < count, 1, 0)
        return total

    filled = lax.fori_loop(0, CHIP_BLOCKS, per_block, jnp.int32(0))
    spare = work[jnp.maximum(filled - 1, 0)]
    for extra in range(unroll - 1):
        work[filled + extra] = spare
    return filled


def position(core, s):
    return jnp.where(s < ROWS, ROWS * core + s, ROWS * (1 - core) + s - ROWS)


def slot_loop(filled, work, unroll, list_ref, tile_start, keys, queries, slot_max, slot_sum, diagonal):
    lane = lax.broadcasted_iota(jnp.int32, (BLOCK, WIDTH), 1) % BLOCK
    key_row = lax.broadcasted_iota(jnp.int32, (BLOCK, WIDTH), 0)

    @pl.loop(0, (filled + unroll - 1) // unroll)
    def _(step):
        found = []
        for e in range(unroll):
            first = work[step * unroll + e]
            s = first // CAND
            rows = [list_ref[s, first - s * CAND + i] for i in range(4)]
            starts = [pl.multiple_of(tile_start(s, row) * BLOCK, BLOCK) for row in rows]
            if diagonal:
                keep = key_row <= lane + jnp.where(first == s * CAND, 0, BLOCK)
            for g in range(KV_HERE):
                tiles = [
                    keys[pl.ds(start, BLOCK), g * HEAD_DIM:(g + 1) * HEAD_DIM] for start in starts
                ]
                scores = lax.dot_general(
                    jnp.concatenate(tiles, axis=0), queries[s * KV_HERE + g],
                    (((1,), (1,)), ((), ())), preferred_element_type=jnp.float32,
                )
                for i, row in enumerate(rows):
                    part = scores[i * BLOCK:(i + 1) * BLOCK, :]
                    if diagonal and i == 0:
                        part = jnp.where(keep, part, LOW)
                    top = jnp.max(part, axis=0, keepdims=True)
                    total = jnp.sum(
                        jnp.exp2((part - top) * EXP_SCALE), axis=0, keepdims=True
                    )
                    found.append((s * KV_HERE + g, row, top, total))
        for index, row, top, total in found:
            slot_max[index, pl.ds(row, 1), :] = top
            slot_sum[index, pl.ds(row, 1), :] = total


def near_kernel(
    place_ref, offsets_ref, counts_ref,
    q_own_hbm, q_other_ref, k_own_ref, k_other_ref, wq_hbm, wk_hbm,
    queries, slot_max, slot_sum, pooled_query, gate_query, pooled_key, gate_key,
    far_list,
    keys, near_vector, near_list, near_work, q_own_ref, wq_ref, wk_ref, sems,
):
    core_ref = place_ref
    core = core_ref[0]
    half = ROWS * BLOCK
    q_copy = pltpu.make_async_copy(
        q_own_hbm.at[:, pl.ds(pl.multiple_of(core * Q_COLS, Q_COLS), Q_COLS)], q_own_ref, sems.at[1]
    )
    wq_copy = pltpu.make_async_copy(
        wq_hbm.at[pl.ds(core * HEADS_HERE, HEADS_HERE)], wq_ref, sems.at[2]
    )
    wk_copy = pltpu.make_async_copy(
        wk_hbm.at[pl.ds(core * KV_HERE, KV_HERE)], wk_ref, sems.at[3]
    )
    q_copy.start()
    wq_copy.start()
    wk_copy.start()
    table = jnp.concatenate(
        [offsets_ref[...], jnp.zeros((ROWS, HEAD_DIM - CAND), jnp.int32)], axis=1
    )
    row = lax.broadcasted_iota(jnp.int32, (ROWS, HEAD_DIM), 0)
    lane = lax.broadcasted_iota(jnp.int32, (ROWS, HEAD_DIM), 1)
    for j in range(ROWS):
        table = jnp.where((lane == CAND) & (row == j), counts_ref[j], table)
    note = q_other_ref[half:, 0:HEAD_DIM].astype(jnp.float32)
    lists = make_lists(
        core, place_ref[1], jnp.concatenate([table.astype(jnp.float32), note[0:ROWS]], axis=0)
    )
    far_list[...] = lists[CHIP_BLOCKS:]
    near_vector[...] = lists[0:CHIP_BLOCKS]
    list_copy = pltpu.make_async_copy(near_vector, near_list, sems.at[0])
    list_copy.start()
    for source, ref in ((core, k_own_ref), (1 - core, k_other_ref)):
        tile = ref[...]
        keys[pl.ds(pl.multiple_of(source * half, half), half), :] = tile
        for g, pooled in enumerate(pool_keys(tile)):
            pooled_key[g, pl.ds(pl.multiple_of(source * ROWS, ROWS), ROWS), :] = pooled

    def prepare(s, q_ref, at):
        for g in range(KV_HERE):
            for r in range(GROUP):
                head = g * GROUP + r
                tile = q_ref[pl.ds(at, BLOCK), head * HEAD_DIM:(head + 1) * HEAD_DIM]
                queries[s * KV_HERE + g, r * BLOCK:(r + 1) * BLOCK, :] = tile
                pooled_query[g, pl.ds(r * CHIP_BLOCKS + s, 1), :] = jnp.sum(
                    tile.astype(jnp.float32), axis=0, keepdims=True
                ) * (1.0 / BLOCK)

    for source in (1, 0):
        q_ref = (q_own_ref, q_other_ref)[source]
        if source == 0:
            q_copy.wait()

        @pl.loop(0, ROWS)
        def _(j):
            prepare(source * ROWS + j, q_ref, pl.multiple_of(j * BLOCK, BLOCK))

    slot_max[...] = jnp.full_like(slot_max, LOW)
    slot_sum[...] = jnp.zeros_like(slot_sum)
    list_copy.wait()
    filled = make_work(near_list, near_work, NEAR_UNROLL)
    slot_loop(
        filled, near_work, NEAR_UNROLL, near_list,
        lambda s, row: position(core, s) + jnp.minimum(row, SPAN) - SPAN,
        keys, queries, slot_max, slot_sum, True,
    )
    wq_copy.wait()
    wk_copy.wait()
    for g in range(KV_HERE):
        gate_key[g] = dot_f32(pooled_key[g], wk_ref[g], ((1,), (0,)))
        for r in range(GROUP):
            picked = slice(r * CHIP_BLOCKS, (r + 1) * CHIP_BLOCKS)
            gate_query[g, picked, :] = dot_f32(
                pooled_query[g, picked, :], wq_ref[g * GROUP + r], ((1,), (0,))
            )


def far_kernel(
    core_ref, far_list,
    k_prev_own_ref, k_prev_other_ref, k_far_ref, queries,
    max_ref, sum_ref, pooled_query, gate_query, near_key, near_gate_key, wk_ref,
    out_ref,
    keys, slot_max, slot_sum, pooled_key, shares, hits, far_work,
):
    core = core_ref[0]
    half = ROWS * BLOCK
    for place, ref in ((0, k_far_ref), (1 + core, k_prev_own_ref), (2 - core, k_prev_other_ref)):
        tile = ref[...]
        at = place * half if isinstance(place, int) else pl.multiple_of(place * half, half)
        row = place * ROWS if isinstance(place, int) else pl.multiple_of(place * ROWS, ROWS)
        keys[pl.ds(at, half), :] = tile
        for g, pooled in enumerate(pool_keys(tile)):
            pooled_key[g, pl.ds(row, ROWS), :] = pooled
    for g in range(KV_HERE):
        pooled_key[g, SPAN:SPAN + CHIP_BLOCKS, :] = near_key[g]
    slot_max[...] = max_ref[...]
    slot_sum[...] = sum_ref[...]
    shares[...] = jnp.zeros_like(shares)
    hits[...] = jnp.zeros_like(hits)
    filled = make_work(far_list, far_work, FAR_UNROLL)
    slot_loop(
        filled, far_work, FAR_UNROLL, far_list,
        lambda s, row: jnp.where(row <= SPAN, position(core, s) + row, 0),
        keys, queries, slot_max, slot_sum, False,
    )

    live = lax.broadcasted_iota(jnp.int32, (SLOT_ROWS, WIDTH), 0) <= SPAN
    spread = jnp.where(
        lax.broadcasted_iota(jnp.int32, (WIDTH, LANES), 0) // BLOCK
        == lax.broadcasted_iota(jnp.int32, (WIDTH, LANES), 1) // CHIP_BLOCKS,
        1.0 / BLOCK, 0.0,
    ).astype(jnp.bfloat16)
    lane_block = lax.broadcasted_iota(jnp.int32, (SLOT_ROWS, LANES), 1) % CHIP_BLOCKS

    @pl.loop(0, CHIP_BLOCKS // 4)
    def _(step):
        found = []
        for e in range(4):
            s = step * 4 + e
            for g in range(KV_HERE):
                tops = jnp.where(live, slot_max[s * KV_HERE + g], LOW)
                top = jnp.max(tops, axis=0, keepdims=True)
                weight = jnp.where(
                    live, slot_sum[s * KV_HERE + g] * jnp.exp2((tops - top) * EXP_SCALE), 0.0
                )
                share = weight / jnp.sum(weight, axis=0, keepdims=True)
                coarse = share.astype(jnp.bfloat16)
                fine = (share - coarse.astype(jnp.float32)).astype(jnp.bfloat16)
                mean = (
                    jnp.dot(coarse, spread, preferred_element_type=jnp.float32)
                    + jnp.dot(fine, spread, preferred_element_type=jnp.float32)
                )
                found.append((shares.at[g], position(core, s), jnp.where(lane_block == s, mean, 0.0)))
                if g == 0:
                    filled = jnp.where(tops > 0.5 * LOW, 1.0, 0.0).astype(jnp.bfloat16)
                    hit = jnp.dot(filled, spread, preferred_element_type=jnp.float32)
                    found.append((hits, position(core, s), jnp.where(lane_block == s, hit, 0.0)))
        for table, block, mine in found:
            table[pl.ds(block, SLOT_ROWS), :] += mine

    scale = 1.0 / math.sqrt(HEAD_DIM)
    window = SPAN + CHIP_BLOCKS
    usable = hits[0:window, :] > 0.5
    divergence = jnp.zeros((1, LANES), jnp.float32)
    key_base = CHIP_BLOCKS + ROWS
    for g in range(KV_HERE):
        far_gate_key = dot_f32(pooled_key[g, 0:SPAN, :], wk_ref[g], ((1,), (0,)))
        gate_key = jnp.concatenate([far_gate_key, near_gate_key[g]], axis=0)
        logits = dot_f32(gate_key, gate_query[g], ((1,), (1,))) * scale
        logits = jnp.where(usable, logits, LOW)
        top = jnp.max(logits, axis=0, keepdims=True)
        weight = jnp.where(usable, jnp.exp(logits - top), 0.0)
        mass = jnp.sum(weight, axis=0, keepdims=True)
        log_gate = jnp.where(usable, logits - top - jnp.log(mass), 0.0)
        target = shares[g, 0:window, :]
        log_target = jnp.log(jnp.where(target > 0.0, target, 1.0))
        terms = jnp.where(usable, target * (log_target - log_gate), 0.0)
        divergence += jnp.sum(terms, axis=0, keepdims=True)
        target = jnp.where(usable, target, 0.0)
        slope = (weight / mass) * jnp.sum(target, axis=0, keepdims=True) - target
        slope = slope * (scale / 32.0)
        d_query = dot_f32(slope, gate_key, ((0,), (0,)))
        d_key = dot_f32(slope, gate_query[g], ((1,), (0,)))
        for r in range(GROUP):
            at = r * CHIP_BLOCKS
            pooled = pooled_query[g, at:at + CHIP_BLOCKS, :]
            for part in range(2):
                share = (g * GROUP + r) * 2 + part
                cols = slice(part * HALF_HEAD, (part + 1) * HALF_HEAD)
                out_ref[share, 0:CHIP_BLOCKS, :] = d_query[at:at + CHIP_BLOCKS, :]
                out_ref[share, CHIP_BLOCKS:key_base, :] = jnp.concatenate(
                    [pooled[0:ROWS, cols], pooled[ROWS:CHIP_BLOCKS, cols]], axis=1
                )
        key_part = dot_f32(pooled_key[g], d_key, ((0,), (0,)))
        for i in range(SHARES // KV_HERE):
            out_ref[g * (SHARES // KV_HERE) + i, key_base:key_base + KEY_ROWS, :] = (
                key_part[i * KEY_ROWS:(i + 1) * KEY_ROWS, :]
            )
    total = jnp.sum(divergence)
    for i in range(SHARES):
        out_ref[i, PART_ROWS - 8:PART_ROWS, :] = jnp.full((8, HEAD_DIM), total, jnp.float32)


def sum_kernel(parts_ref, out_ref):
    parts = parts_ref[...]
    pooled = parts[:, CHIP_BLOCKS:CHIP_BLOCKS + ROWS, :].reshape(SHARES * ROWS, HEAD_DIM)
    early = parts[:, 0:ROWS, :].reshape(SHARES * ROWS, HEAD_DIM)
    late = parts[:, ROWS:CHIP_BLOCKS, :].reshape(SHARES * ROWS, HEAD_DIM)
    out_ref[0:HALF_HEAD, :] = (
        dot_f32(pooled[:, :HALF_HEAD], early, ((0,), (0,)))
        + dot_f32(pooled[:, HALF_HEAD:], late, ((0,), (0,)))
    )
    out_ref[HALF_HEAD:, :] = jnp.sum(parts[:, CHIP_BLOCKS + ROWS:, :], axis=0)


def pack_kernel(own_ref, one_ref, two_ref, three_ref, out_ref, total_ref):
    got = (own_ref[...] + one_ref[...]) + (two_ref[...] + three_ref[...])
    total_ref[...] = got[SUM_ROWS:, :]
    coded = []
    powers = jnp.zeros((TILE, HEAD_DIM), jnp.float32)
    row = lax.broadcasted_iota(jnp.int32, (TILE, HEAD_DIM), 0)
    for tile in range(SUM_ROWS // TILE):
        value = got[tile * TILE:(tile + 1) * TILE, :]
        top = jnp.max(jnp.abs(value), axis=0, keepdims=True)
        power = jnp.clip(jnp.ceil(jnp.log2(jnp.maximum(top, 1e-35))), -110.0, 110.0)
        level = jnp.clip(jnp.round(value * jnp.exp2(-power) * LEVELS), -32767.0, 32767.0)
        coded.append(level.astype(jnp.int32).astype(jnp.int16))
        powers = jnp.where(row == tile, power, powers)
    coded.append(powers.astype(jnp.int32).astype(jnp.int16))
    coded = jnp.concatenate(coded, axis=0)
    for i in range(SHARES):
        out_ref[i] = coded


def unpack_kernel(place_ref, mine_ref, other_ref, query_ref, key_ref):
    core = place_ref[0]
    for source, ref in ((core, mine_ref), (1 - core, other_ref)):
        for share in range(SHARES):
            powers = ref[share, SUM_ROWS:SUM_ROWS + TILE, :].astype(jnp.int32).astype(jnp.float32)
            scale = jnp.exp2(powers[0:8, :]) * (1.0 / LEVELS)
            for tile in range(SUM_ROWS // TILE):
                coded = ref[share, tile * TILE:(tile + 1) * TILE, :]
                value = coded.astype(jnp.int32).astype(jnp.float32) * scale[tile:tile + 1, :]
                if tile < HALF_HEAD // TILE:
                    query_ref[source, pl.ds(share * HALF_HEAD + tile * TILE, TILE), :] = value
                else:
                    at = share * KEY_ROWS + tile * TILE - HALF_HEAD
                    key_ref[source, pl.ds(at, TILE), :] = value


def pack(*parts):
    return pl.pallas_call(
        pack_kernel,
        out_shape=[
            shaped((SHARES, SUM_ROWS + TILE, HEAD_DIM), jnp.int16), shaped((8, HEAD_DIM)),
        ],
        name="pack",
    )(*parts)


def unpack(place, mine, other):
    rows = SHARES * HALF_HEAD, SHARES * KEY_ROWS
    return pl.pallas_call(
        unpack_kernel,
        grid_spec=pltpu.PrefetchScalarGridSpec(
            num_scalar_prefetch=1,
            grid=(1,),
            in_specs=[whole(*mine.shape)] * 2,
            out_specs=[whole(2, n, HEAD_DIM) for n in rows],
        ),
        out_shape=[shaped((2, n, HEAD_DIM)) for n in rows],
        name="unpack",
    )(place, mine, other)


def cut_queries_kernel(place_ref, counts_ref, offsets_ref, give_in, after_ref, give_ref):
    half = ROWS * BLOCK
    give_ref[0:half, :] = give_in[...]
    row = lax.broadcasted_iota(jnp.int32, (ROWS, HEAD_DIM), 0)
    lane = lax.broadcasted_iota(jnp.int32, (ROWS, HEAD_DIM), 1)
    note = jnp.concatenate(
        [offsets_ref[...], jnp.zeros((ROWS, HEAD_DIM - CAND), jnp.int32)], axis=1
    )
    for j in range(ROWS):
        note = jnp.where((lane == CAND) & (row == j), counts_ref[j], note)
    note = note.astype(jnp.float32).astype(jnp.bfloat16)
    give_ref[half:, :] = jnp.zeros((NOTE_ROWS, Q_COLS), jnp.bfloat16)
    give_ref[half:, 0:HEAD_DIM] = jnp.concatenate([note, jnp.zeros_like(note)], axis=0)


def swap(x, axis):
    return lax.ppermute(x, axis, [(0, 1), (1, 0)])


def whole(*shape):
    return pl.BlockSpec(shape, lambda i, *_: (0,) * len(shape))


def shaped(shape, dtype=jnp.float32):
    return jax.ShapeDtypeStruct(shape, dtype)


def smem():
    return pl.BlockSpec(memory_space=pltpu.SMEM)


def cut_queries(place, queries, offsets, counts, after):
    half = ROWS * BLOCK
    return pl.pallas_call(
        cut_queries_kernel,
        grid_spec=pltpu.PrefetchScalarGridSpec(
            num_scalar_prefetch=1,
            grid=(1,),
            in_specs=[
                smem(),
                whole(ROWS, CAND),
                pl.BlockSpec((half, Q_COLS), lambda i, c: (0, 1 - c[0])),
                pl.BlockSpec(memory_space=pl.ANY),
            ],
            out_specs=whole(half + NOTE_ROWS, Q_COLS),
        ),
        out_shape=shaped((half + NOTE_ROWS, Q_COLS), jnp.bfloat16),
        cost_estimate=pl.CostEstimate(
            flops=0, bytes_accessed=30_000_000, transcendentals=0
        ),
        name="cut_queries",
    )(place, counts, offsets, queries, after)


def near_call(place, tables, q_own, q_other, k_mine, k_other, wq, wk):
    half = ROWS * BLOCK
    outs = [
        shaped((CHIP_BLOCKS * KV_HERE, WIDTH, HEAD_DIM), jnp.bfloat16),
        shaped((CHIP_BLOCKS * KV_HERE, SLOT_ROWS, WIDTH)),
        shaped((CHIP_BLOCKS * KV_HERE, SLOT_ROWS, WIDTH)),
        shaped((KV_HERE, LANES, HEAD_DIM)),
        shaped((KV_HERE, LANES, HEAD_DIM)),
        shaped((KV_HERE, CHIP_BLOCKS, POOL)),
        shaped((KV_HERE, CHIP_BLOCKS, HEAD_DIM)),
        shaped((CHIP_BLOCKS, HEAD_DIM), jnp.int32),
    ]
    return pl.pallas_call(
        near_kernel,
        grid_spec=pltpu.PrefetchScalarGridSpec(
            num_scalar_prefetch=1,
            grid=(1,),
            in_specs=[whole(ROWS, CAND), smem()] + [
                pl.BlockSpec(memory_space=pltpu.HBM),
                whole(half + NOTE_ROWS, Q_COLS),
                whole(half, K_COLS),
                whole(half, K_COLS),
                pl.BlockSpec(memory_space=pltpu.HBM),
                pl.BlockSpec(memory_space=pltpu.HBM),
            ],
            out_specs=[whole(*o.shape) for o in outs],
            scratch_shapes=[
                pltpu.VMEM((CHIP_BLOCKS * BLOCK, K_COLS), jnp.bfloat16),
                pltpu.VMEM((CHIP_BLOCKS, HEAD_DIM), jnp.int32),
                pltpu.SMEM((CHIP_BLOCKS, HEAD_DIM), jnp.int32),
                pltpu.SMEM((WORK_SIZE,), jnp.int32),
                pltpu.VMEM((half, Q_COLS), jnp.bfloat16),
                pltpu.VMEM((HEADS_HERE, HEAD_DIM, HEAD_DIM), jnp.float32),
                pltpu.VMEM((KV_HERE, POOL, HEAD_DIM), jnp.float32),
                pltpu.SemaphoreType.DMA((4,)),
            ],
        ),
        out_shape=outs,
        compiler_params=pltpu.CompilerParams(vmem_limit_bytes=VMEM_BYTES),
        cost_estimate=pl.CostEstimate(
            flops=2_000_000_000, bytes_accessed=8_000_000, transcendentals=8_000_000
        ),
        name="near",
    )(place, *tables, q_own, q_other, k_mine, k_other, wq, wk)


def far_call(place, k_prev_own, k_prev_other, k_far, near, wk):
    args = (k_prev_own, k_prev_other, k_far, *near[:-1])
    return pl.pallas_call(
        far_kernel,
        grid_spec=pltpu.PrefetchScalarGridSpec(
            num_scalar_prefetch=1,
            grid=(1,),
            in_specs=[smem()] + [whole(*a.shape) for a in args] + [
                pl.BlockSpec((KV_HERE, POOL, HEAD_DIM), lambda i, c: (c[0], 0, 0)),
            ],
            out_specs=whole(SHARES, PART_ROWS, HEAD_DIM),
            scratch_shapes=[
                pltpu.VMEM((SPAN * BLOCK, K_COLS), jnp.bfloat16),
                pltpu.VMEM((CHIP_BLOCKS * KV_HERE, SLOT_ROWS, WIDTH), jnp.float32),
                pltpu.VMEM((CHIP_BLOCKS * KV_HERE, SLOT_ROWS, WIDTH), jnp.float32),
                pltpu.VMEM((KV_HERE, SPAN + CHIP_BLOCKS, POOL), jnp.float32),
                pltpu.VMEM((KV_HERE, PADDED, LANES), jnp.float32),
                pltpu.VMEM((PADDED, LANES), jnp.float32),
                pltpu.SMEM((WORK_SIZE,), jnp.int32),
            ],
        ),
        out_shape=shaped((SHARES, PART_ROWS, HEAD_DIM)),
        compiler_params=pltpu.CompilerParams(vmem_limit_bytes=VMEM_BYTES),
        cost_estimate=pl.CostEstimate(
            flops=2_000_000_000, bytes_accessed=8_000_000, transcendentals=8_000_000
        ),
        name="far",
    )(place, near[-1], *args, wk)


def body(
    teacher_queries, teacher_keys, query_projection, key_projection, block_offsets, valid_counts
):
    chips = ("za", "zb", "yh", "x")
    places = chips + ("core",)
    count = lax.axis_size(places)
    core = lax.axis_index("core")
    place = jnp.stack([core, lax.axis_index(chips)]).astype(jnp.int32)

    k_mine = lax.dynamic_slice_in_dim(teacher_keys, core * K_COLS, K_COLS, 1)
    k_give = lax.dynamic_slice_in_dim(teacher_keys, (1 - core) * K_COLS, K_COLS, 1)
    k_prev_own = lax.ppermute(k_mine, places, [(i, i + 2) for i in range(count - 2)])
    k_prev_other = lax.ppermute(
        k_give, places, [(i, (i ^ 1) + 2) for i in range(count - 2)]
    )
    k_other = swap(k_give, "core")
    q_other = swap(cut_queries(place, teacher_queries, block_offsets, valid_counts, k_mine), "core")
    k_far = lax.ppermute(
        jnp.where(core == 1, k_mine, k_other), places, [(i, i + 4) for i in range(count - 4)]
    )
    near = near_call(
        place, (block_offsets, valid_counts), teacher_queries, q_other, k_mine, k_other, query_projection, key_projection
    )
    parts = far_call(place, k_prev_own, k_prev_other, k_far, near, key_projection)

    group = ("zb", "yh", "x")
    got = lax.all_to_all(parts, group, 0, 0)
    got = pl.pallas_call(sum_kernel, out_shape=shaped((SUM_ROWS + 8, HEAD_DIM)), name="sum")(got)
    one, two, three = (
        lax.ppermute(got, "za", [(i, i ^ step) for i in range(4)]) for step in (1, 2, 3)
    )
    coded, total = pack(got, one, two, three)
    total = total[:1]
    total = total + swap(total, "head")
    total = total + swap(total, "core")
    mine = lax.all_to_all(coded, group, 0, 0)
    query_gradient, key_gradient = unpack(place, mine, swap(mine, "core"))
    return (
        query_gradient.reshape(2 * HEADS_HERE, HEAD_DIM, HEAD_DIM),
        key_gradient.reshape(2 * KV_HERE, POOL, HEAD_DIM),
        total[0, 0] / (1024 * HEADS),
    )


def solution(mesh):
    split = Mesh(mesh.devices.reshape(4, 2, 2, 4, 2, 2), ("za", "zb", "yh", "x", "core", "head"))
    ctx = ("za", "zb", "yh", "x", "core")
    placed = (
        P(ctx, "head"),
        P(ctx, "head"),
        P("head", None, None),
        P("head", None, None),
        P(ctx, None),
        P(ctx),
    )
    return jax.shard_map(
        body,
        mesh=split,
        in_specs=placed,
        out_specs=(P("head", None, None), P("head", None, None), P()),
        check_vma=False,
    )
```

```python
import math

import jax
import jax.numpy as jnp
from jax import lax
from jax.experimental import pallas as pl
from jax.experimental.pallas import tpu as pltpu
from jax.sharding import Mesh, PartitionSpec as P

HEADS = 32
KV_HEADS = 8
HEAD_DIM = 128
BLOCK = 64
CAND = 24
REACH = 4

ROWS = 8
SPAN = 24
CHIP_BLOCKS = 2 * ROWS
PADDED = 48
KV_HERE = 2
GROUP = HEADS // KV_HEADS
HEADS_HERE = KV_HERE * GROUP
Q_COLS = HEADS_HERE * HEAD_DIM
K_COLS = KV_HERE * HEAD_DIM
POOL = 3 * HEAD_DIM
WIDTH = GROUP * BLOCK
DUMMY = 31
SLOT_ROWS = 32
LANES = GROUP * CHIP_BLOCKS
SHARES = 16
KEY_ROWS = KV_HERE * POOL // SHARES
HALF_HEAD = HEAD_DIM // 2
PART_ROWS = CHIP_BLOCKS + ROWS + KEY_ROWS + 8
SUM_ROWS = HALF_HEAD + KEY_ROWS
VMEM_BYTES = 40 * 1024 * 1024
NEAR_UNROLL = 4
FAR_UNROLL = 6
TILE = 16
STEP_SHARES = 4
LEVELS = 32760.0
WORK_SIZE = CHIP_BLOCKS * CAND // 4 + 16
LOW = -1e30
EXP_SCALE = math.log2(math.e) / math.sqrt(HEAD_DIM)


def dot_f32(a, b, dims):
    def one(x, y):
        return lax.dot_general(x, y, (dims, ((), ())), preferred_element_type=jnp.float32)

    a_top = a.astype(jnp.bfloat16)
    b_top = b.astype(jnp.bfloat16)
    a_low = (a - a_top.astype(jnp.float32)).astype(jnp.bfloat16)
    b_low = (b - b_top.astype(jnp.float32)).astype(jnp.bfloat16)
    return one(a_top, b_top) + (one(a_top, b_low) + one(a_low, b_top))


def pool_keys(tile):
    wide = tile.astype(jnp.float32).reshape(ROWS, BLOCK, K_COLS)
    top = jnp.max(wide, axis=1)
    low = jnp.min(wide, axis=1)
    mean = jnp.sum(wide, axis=1) * (1.0 / BLOCK)
    return [
        jnp.concatenate(
            [v[:, g * HEAD_DIM:(g + 1) * HEAD_DIM] for v in (top, low, mean)], axis=1
        )
        for g in range(KV_HERE)
    ]


def slot_table(offsets_ref, counts_ref):
    table = jnp.concatenate(
        [offsets_ref[...], jnp.zeros((ROWS, HEAD_DIM - CAND), jnp.int32)], axis=1
    )
    row = lax.broadcasted_iota(jnp.int32, (ROWS, HEAD_DIM), 0)
    lane = lax.broadcasted_iota(jnp.int32, (ROWS, HEAD_DIM), 1)
    for j in range(ROWS):
        table = jnp.where((lane == CAND) & (row == j), counts_ref[j], table)
    return table.astype(jnp.float32)


def make_lists(core, chip, table):
    shape = (CHIP_BLOCKS, HEAD_DIM)
    lane = lax.broadcasted_iota(jnp.int32, shape, 1)
    row = lax.broadcasted_iota(jnp.int32, shape, 0)
    block = position(core, row)
    offset = table.astype(jnp.int32)
    count = jnp.sum(jnp.where(lane == CAND, table, 0.0), axis=1, keepdims=True).astype(jnp.int32)
    usable = (lane < count) & (offset <= chip * CHIP_BLOCKS + block)
    near = jnp.where(usable & (offset <= block), 1.0, 0.0)
    far = jnp.where(usable & (offset > block), 1.0, 0.0)
    picked = jnp.concatenate([near, far], axis=0)
    before = jnp.where(
        lax.broadcasted_iota(jnp.int32, (HEAD_DIM, HEAD_DIM), 0)
        < lax.broadcasted_iota(jnp.int32, (HEAD_DIM, HEAD_DIM), 1), 1.0, 0.0,
    ).astype(jnp.bfloat16)
    rank = jnp.dot(picked.astype(jnp.bfloat16), before, preferred_element_type=jnp.float32)
    rank = jnp.where(picked > 0.0, rank, -1.0)
    value = (SPAN - DUMMY) - jnp.concatenate([table, table], axis=0)
    lane = jnp.concatenate([lane, lane], axis=0)
    packed = jnp.where(lane == CAND, jnp.sum(picked, axis=1, keepdims=True), float(DUMMY))
    for slot in range(CAND):
        here = jnp.sum(jnp.where(rank == slot, value, 0.0), axis=1, keepdims=True)
        packed = jnp.where(lane == slot, here + DUMMY, packed)
    return packed.astype(jnp.int32)


def make_work(list_ref, work, unroll):
    def per_block(s, total):
        count = list_ref[s, CAND]
        for i in range(CAND // 4):
            work[total] = s * CAND + i * 4
            total += jnp.where(i * 4 < count, 1, 0)
        return total

    filled = lax.fori_loop(0, CHIP_BLOCKS, per_block, jnp.int32(0))
    spare = work[jnp.maximum(filled - 1, 0)]
    for extra in range(unroll - 1):
        work[filled + extra] = spare
    return filled


def position(core, s):
    return jnp.where(s < ROWS, ROWS * core + s, ROWS * (1 - core) + s - ROWS)


def slot_loop(filled, work, unroll, list_ref, tile_start, keys, queries, slot_max, slot_sum, diagonal):
    lane = lax.broadcasted_iota(jnp.int32, (BLOCK, WIDTH), 1) % BLOCK
    key_row = lax.broadcasted_iota(jnp.int32, (BLOCK, WIDTH), 0)

    @pl.loop(0, (filled + unroll - 1) // unroll)
    def _(step):
        found = []
        for e in range(unroll):
            first = work[step * unroll + e]
            s = first // CAND
            rows = [list_ref[s, first - s * CAND + i] for i in range(4)]
            starts = [pl.multiple_of(tile_start(s, row) * BLOCK, BLOCK) for row in rows]
            if diagonal:
                keep = key_row <= lane + jnp.where(first == s * CAND, 0, BLOCK)
            for g in range(KV_HERE):
                tiles = [
                    keys[pl.ds(start, BLOCK), g * HEAD_DIM:(g + 1) * HEAD_DIM] for start in starts
                ]
                scores = lax.dot_general(
                    jnp.concatenate(tiles, axis=0), queries[s * KV_HERE + g],
                    (((1,), (1,)), ((), ())), preferred_element_type=jnp.float32,
                )
                for i, row in enumerate(rows):
                    part = scores[i * BLOCK:(i + 1) * BLOCK, :]
                    if diagonal and i == 0:
                        part = jnp.where(keep, part, LOW)
                    top = jnp.max(part, axis=0, keepdims=True)
                    total = jnp.sum(
                        jnp.exp2((part - top) * EXP_SCALE), axis=0, keepdims=True
                    )
                    found.append((s * KV_HERE + g, row, top, total))
        for index, row, top, total in found:
            slot_max[index, pl.ds(row, 1), :] = top
            slot_sum[index, pl.ds(row, 1), :] = total


def near_kernel(
    place_ref, offsets_own_ref, counts_own_ref, offsets_other_ref, counts_other_ref,
    q_own_hbm, q_other_ref, k_own_ref, k_other_ref, wq_hbm, wk_hbm,
    queries, slot_max, slot_sum, pooled_query, gate_query, pooled_key, gate_key,
    far_list,
    keys, near_vector, near_list, near_work, q_own_ref, wq_ref, wk_ref, sems,
):
    core_ref = place_ref
    core = core_ref[0]
    half = ROWS * BLOCK
    q_copy = pltpu.make_async_copy(
        q_own_hbm.at[:, pl.ds(pl.multiple_of(core * Q_COLS, Q_COLS), Q_COLS)], q_own_ref, sems.at[1]
    )
    wq_copy = pltpu.make_async_copy(
        wq_hbm.at[pl.ds(core * HEADS_HERE, HEADS_HERE)], wq_ref, sems.at[2]
    )
    wk_copy = pltpu.make_async_copy(
        wk_hbm.at[pl.ds(core * KV_HERE, KV_HERE)], wk_ref, sems.at[3]
    )
    q_copy.start()
    wq_copy.start()
    wk_copy.start()
    lists = make_lists(
        core, place_ref[1],
        jnp.concatenate(
            [
                slot_table(offsets_own_ref, counts_own_ref),
                slot_table(offsets_other_ref, counts_other_ref),
            ],
            axis=0,
        ),
    )
    far_list[...] = lists[CHIP_BLOCKS:]
    near_vector[...] = lists[0:CHIP_BLOCKS]
    list_copy = pltpu.make_async_copy(near_vector, near_list, sems.at[0])
    list_copy.start()
    for source, ref in ((core, k_own_ref), (1 - core, k_other_ref)):
        tile = ref[...]
        keys[pl.ds(pl.multiple_of(source * half, half), half), :] = tile
        for g, pooled in enumerate(pool_keys(tile)):
            pooled_key[g, pl.ds(pl.multiple_of(source * ROWS, ROWS), ROWS), :] = pooled

    def prepare(s, q_ref, at):
        for g in range(KV_HERE):
            for r in range(GROUP):
                head = g * GROUP + r
                tile = q_ref[pl.ds(at, BLOCK), head * HEAD_DIM:(head + 1) * HEAD_DIM]
                queries[s * KV_HERE + g, r * BLOCK:(r + 1) * BLOCK, :] = tile
                pooled_query[g, pl.ds(r * CHIP_BLOCKS + s, 1), :] = jnp.sum(
                    tile.astype(jnp.float32), axis=0, keepdims=True
                ) * (1.0 / BLOCK)

    for source in (1, 0):
        q_ref = (q_own_ref, q_other_ref)[source]
        if source == 0:
            q_copy.wait()

        @pl.loop(0, ROWS)
        def _(j):
            prepare(source * ROWS + j, q_ref, pl.multiple_of(j * BLOCK, BLOCK))

    slot_max[...] = jnp.full_like(slot_max, LOW)
    slot_sum[...] = jnp.zeros_like(slot_sum)
    list_copy.wait()
    filled = make_work(near_list, near_work, NEAR_UNROLL)
    slot_loop(
        filled, near_work, NEAR_UNROLL, near_list,
        lambda s, row: position(core, s) + jnp.minimum(row, SPAN) - SPAN,
        keys, queries, slot_max, slot_sum, True,
    )
    wq_copy.wait()
    wk_copy.wait()
    for g in range(KV_HERE):
        gate_key[g] = dot_f32(pooled_key[g], wk_ref[g], ((1,), (0,)))
        for r in range(GROUP):
            picked = slice(r * CHIP_BLOCKS, (r + 1) * CHIP_BLOCKS)
            gate_query[g, picked, :] = dot_f32(
                pooled_query[g, picked, :], wq_ref[g * GROUP + r], ((1,), (0,))
            )


def far_kernel(
    core_ref, far_list,
    k_prev_own_ref, k_prev_other_ref, k_far_ref, queries,
    max_ref, sum_ref, pooled_query, gate_query, near_key, near_gate_key, wk_ref,
    out_ref,
    keys, slot_max, slot_sum, pooled_key, shares, hits, far_work,
):
    core = core_ref[0]
    half = ROWS * BLOCK
    for place, ref in ((0, k_far_ref), (1 + core, k_prev_own_ref), (2 - core, k_prev_other_ref)):
        tile = ref[...]
        at = place * half if isinstance(place, int) else pl.multiple_of(place * half, half)
        row = place * ROWS if isinstance(place, int) else pl.multiple_of(place * ROWS, ROWS)
        keys[pl.ds(at, half), :] = tile
        for g, pooled in enumerate(pool_keys(tile)):
            pooled_key[g, pl.ds(row, ROWS), :] = pooled
    for g in range(KV_HERE):
        pooled_key[g, SPAN:SPAN + CHIP_BLOCKS, :] = near_key[g]
    slot_max[...] = max_ref[...]
    slot_sum[...] = sum_ref[...]
    shares[...] = jnp.zeros_like(shares)
    hits[...] = jnp.zeros_like(hits)
    filled = make_work(far_list, far_work, FAR_UNROLL)
    slot_loop(
        filled, far_work, FAR_UNROLL, far_list,
        lambda s, row: jnp.where(row <= SPAN, position(core, s) + row, 0),
        keys, queries, slot_max, slot_sum, False,
    )

    live = lax.broadcasted_iota(jnp.int32, (SLOT_ROWS, WIDTH), 0) <= SPAN
    spread = jnp.where(
        lax.broadcasted_iota(jnp.int32, (WIDTH, LANES), 0) // BLOCK
        == lax.broadcasted_iota(jnp.int32, (WIDTH, LANES), 1) // CHIP_BLOCKS,
        1.0 / BLOCK, 0.0,
    ).astype(jnp.bfloat16)
    lane_block = lax.broadcasted_iota(jnp.int32, (SLOT_ROWS, LANES), 1) % CHIP_BLOCKS

    @pl.loop(0, CHIP_BLOCKS // 4)
    def _(step):
        found = []
        for e in range(4):
            s = step * 4 + e
            for g in range(KV_HERE):
                tops = jnp.where(live, slot_max[s * KV_HERE + g], LOW)
                top = jnp.max(tops, axis=0, keepdims=True)
                weight = jnp.where(
                    live, slot_sum[s * KV_HERE + g] * jnp.exp2((tops - top) * EXP_SCALE), 0.0
                )
                share = weight / jnp.sum(weight, axis=0, keepdims=True)
                coarse = share.astype(jnp.bfloat16)
                fine = (share - coarse.astype(jnp.float32)).astype(jnp.bfloat16)
                mean = (
                    jnp.dot(coarse, spread, preferred_element_type=jnp.float32)
                    + jnp.dot(fine, spread, preferred_element_type=jnp.float32)
                )
                found.append((shares.at[g], position(core, s), jnp.where(lane_block == s, mean, 0.0)))
                if g == 0:
                    filled = jnp.where(tops > 0.5 * LOW, 1.0, 0.0).astype(jnp.bfloat16)
                    hit = jnp.dot(filled, spread, preferred_element_type=jnp.float32)
                    found.append((hits, position(core, s), jnp.where(lane_block == s, hit, 0.0)))
        for table, block, mine in found:
            table[pl.ds(block, SLOT_ROWS), :] += mine

    scale = 1.0 / math.sqrt(HEAD_DIM)
    window = SPAN + CHIP_BLOCKS
    usable = hits[0:window, :] > 0.5
    divergence = jnp.zeros((1, LANES), jnp.float32)
    key_base = CHIP_BLOCKS + ROWS
    for g in range(KV_HERE):
        far_gate_key = dot_f32(pooled_key[g, 0:SPAN, :], wk_ref[g], ((1,), (0,)))
        gate_key = jnp.concatenate([far_gate_key, near_gate_key[g]], axis=0)
        logits = dot_f32(gate_key, gate_query[g], ((1,), (1,))) * scale
        logits = jnp.where(usable, logits, LOW)
        top = jnp.max(logits, axis=0, keepdims=True)
        weight = jnp.where(usable, jnp.exp(logits - top), 0.0)
        mass = jnp.sum(weight, axis=0, keepdims=True)
        log_gate = jnp.where(usable, logits - top - jnp.log(mass), 0.0)
        target = shares[g, 0:window, :]
        log_target = jnp.log(jnp.where(target > 0.0, target, 1.0))
        terms = jnp.where(usable, target * (log_target - log_gate), 0.0)
        divergence += jnp.sum(terms, axis=0, keepdims=True)
        target = jnp.where(usable, target, 0.0)
        slope = (weight / mass) * jnp.sum(target, axis=0, keepdims=True) - target
        slope = slope * (scale / 32.0)
        d_query = dot_f32(slope, gate_key, ((0,), (0,)))
        d_key = dot_f32(slope, gate_query[g], ((1,), (0,)))
        for r in range(GROUP):
            at = r * CHIP_BLOCKS
            pooled = pooled_query[g, at:at + CHIP_BLOCKS, :]
            for part in range(2):
                share = (g * GROUP + r) * 2 + part
                cols = slice(part * HALF_HEAD, (part + 1) * HALF_HEAD)
                out_ref[share, 0:CHIP_BLOCKS, :] = d_query[at:at + CHIP_BLOCKS, :]
                out_ref[share, CHIP_BLOCKS:key_base, :] = jnp.concatenate(
                    [pooled[0:ROWS, cols], pooled[ROWS:CHIP_BLOCKS, cols]], axis=1
                )
        key_part = dot_f32(pooled_key[g], d_key, ((0,), (0,)))
        for i in range(SHARES // KV_HERE):
            out_ref[g * (SHARES // KV_HERE) + i, key_base:key_base + KEY_ROWS, :] = (
                key_part[i * KEY_ROWS:(i + 1) * KEY_ROWS, :]
            )
    total = jnp.sum(divergence)
    for i in range(SHARES):
        out_ref[i, PART_ROWS - 8:PART_ROWS, :] = jnp.full((8, HEAD_DIM), total, jnp.float32)


def sum_kernel(parts_ref, out_ref):
    parts = parts_ref[...]
    pooled = parts[:, CHIP_BLOCKS:CHIP_BLOCKS + ROWS, :].reshape(SHARES * ROWS, HEAD_DIM)
    early = parts[:, 0:ROWS, :].reshape(SHARES * ROWS, HEAD_DIM)
    late = parts[:, ROWS:CHIP_BLOCKS, :].reshape(SHARES * ROWS, HEAD_DIM)
    out_ref[0:HALF_HEAD, :] = (
        dot_f32(pooled[:, :HALF_HEAD], early, ((0,), (0,)))
        + dot_f32(pooled[:, HALF_HEAD:], late, ((0,), (0,)))
    )
    out_ref[HALF_HEAD:, :] = jnp.sum(parts[:, CHIP_BLOCKS + ROWS:, :], axis=0)


def pack_kernel(own_ref, one_ref, two_ref, three_ref, out_ref, total_ref):
    got = (own_ref[...] + one_ref[...]) + (two_ref[...] + three_ref[...])
    total_ref[...] = got[SUM_ROWS:, :]
    coded = []
    powers = jnp.zeros((TILE, HEAD_DIM), jnp.float32)
    row = lax.broadcasted_iota(jnp.int32, (TILE, HEAD_DIM), 0)
    for tile in range(SUM_ROWS // TILE):
        value = got[tile * TILE:(tile + 1) * TILE, :]
        top = jnp.max(jnp.abs(value), axis=0, keepdims=True)
        power = jnp.clip(jnp.ceil(jnp.log2(jnp.maximum(top, 1e-35))), -110.0, 110.0)
        level = jnp.clip(jnp.round(value * jnp.exp2(-power) * LEVELS), -32767.0, 32767.0)
        coded.append(level.astype(jnp.int32).astype(jnp.int16))
        powers = jnp.where(row == tile, power, powers)
    coded.append(powers.astype(jnp.int32).astype(jnp.int16))
    coded = jnp.concatenate(coded, axis=0)
    for i in range(SHARES):
        out_ref[i] = coded


def unpack_kernel(place_ref, mine_ref, other_ref, query_ref, key_ref):
    core = place_ref[0]
    for source, ref in ((core, mine_ref), (1 - core, other_ref)):
        for share in range(STEP_SHARES):
            powers = ref[share, SUM_ROWS:SUM_ROWS + TILE, :].astype(jnp.int32).astype(jnp.float32)
            scale = jnp.exp2(powers[0:8, :]) * (1.0 / LEVELS)
            for tile in range(SUM_ROWS // TILE):
                coded = ref[share, tile * TILE:(tile + 1) * TILE, :]
                value = coded.astype(jnp.int32).astype(jnp.float32) * scale[tile:tile + 1, :]
                if tile < HALF_HEAD // TILE:
                    query_ref[source, pl.ds(share * HALF_HEAD + tile * TILE, TILE), :] = value
                else:
                    at = share * KEY_ROWS + tile * TILE - HALF_HEAD
                    key_ref[source, pl.ds(at, TILE), :] = value


def pack(*parts):
    return pl.pallas_call(
        pack_kernel,
        out_shape=[
            shaped((SHARES, SUM_ROWS + TILE, HEAD_DIM), jnp.int16), shaped((8, HEAD_DIM)),
        ],
        name="pack",
    )(*parts)


def unpack(place, mine, other):
    rows = HALF_HEAD, KEY_ROWS
    return pl.pallas_call(
        unpack_kernel,
        grid_spec=pltpu.PrefetchScalarGridSpec(
            num_scalar_prefetch=1,
            grid=(SHARES // STEP_SHARES,),
            in_specs=[
                pl.BlockSpec((STEP_SHARES, SUM_ROWS + TILE, HEAD_DIM), lambda i, c: (i, 0, 0))
            ] * 2,
            out_specs=[
                pl.BlockSpec((2, STEP_SHARES * n, HEAD_DIM), lambda i, c: (0, i, 0)) for n in rows
            ],
        ),
        out_shape=[shaped((2, SHARES * n, HEAD_DIM)) for n in rows],
        name="unpack",
    )(place, mine, other)


def swap(x, axis):
    return lax.ppermute(x, axis, [(0, 1), (1, 0)])


def whole(*shape):
    return pl.BlockSpec(shape, lambda i, *_: (0,) * len(shape))


def shaped(shape, dtype=jnp.float32):
    return jax.ShapeDtypeStruct(shape, dtype)


def smem():
    return pl.BlockSpec(memory_space=pltpu.SMEM)


def cut_prev_kernel(place_ref, give_in, after_ref, give_ref):
    give_ref[...] = give_in[...]


def cut_prev(place, keys, after):
    half = ROWS * BLOCK
    return pl.pallas_call(
        cut_prev_kernel,
        grid_spec=pltpu.PrefetchScalarGridSpec(
            num_scalar_prefetch=1,
            grid=(1,),
            in_specs=[
                pl.BlockSpec((half, K_COLS), lambda i, c: (0, 1 - c[0])),
                pl.BlockSpec(memory_space=pl.ANY),
            ],
            out_specs=whole(half, K_COLS),
        ),
        out_shape=shaped((half, K_COLS), jnp.bfloat16),
        name="cut_prev",
    )(place, keys, after)


def near_call(place, tables, q_own, q_other, k_mine, k_other, wq, wk):
    half = ROWS * BLOCK
    outs = [
        shaped((CHIP_BLOCKS * KV_HERE, WIDTH, HEAD_DIM), jnp.bfloat16),
        shaped((CHIP_BLOCKS * KV_HERE, SLOT_ROWS, WIDTH)),
        shaped((CHIP_BLOCKS * KV_HERE, SLOT_ROWS, WIDTH)),
        shaped((KV_HERE, LANES, HEAD_DIM)),
        shaped((KV_HERE, LANES, HEAD_DIM)),
        shaped((KV_HERE, CHIP_BLOCKS, POOL)),
        shaped((KV_HERE, CHIP_BLOCKS, HEAD_DIM)),
        shaped((CHIP_BLOCKS, HEAD_DIM), jnp.int32),
    ]
    return pl.pallas_call(
        near_kernel,
        grid_spec=pltpu.PrefetchScalarGridSpec(
            num_scalar_prefetch=1,
            grid=(1,),
            in_specs=[whole(ROWS, CAND), smem()] * 2 + [
                pl.BlockSpec(memory_space=pltpu.HBM),
                pl.BlockSpec((half, Q_COLS), lambda i, c: (0, c[0])),
                pl.BlockSpec((half, K_COLS), lambda i, c: (0, c[0])),
                pl.BlockSpec((half, K_COLS), lambda i, c: (0, c[0])),
                pl.BlockSpec(memory_space=pltpu.HBM),
                pl.BlockSpec(memory_space=pltpu.HBM),
            ],
            out_specs=[whole(*o.shape) for o in outs],
            scratch_shapes=[
                pltpu.VMEM((CHIP_BLOCKS * BLOCK, K_COLS), jnp.bfloat16),
                pltpu.VMEM((CHIP_BLOCKS, HEAD_DIM), jnp.int32),
                pltpu.SMEM((CHIP_BLOCKS, HEAD_DIM), jnp.int32),
                pltpu.SMEM((WORK_SIZE,), jnp.int32),
                pltpu.VMEM((half, Q_COLS), jnp.bfloat16),
                pltpu.VMEM((HEADS_HERE, HEAD_DIM, HEAD_DIM), jnp.float32),
                pltpu.VMEM((KV_HERE, POOL, HEAD_DIM), jnp.float32),
                pltpu.SemaphoreType.DMA((4,)),
            ],
        ),
        out_shape=outs,
        compiler_params=pltpu.CompilerParams(vmem_limit_bytes=VMEM_BYTES),
        cost_estimate=pl.CostEstimate(
            flops=2_000_000_000, bytes_accessed=8_000_000, transcendentals=8_000_000
        ),
        name="near",
    )(place, *tables, q_own, q_other, k_mine, k_other, wq, wk)


def far_call(place, k_prev_own, k_prev_other, k_far, near, wk):
    half = ROWS * BLOCK
    args = (k_prev_own, k_prev_other, k_far, *near[:-1])
    return pl.pallas_call(
        far_kernel,
        grid_spec=pltpu.PrefetchScalarGridSpec(
            num_scalar_prefetch=1,
            grid=(1,),
            in_specs=[smem(), pl.BlockSpec((half, K_COLS), lambda i, c: (0, c[0]))]
            + [whole(*a.shape) for a in args[1:]] + [
                pl.BlockSpec((KV_HERE, POOL, HEAD_DIM), lambda i, c: (c[0], 0, 0)),
            ],
            out_specs=whole(SHARES, PART_ROWS, HEAD_DIM),
            scratch_shapes=[
                pltpu.VMEM((SPAN * BLOCK, K_COLS), jnp.bfloat16),
                pltpu.VMEM((CHIP_BLOCKS * KV_HERE, SLOT_ROWS, WIDTH), jnp.float32),
                pltpu.VMEM((CHIP_BLOCKS * KV_HERE, SLOT_ROWS, WIDTH), jnp.float32),
                pltpu.VMEM((KV_HERE, SPAN + CHIP_BLOCKS, POOL), jnp.float32),
                pltpu.VMEM((KV_HERE, PADDED, LANES), jnp.float32),
                pltpu.VMEM((PADDED, LANES), jnp.float32),
                pltpu.SMEM((WORK_SIZE,), jnp.int32),
            ],
        ),
        out_shape=shaped((SHARES, PART_ROWS, HEAD_DIM)),
        compiler_params=pltpu.CompilerParams(vmem_limit_bytes=VMEM_BYTES),
        cost_estimate=pl.CostEstimate(
            flops=2_000_000_000, bytes_accessed=8_000_000, transcendentals=8_000_000
        ),
        name="far",
    )(place, near[-1], *args, wk)


def body(
    teacher_queries, teacher_keys, query_projection, key_projection, block_offsets, valid_counts
):
    chips = ("za", "zb", "yh", "x")
    places = chips + ("core",)
    count = lax.axis_size(places)
    core = lax.axis_index("core")
    place = jnp.stack([core, lax.axis_index(chips)]).astype(jnp.int32)

    columns = lambda x, which: lax.dynamic_slice_in_dim(x, which * K_COLS, K_COLS, 1)
    k_prev = lax.ppermute(teacher_keys, places, [(i, i + 2) for i in range(count - 2)])
    k_other = swap(teacher_keys, "core")
    q_other = swap(teacher_queries, "core")
    tables = (block_offsets, valid_counts, swap(block_offsets, "core"), swap(valid_counts, "core"))
    k_far = lax.ppermute(
        jnp.where(core == 1, columns(teacher_keys, core), columns(k_other, core)),
        places, [(i, i + 4) for i in range(count - 4)],
    )
    near = near_call(
        place, tables, teacher_queries, q_other, teacher_keys, k_other,
        query_projection, key_projection,
    )
    k_prev_other = swap(cut_prev(place, k_prev, near[-1]), "core")
    parts = far_call(place, k_prev, k_prev_other, k_far, near, key_projection)

    group = ("zb", "yh", "x")
    got = lax.all_to_all(parts, group, 0, 0)
    got = pl.pallas_call(sum_kernel, out_shape=shaped((SUM_ROWS + 8, HEAD_DIM)), name="sum")(got)
    one, two, three = (
        lax.ppermute(got, "za", [(i, i ^ step) for i in range(4)]) for step in (1, 2, 3)
    )
    coded, total = pack(got, one, two, three)
    total = total + swap(total, "head")
    total = total + swap(total, "core")
    mine = lax.all_to_all(coded, group, 0, 0)
    query_gradient, key_gradient = unpack(place, mine, swap(mine, "core"))
    return (
        query_gradient.reshape(2 * HEADS_HERE, HEAD_DIM, HEAD_DIM),
        key_gradient.reshape(2 * KV_HERE, POOL, HEAD_DIM),
        total[0, 0] / (1024 * HEADS),
    )


def solution(mesh):
    split = Mesh(mesh.devices.reshape(4, 2, 2, 4, 2, 2), ("za", "zb", "yh", "x", "core", "head"))
    ctx = ("za", "zb", "yh", "x", "core")
    placed = (
        P(ctx, "head"),
        P(ctx, "head"),
        P("head", None, None),
        P("head", None, None),
        P(ctx, None),
        P(ctx),
    )
    return jax.shard_map(
        body,
        mesh=split,
        in_specs=placed,
        out_specs=(P("head", None, None), P("head", None, None), P()),
        check_vma=False,
    )
```

```python
import math

import jax
import jax.numpy as jnp
from jax import lax
from jax.experimental import pallas as pl
from jax.experimental.pallas import tpu as pltpu
from jax.sharding import Mesh, PartitionSpec as P

HEADS = 32
KV_HEADS = 8
HEAD_DIM = 128
BLOCK = 64
CAND = 24
REACH = 4

ROWS = 8
SPAN = 24
CHIP_BLOCKS = 2 * ROWS
PADDED = 48
KV_HERE = 2
GROUP = HEADS // KV_HEADS
HEADS_HERE = KV_HERE * GROUP
Q_COLS = HEADS_HERE * HEAD_DIM
K_COLS = KV_HERE * HEAD_DIM
POOL = 3 * HEAD_DIM
WIDTH = GROUP * BLOCK
DUMMY = 31
SLOT_ROWS = 32
LANES = GROUP * CHIP_BLOCKS
SHARES = 16
KEY_ROWS = KV_HERE * POOL // SHARES
HALF_HEAD = HEAD_DIM // 2
PART_ROWS = CHIP_BLOCKS + ROWS + KEY_ROWS + 8
SUM_ROWS = HALF_HEAD + KEY_ROWS
VMEM_BYTES = 40 * 1024 * 1024
NEAR_UNROLL = 4
FAR_UNROLL = 6
TILE = 16
STEP_SHARES = 16
LEVELS = 32760.0
WORK_SIZE = CHIP_BLOCKS * CAND // 4 + 16
LOW = -1e30
EXP_SCALE = math.log2(math.e) / math.sqrt(HEAD_DIM)


def dot_f32(a, b, dims):
    def one(x, y):
        return lax.dot_general(x, y, (dims, ((), ())), preferred_element_type=jnp.float32)

    a_top = a.astype(jnp.bfloat16)
    b_top = b.astype(jnp.bfloat16)
    a_low = (a - a_top.astype(jnp.float32)).astype(jnp.bfloat16)
    b_low = (b - b_top.astype(jnp.float32)).astype(jnp.bfloat16)
    return one(a_top, b_top) + (one(a_top, b_low) + one(a_low, b_top))


def pool_keys(tile):
    wide = tile.astype(jnp.float32).reshape(ROWS, BLOCK, K_COLS)
    top = jnp.max(wide, axis=1)
    low = jnp.min(wide, axis=1)
    mean = jnp.sum(wide, axis=1) * (1.0 / BLOCK)
    return [
        jnp.concatenate(
            [v[:, g * HEAD_DIM:(g + 1) * HEAD_DIM] for v in (top, low, mean)], axis=1
        )
        for g in range(KV_HERE)
    ]


def slot_table(offsets_ref, counts_ref):
    table = jnp.concatenate(
        [offsets_ref[...], jnp.zeros((ROWS, HEAD_DIM - CAND), jnp.int32)], axis=1
    )
    row = lax.broadcasted_iota(jnp.int32, (ROWS, HEAD_DIM), 0)
    lane = lax.broadcasted_iota(jnp.int32, (ROWS, HEAD_DIM), 1)
    for j in range(ROWS):
        table = jnp.where((lane == CAND) & (row == j), counts_ref[j], table)
    return table.astype(jnp.float32)


def make_lists(core, chip, table):
    shape = (CHIP_BLOCKS, HEAD_DIM)
    lane = lax.broadcasted_iota(jnp.int32, shape, 1)
    row = lax.broadcasted_iota(jnp.int32, shape, 0)
    block = position(core, row)
    offset = table.astype(jnp.int32)
    count = jnp.sum(jnp.where(lane == CAND, table, 0.0), axis=1, keepdims=True).astype(jnp.int32)
    usable = (lane < count) & (offset <= chip * CHIP_BLOCKS + block)
    near = jnp.where(usable & (offset <= block), 1.0, 0.0)
    far = jnp.where(usable & (offset > block), 1.0, 0.0)
    picked = jnp.concatenate([near, far], axis=0)
    before = jnp.where(
        lax.broadcasted_iota(jnp.int32, (HEAD_DIM, HEAD_DIM), 0)
        < lax.broadcasted_iota(jnp.int32, (HEAD_DIM, HEAD_DIM), 1), 1.0, 0.0,
    ).astype(jnp.bfloat16)
    rank = jnp.dot(picked.astype(jnp.bfloat16), before, preferred_element_type=jnp.float32)
    rank = jnp.where(picked > 0.0, rank, -1.0)
    value = (SPAN - DUMMY) - jnp.concatenate([table, table], axis=0)
    lane = jnp.concatenate([lane, lane], axis=0)
    packed = jnp.where(lane == CAND, jnp.sum(picked, axis=1, keepdims=True), float(DUMMY))
    for slot in range(CAND):
        here = jnp.sum(jnp.where(rank == slot, value, 0.0), axis=1, keepdims=True)
        packed = jnp.where(lane == slot, here + DUMMY, packed)
    return packed.astype(jnp.int32)


def make_work(list_ref, work, unroll):
    def per_block(s, total):
        count = list_ref[s, CAND]
        for i in range(CAND // 4):
            work[total] = s * CAND + i * 4
            total += jnp.where(i * 4 < count, 1, 0)
        return total

    filled = lax.fori_loop(0, CHIP_BLOCKS, per_block, jnp.int32(0))
    spare = work[jnp.maximum(filled - 1, 0)]
    for extra in range(unroll - 1):
        work[filled + extra] = spare
    return filled


def position(core, s):
    return jnp.where(s < ROWS, ROWS * core + s, ROWS * (1 - core) + s - ROWS)


def slot_loop(filled, work, unroll, list_ref, tile_start, keys, queries, slot_max, slot_sum, diagonal):
    lane = lax.broadcasted_iota(jnp.int32, (BLOCK, WIDTH), 1) % BLOCK
    key_row = lax.broadcasted_iota(jnp.int32, (BLOCK, WIDTH), 0)

    @pl.loop(0, (filled + unroll - 1) // unroll)
    def _(step):
        found = []
        for e in range(unroll):
            first = work[step * unroll + e]
            s = first // CAND
            rows = [list_ref[s, first - s * CAND + i] for i in range(4)]
            starts = [pl.multiple_of(tile_start(s, row) * BLOCK, BLOCK) for row in rows]
            if diagonal:
                keep = key_row <= lane + jnp.where(first == s * CAND, 0, BLOCK)
            for g in range(KV_HERE):
                tiles = [
                    keys[pl.ds(start, BLOCK), g * HEAD_DIM:(g + 1) * HEAD_DIM] for start in starts
                ]
                scores = lax.dot_general(
                    jnp.concatenate(tiles, axis=0), queries[s * KV_HERE + g],
                    (((1,), (1,)), ((), ())), preferred_element_type=jnp.float32,
                )
                for i, row in enumerate(rows):
                    part = scores[i * BLOCK:(i + 1) * BLOCK, :]
                    if diagonal and i == 0:
                        part = jnp.where(keep, part, LOW)
                    top = jnp.max(part, axis=0, keepdims=True)
                    total = jnp.sum(
                        jnp.exp2((part - top) * EXP_SCALE), axis=0, keepdims=True
                    )
                    found.append((s * KV_HERE + g, row, top, total))
        for index, row, top, total in found:
            slot_max[index, pl.ds(row, 1), :] = top
            slot_sum[index, pl.ds(row, 1), :] = total


def near_kernel(
    place_ref, offsets_own_ref, counts_own_ref, offsets_other_ref, counts_other_ref,
    q_own_hbm, q_other_hbm, k_own_hbm, k_other_hbm, wq_hbm, wk_hbm,
    queries, slot_max, slot_sum, pooled_query, gate_query, pooled_key, gate_key,
    far_list,
    keys, near_vector, near_list, near_work, q_own_ref, q_other_ref, k_own_ref, k_other_ref,
    wq_ref, wk_ref, sems,
):
    core_ref = place_ref
    core = core_ref[0]
    half = ROWS * BLOCK
    q_copy = pltpu.make_async_copy(
        q_own_hbm.at[:, pl.ds(pl.multiple_of(core * Q_COLS, Q_COLS), Q_COLS)], q_own_ref, sems.at[1]
    )
    wq_copy = pltpu.make_async_copy(
        wq_hbm.at[pl.ds(core * HEADS_HERE, HEADS_HERE)], wq_ref, sems.at[2]
    )
    wk_copy = pltpu.make_async_copy(
        wk_hbm.at[pl.ds(core * KV_HERE, KV_HERE)], wk_ref, sems.at[3]
    )
    q_cols = pl.ds(pl.multiple_of(core * Q_COLS, Q_COLS), Q_COLS)
    k_cols = pl.ds(pl.multiple_of(core * K_COLS, K_COLS), K_COLS)
    q_other_copy = pltpu.make_async_copy(q_other_hbm.at[:, q_cols], q_other_ref, sems.at[4])
    k_own_copy = pltpu.make_async_copy(k_own_hbm.at[:, k_cols], k_own_ref, sems.at[5])
    k_other_copy = pltpu.make_async_copy(k_other_hbm.at[:, k_cols], k_other_ref, sems.at[6])
    k_own_copy.start()
    k_other_copy.start()
    q_other_copy.start()
    q_copy.start()
    wq_copy.start()
    wk_copy.start()
    lists = make_lists(
        core, place_ref[1],
        jnp.concatenate(
            [
                slot_table(offsets_own_ref, counts_own_ref),
                slot_table(offsets_other_ref, counts_other_ref),
            ],
            axis=0,
        ),
    )
    far_list[...] = lists[CHIP_BLOCKS:]
    near_vector[...] = lists[0:CHIP_BLOCKS]
    list_copy = pltpu.make_async_copy(near_vector, near_list, sems.at[0])
    list_copy.start()
    k_own_copy.wait()
    k_other_copy.wait()
    for source, ref in ((core, k_own_ref), (1 - core, k_other_ref)):
        tile = ref[...]
        keys[pl.ds(pl.multiple_of(source * half, half), half), :] = tile
        for g, pooled in enumerate(pool_keys(tile)):
            pooled_key[g, pl.ds(pl.multiple_of(source * ROWS, ROWS), ROWS), :] = pooled

    def prepare(s, q_ref, at):
        for g in range(KV_HERE):
            for r in range(GROUP):
                head = g * GROUP + r
                tile = q_ref[pl.ds(at, BLOCK), head * HEAD_DIM:(head + 1) * HEAD_DIM]
                queries[s * KV_HERE + g, r * BLOCK:(r + 1) * BLOCK, :] = tile
                pooled_query[g, pl.ds(r * CHIP_BLOCKS + s, 1), :] = jnp.sum(
                    tile.astype(jnp.float32), axis=0, keepdims=True
                ) * (1.0 / BLOCK)

    q_other_copy.wait()
    for source in (1, 0):
        q_ref = (q_own_ref, q_other_ref)[source]
        if source == 0:
            q_copy.wait()

        @pl.loop(0, ROWS)
        def _(j):
            prepare(source * ROWS + j, q_ref, pl.multiple_of(j * BLOCK, BLOCK))

    slot_max[...] = jnp.full_like(slot_max, LOW)
    slot_sum[...] = jnp.zeros_like(slot_sum)
    list_copy.wait()
    filled = make_work(near_list, near_work, NEAR_UNROLL)
    slot_loop(
        filled, near_work, NEAR_UNROLL, near_list,
        lambda s, row: position(core, s) + jnp.minimum(row, SPAN) - SPAN,
        keys, queries, slot_max, slot_sum, True,
    )
    wq_copy.wait()
    wk_copy.wait()
    for g in range(KV_HERE):
        gate_key[g] = dot_f32(pooled_key[g], wk_ref[g], ((1,), (0,)))
        for r in range(GROUP):
            picked = slice(r * CHIP_BLOCKS, (r + 1) * CHIP_BLOCKS)
            gate_query[g, picked, :] = dot_f32(
                pooled_query[g, picked, :], wq_ref[g * GROUP + r], ((1,), (0,))
            )


def far_kernel(
    core_ref, far_list,
    k_prev_hbm, k_prev_other_ref, k_far_ref, queries,
    max_ref, sum_ref, pooled_query, gate_query, near_key, near_gate_key, wk_ref,
    out_ref,
    keys, slot_max, slot_sum, pooled_key, shares, hits, far_work,
    k_prev_own_ref, sems,
):
    core = core_ref[0]
    half = ROWS * BLOCK
    k_copy = pltpu.make_async_copy(
        k_prev_hbm.at[:, pl.ds(pl.multiple_of(core * K_COLS, K_COLS), K_COLS)],
        k_prev_own_ref, sems.at[0],
    )
    k_copy.start()
    for place, ref in ((0, k_far_ref), (2 - core, k_prev_other_ref), (1 + core, k_prev_own_ref)):
        if ref is k_prev_own_ref:
            k_copy.wait()
        tile = ref[...]
        at = place * half if isinstance(place, int) else pl.multiple_of(place * half, half)
        row = place * ROWS if isinstance(place, int) else pl.multiple_of(place * ROWS, ROWS)
        keys[pl.ds(at, half), :] = tile
        for g, pooled in enumerate(pool_keys(tile)):
            pooled_key[g, pl.ds(row, ROWS), :] = pooled
    for g in range(KV_HERE):
        pooled_key[g, SPAN:SPAN + CHIP_BLOCKS, :] = near_key[g]
    slot_max[...] = max_ref[...]
    slot_sum[...] = sum_ref[...]
    shares[...] = jnp.zeros_like(shares)
    hits[...] = jnp.zeros_like(hits)
    filled = make_work(far_list, far_work, FAR_UNROLL)
    slot_loop(
        filled, far_work, FAR_UNROLL, far_list,
        lambda s, row: jnp.where(row <= SPAN, position(core, s) + row, 0),
        keys, queries, slot_max, slot_sum, False,
    )

    live = lax.broadcasted_iota(jnp.int32, (SLOT_ROWS, WIDTH), 0) <= SPAN
    spread = jnp.where(
        lax.broadcasted_iota(jnp.int32, (WIDTH, LANES), 0) // BLOCK
        == lax.broadcasted_iota(jnp.int32, (WIDTH, LANES), 1) // CHIP_BLOCKS,
        1.0 / BLOCK, 0.0,
    ).astype(jnp.bfloat16)
    lane_block = lax.broadcasted_iota(jnp.int32, (SLOT_ROWS, LANES), 1) % CHIP_BLOCKS

    @pl.loop(0, CHIP_BLOCKS // 4)
    def _(step):
        found = []
        for e in range(4):
            s = step * 4 + e
            for g in range(KV_HERE):
                tops = jnp.where(live, slot_max[s * KV_HERE + g], LOW)
                top = jnp.max(tops, axis=0, keepdims=True)
                weight = jnp.where(
                    live, slot_sum[s * KV_HERE + g] * jnp.exp2((tops - top) * EXP_SCALE), 0.0
                )
                share = weight / jnp.sum(weight, axis=0, keepdims=True)
                coarse = share.astype(jnp.bfloat16)
                fine = (share - coarse.astype(jnp.float32)).astype(jnp.bfloat16)
                mean = (
                    jnp.dot(coarse, spread, preferred_element_type=jnp.float32)
                    + jnp.dot(fine, spread, preferred_element_type=jnp.float32)
                )
                found.append((shares.at[g], position(core, s), jnp.where(lane_block == s, mean, 0.0)))
                if g == 0:
                    filled = jnp.where(tops > 0.5 * LOW, 1.0, 0.0).astype(jnp.bfloat16)
                    hit = jnp.dot(filled, spread, preferred_element_type=jnp.float32)
                    found.append((hits, position(core, s), jnp.where(lane_block == s, hit, 0.0)))
        for table, block, mine in found:
            table[pl.ds(block, SLOT_ROWS), :] += mine

    scale = 1.0 / math.sqrt(HEAD_DIM)
    window = SPAN + CHIP_BLOCKS
    usable = hits[0:window, :] > 0.5
    divergence = jnp.zeros((1, LANES), jnp.float32)
    key_base = CHIP_BLOCKS + ROWS
    for g in range(KV_HERE):
        far_gate_key = dot_f32(pooled_key[g, 0:SPAN, :], wk_ref[g], ((1,), (0,)))
        gate_key = jnp.concatenate([far_gate_key, near_gate_key[g]], axis=0)
        logits = dot_f32(gate_key, gate_query[g], ((1,), (1,))) * scale
        logits = jnp.where(usable, logits, LOW)
        top = jnp.max(logits, axis=0, keepdims=True)
        weight = jnp.where(usable, jnp.exp(logits - top), 0.0)
        mass = jnp.sum(weight, axis=0, keepdims=True)
        log_gate = jnp.where(usable, logits - top - jnp.log(mass), 0.0)
        target = shares[g, 0:window, :]
        log_target = jnp.log(jnp.where(target > 0.0, target, 1.0))
        terms = jnp.where(usable, target * (log_target - log_gate), 0.0)
        divergence += jnp.sum(terms, axis=0, keepdims=True)
        target = jnp.where(usable, target, 0.0)
        slope = (weight / mass) * jnp.sum(target, axis=0, keepdims=True) - target
        slope = slope * (scale / 32.0)
        d_query = dot_f32(slope, gate_key, ((0,), (0,)))
        d_key = dot_f32(slope, gate_query[g], ((1,), (0,)))
        for r in range(GROUP):
            at = r * CHIP_BLOCKS
            pooled = pooled_query[g, at:at + CHIP_BLOCKS, :]
            for part in range(2):
                share = (g * GROUP + r) * 2 + part
                cols = slice(part * HALF_HEAD, (part + 1) * HALF_HEAD)
                out_ref[share, 0:CHIP_BLOCKS, :] = d_query[at:at + CHIP_BLOCKS, :]
                out_ref[share, CHIP_BLOCKS:key_base, :] = jnp.concatenate(
                    [pooled[0:ROWS, cols], pooled[ROWS:CHIP_BLOCKS, cols]], axis=1
                )
        key_part = dot_f32(pooled_key[g], d_key, ((0,), (0,)))
        for i in range(SHARES // KV_HERE):
            out_ref[g * (SHARES // KV_HERE) + i, key_base:key_base + KEY_ROWS, :] = (
                key_part[i * KEY_ROWS:(i + 1) * KEY_ROWS, :]
            )
    total = jnp.sum(divergence)
    for i in range(SHARES):
        out_ref[i, PART_ROWS - 8:PART_ROWS, :] = jnp.full((8, HEAD_DIM), total, jnp.float32)


def sum_kernel(parts_ref, out_ref):
    parts = parts_ref[...]
    pooled = parts[:, CHIP_BLOCKS:CHIP_BLOCKS + ROWS, :].reshape(SHARES * ROWS, HEAD_DIM)
    early = parts[:, 0:ROWS, :].reshape(SHARES * ROWS, HEAD_DIM)
    late = parts[:, ROWS:CHIP_BLOCKS, :].reshape(SHARES * ROWS, HEAD_DIM)
    out_ref[0:HALF_HEAD, :] = (
        dot_f32(pooled[:, :HALF_HEAD], early, ((0,), (0,)))
        + dot_f32(pooled[:, HALF_HEAD:], late, ((0,), (0,)))
    )
    out_ref[HALF_HEAD:, :] = jnp.sum(parts[:, CHIP_BLOCKS + ROWS:, :], axis=0)


def pack_kernel(own_ref, one_ref, two_ref, three_ref, out_ref, total_ref):
    got = (own_ref[...] + one_ref[...]) + (two_ref[...] + three_ref[...])
    total_ref[...] = got[SUM_ROWS:, :]
    coded = []
    powers = jnp.zeros((TILE, HEAD_DIM), jnp.float32)
    row = lax.broadcasted_iota(jnp.int32, (TILE, HEAD_DIM), 0)
    for tile in range(SUM_ROWS // TILE):
        value = got[tile * TILE:(tile + 1) * TILE, :]
        top = jnp.max(jnp.abs(value), axis=0, keepdims=True)
        power = jnp.clip(jnp.ceil(jnp.log2(jnp.maximum(top, 1e-35))), -110.0, 110.0)
        level = jnp.clip(jnp.round(value * jnp.exp2(-power) * LEVELS), -32767.0, 32767.0)
        coded.append(level.astype(jnp.int32).astype(jnp.int16))
        powers = jnp.where(row == tile, power, powers)
    coded.append(powers.astype(jnp.int32).astype(jnp.int16))
    coded = jnp.concatenate(coded, axis=0)
    for i in range(SHARES):
        out_ref[i] = coded


def unpack_kernel(place_ref, mine_ref, other_ref, query_ref, key_ref):
    core = place_ref[0]
    for source, ref in ((core, mine_ref), (1 - core, other_ref)):
        for share in range(STEP_SHARES):
            powers = ref[share, SUM_ROWS:SUM_ROWS + TILE, :].astype(jnp.int32).astype(jnp.float32)
            scale = jnp.exp2(powers[0:8, :]) * (1.0 / LEVELS)
            for tile in range(SUM_ROWS // TILE):
                coded = ref[share, tile * TILE:(tile + 1) * TILE, :]
                value = coded.astype(jnp.int32).astype(jnp.float32) * scale[tile:tile + 1, :]
                if tile < HALF_HEAD // TILE:
                    query_ref[source, pl.ds(share * HALF_HEAD + tile * TILE, TILE), :] = value
                else:
                    at = share * KEY_ROWS + tile * TILE - HALF_HEAD
                    key_ref[source, pl.ds(at, TILE), :] = value


def pack(*parts):
    return pl.pallas_call(
        pack_kernel,
        out_shape=[
            shaped((SHARES, SUM_ROWS + TILE, HEAD_DIM), jnp.int16), shaped((8, HEAD_DIM)),
        ],
        name="pack",
    )(*parts)


def unpack(place, mine, other):
    rows = HALF_HEAD, KEY_ROWS
    return pl.pallas_call(
        unpack_kernel,
        grid_spec=pltpu.PrefetchScalarGridSpec(
            num_scalar_prefetch=1,
            grid=(SHARES // STEP_SHARES,),
            in_specs=[
                pl.BlockSpec((STEP_SHARES, SUM_ROWS + TILE, HEAD_DIM), lambda i, c: (i, 0, 0))
            ] * 2,
            out_specs=[
                pl.BlockSpec((2, STEP_SHARES * n, HEAD_DIM), lambda i, c: (0, i, 0)) for n in rows
            ],
        ),
        out_shape=[shaped((2, SHARES * n, HEAD_DIM)) for n in rows],
        name="unpack",
    )(place, mine, other)


def swap(x, axis):
    return lax.ppermute(x, axis, [(0, 1), (1, 0)])


def whole(*shape):
    return pl.BlockSpec(shape, lambda i, *_: (0,) * len(shape))


def shaped(shape, dtype=jnp.float32):
    return jax.ShapeDtypeStruct(shape, dtype)


def smem():
    return pl.BlockSpec(memory_space=pltpu.SMEM)


def cut_prev_kernel(place_ref, keys_hbm, after_ref, give_ref, sems):
    cols = pl.ds(pl.multiple_of((1 - place_ref[0]) * K_COLS, K_COLS), K_COLS)
    give = pltpu.make_async_copy(keys_hbm.at[:, cols], give_ref, sems.at[0])
    give.start()
    give.wait()


def cut_prev(place, keys, after):
    half = ROWS * BLOCK
    return pl.pallas_call(
        cut_prev_kernel,
        grid_spec=pltpu.PrefetchScalarGridSpec(
            num_scalar_prefetch=1,
            grid=(1,),
            in_specs=[
                pl.BlockSpec(memory_space=pltpu.HBM),
                pl.BlockSpec(memory_space=pl.ANY),
            ],
            out_specs=whole(half, K_COLS),
            scratch_shapes=[pltpu.SemaphoreType.DMA((1,))],
        ),
        out_shape=shaped((half, K_COLS), jnp.bfloat16),
        compiler_params=pltpu.CompilerParams(vmem_limit_bytes=4 * 1024 * 1024),
        name="cut_prev",
    )(place, keys, after)


def near_call(place, tables, q_own, q_other, k_mine, k_other, wq, wk):
    half = ROWS * BLOCK
    outs = [
        shaped((CHIP_BLOCKS * KV_HERE, WIDTH, HEAD_DIM), jnp.bfloat16),
        shaped((CHIP_BLOCKS * KV_HERE, SLOT_ROWS, WIDTH)),
        shaped((CHIP_BLOCKS * KV_HERE, SLOT_ROWS, WIDTH)),
        shaped((KV_HERE, LANES, HEAD_DIM)),
        shaped((KV_HERE, LANES, HEAD_DIM)),
        shaped((KV_HERE, CHIP_BLOCKS, POOL)),
        shaped((KV_HERE, CHIP_BLOCKS, HEAD_DIM)),
        shaped((CHIP_BLOCKS, HEAD_DIM), jnp.int32),
    ]
    return pl.pallas_call(
        near_kernel,
        grid_spec=pltpu.PrefetchScalarGridSpec(
            num_scalar_prefetch=1,
            grid=(1,),
            in_specs=[whole(ROWS, CAND), smem()] * 2 + [pl.BlockSpec(memory_space=pltpu.HBM)] * 6,
            out_specs=[whole(*o.shape) for o in outs],
            scratch_shapes=[
                pltpu.VMEM((CHIP_BLOCKS * BLOCK, K_COLS), jnp.bfloat16),
                pltpu.VMEM((CHIP_BLOCKS, HEAD_DIM), jnp.int32),
                pltpu.SMEM((CHIP_BLOCKS, HEAD_DIM), jnp.int32),
                pltpu.SMEM((WORK_SIZE,), jnp.int32),
                pltpu.VMEM((half, Q_COLS), jnp.bfloat16),
                pltpu.VMEM((half, Q_COLS), jnp.bfloat16),
                pltpu.VMEM((half, K_COLS), jnp.bfloat16),
                pltpu.VMEM((half, K_COLS), jnp.bfloat16),
                pltpu.VMEM((HEADS_HERE, HEAD_DIM, HEAD_DIM), jnp.float32),
                pltpu.VMEM((KV_HERE, POOL, HEAD_DIM), jnp.float32),
                pltpu.SemaphoreType.DMA((7,)),
            ],
        ),
        out_shape=outs,
        compiler_params=pltpu.CompilerParams(vmem_limit_bytes=VMEM_BYTES),
        cost_estimate=pl.CostEstimate(
            flops=2_000_000_000, bytes_accessed=8_000_000, transcendentals=8_000_000
        ),
        name="near",
    )(place, *tables, q_own, q_other, k_mine, k_other, wq, wk)


def far_call(place, k_prev_own, k_prev_other, k_far, near, wk):
    half = ROWS * BLOCK
    args = (k_prev_own, k_prev_other, k_far, *near[:-1])
    return pl.pallas_call(
        far_kernel,
        grid_spec=pltpu.PrefetchScalarGridSpec(
            num_scalar_prefetch=1,
            grid=(1,),
            in_specs=[smem(), pl.BlockSpec(memory_space=pltpu.HBM)]
            + [whole(*a.shape) for a in args[1:]] + [
                pl.BlockSpec((KV_HERE, POOL, HEAD_DIM), lambda i, c: (c[0], 0, 0)),
            ],
            out_specs=whole(SHARES, PART_ROWS, HEAD_DIM),
            scratch_shapes=[
                pltpu.VMEM((SPAN * BLOCK, K_COLS), jnp.bfloat16),
                pltpu.VMEM((CHIP_BLOCKS * KV_HERE, SLOT_ROWS, WIDTH), jnp.float32),
                pltpu.VMEM((CHIP_BLOCKS * KV_HERE, SLOT_ROWS, WIDTH), jnp.float32),
                pltpu.VMEM((KV_HERE, SPAN + CHIP_BLOCKS, POOL), jnp.float32),
                pltpu.VMEM((KV_HERE, PADDED, LANES), jnp.float32),
                pltpu.VMEM((PADDED, LANES), jnp.float32),
                pltpu.SMEM((WORK_SIZE,), jnp.int32),
                pltpu.VMEM((half, K_COLS), jnp.bfloat16),
                pltpu.SemaphoreType.DMA((1,)),
            ],
        ),
        out_shape=shaped((SHARES, PART_ROWS, HEAD_DIM)),
        compiler_params=pltpu.CompilerParams(vmem_limit_bytes=VMEM_BYTES),
        cost_estimate=pl.CostEstimate(
            flops=2_000_000_000, bytes_accessed=8_000_000, transcendentals=8_000_000
        ),
        name="far",
    )(place, near[-1], *args, wk)


def body(
    teacher_queries, teacher_keys, query_projection, key_projection, block_offsets, valid_counts
):
    chips = ("za", "zb", "yh", "x")
    places = chips + ("core",)
    count = lax.axis_size(places)
    core = lax.axis_index("core")
    place = jnp.stack([core, lax.axis_index(chips)]).astype(jnp.int32)

    columns = lambda x, which: lax.dynamic_slice_in_dim(x, which * K_COLS, K_COLS, 1)
    k_prev = lax.ppermute(teacher_keys, places, [(i, i + 2) for i in range(count - 2)])
    k_other = swap(teacher_keys, "core")
    q_other = swap(teacher_queries, "core")
    tables = (block_offsets, valid_counts, swap(block_offsets, "core"), swap(valid_counts, "core"))
    k_far = lax.ppermute(
        jnp.where(core == 1, columns(teacher_keys, core), columns(k_other, core)),
        places, [(i, i + 4) for i in range(count - 4)],
    )
    near = near_call(
        place, tables, teacher_queries, q_other, teacher_keys, k_other,
        query_projection, key_projection,
    )
    k_prev_other = swap(cut_prev(place, k_prev, near[-1]), "core")
    parts = far_call(place, k_prev, k_prev_other, k_far, near, key_projection)

    group = ("zb", "yh", "x")
    got = lax.all_to_all(parts, group, 0, 0)
    got = pl.pallas_call(sum_kernel, out_shape=shaped((SUM_ROWS + 8, HEAD_DIM)), name="sum")(got)
    one, two, three = (
        lax.ppermute(got, "za", [(i, i ^ step) for i in range(4)]) for step in (1, 2, 3)
    )
    coded, total = pack(got, one, two, three)
    total = total + swap(total, "head")
    total = total + swap(total, "core")
    mine = lax.all_to_all(coded, group, 0, 0)
    query_gradient, key_gradient = unpack(place, mine, swap(mine, "core"))
    return (
        query_gradient.reshape(2 * HEADS_HERE, HEAD_DIM, HEAD_DIM),
        key_gradient.reshape(2 * KV_HERE, POOL, HEAD_DIM),
        total[0, 0] / (1024 * HEADS),
    )


def solution(mesh):
    split = Mesh(mesh.devices.reshape(4, 2, 2, 4, 2, 2), ("za", "zb", "yh", "x", "core", "head"))
    ctx = ("za", "zb", "yh", "x", "core")
    placed = (
        P(ctx, "head"),
        P(ctx, "head"),
        P("head", None, None),
        P("head", None, None),
        P(ctx, None),
        P(ctx),
    )
    return jax.shard_map(
        body,
        mesh=split,
        in_specs=placed,
        out_specs=(P("head", None, None), P("head", None, None), P()),
        check_vma=False,
    )
```

```python
import math

import jax
import jax.numpy as jnp
from jax import lax
from jax.experimental import pallas as pl
from jax.experimental.pallas import tpu as pltpu
from jax.sharding import Mesh, PartitionSpec as P

HEADS = 32
KV_HEADS = 8
HEAD_DIM = 128
BLOCK = 64
CAND = 24
REACH = 4

ROWS = 8
SPAN = 24
CHIP_BLOCKS = 2 * ROWS
PADDED = 48
KV_HERE = 2
GROUP = HEADS // KV_HEADS
HEADS_HERE = KV_HERE * GROUP
Q_COLS = HEADS_HERE * HEAD_DIM
K_COLS = KV_HERE * HEAD_DIM
POOL = 3 * HEAD_DIM
WIDTH = GROUP * BLOCK
DUMMY = 31
SLOT_ROWS = 32
LANES = GROUP * CHIP_BLOCKS
SHARES = 16
KEY_ROWS = KV_HERE * POOL // SHARES
HALF_HEAD = HEAD_DIM // 2
PART_ROWS = CHIP_BLOCKS + ROWS + KEY_ROWS + 8
SUM_ROWS = HALF_HEAD + KEY_ROWS
VMEM_BYTES = 40 * 1024 * 1024
NEAR_UNROLL = 4
FAR_UNROLL = 8
TILE = 16
STEP_SHARES = 16
LEVELS = 32760.0
WORK_SIZE = CHIP_BLOCKS * CAND // 4 + 16
LOW = -1e30
EXP_SCALE = math.log2(math.e) / math.sqrt(HEAD_DIM)


def dot_f32(a, b, dims):
    def one(x, y):
        return lax.dot_general(x, y, (dims, ((), ())), preferred_element_type=jnp.float32)

    a_top = a.astype(jnp.bfloat16)
    b_top = b.astype(jnp.bfloat16)
    a_low = (a - a_top.astype(jnp.float32)).astype(jnp.bfloat16)
    b_low = (b - b_top.astype(jnp.float32)).astype(jnp.bfloat16)
    return one(a_top, b_top) + (one(a_top, b_low) + one(a_low, b_top))


def pool_keys(tile):
    wide = tile.astype(jnp.float32).reshape(ROWS, BLOCK, K_COLS)
    top = jnp.max(wide, axis=1)
    low = jnp.min(wide, axis=1)
    mean = jnp.sum(wide, axis=1) * (1.0 / BLOCK)
    return [
        jnp.concatenate(
            [v[:, g * HEAD_DIM:(g + 1) * HEAD_DIM] for v in (top, low, mean)], axis=1
        )
        for g in range(KV_HERE)
    ]


def slot_table(offsets_ref, counts_ref):
    table = jnp.concatenate(
        [offsets_ref[...], jnp.zeros((ROWS, HEAD_DIM - CAND), jnp.int32)], axis=1
    )
    row = lax.broadcasted_iota(jnp.int32, (ROWS, HEAD_DIM), 0)
    lane = lax.broadcasted_iota(jnp.int32, (ROWS, HEAD_DIM), 1)
    for j in range(ROWS):
        table = jnp.where((lane == CAND) & (row == j), counts_ref[j], table)
    return table.astype(jnp.float32)


def make_lists(core, chip, table):
    shape = (CHIP_BLOCKS, HEAD_DIM)
    lane = lax.broadcasted_iota(jnp.int32, shape, 1)
    row = lax.broadcasted_iota(jnp.int32, shape, 0)
    block = position(core, row)
    offset = table.astype(jnp.int32)
    count = jnp.sum(jnp.where(lane == CAND, table, 0.0), axis=1, keepdims=True).astype(jnp.int32)
    usable = (lane < count) & (offset <= chip * CHIP_BLOCKS + block)
    near = jnp.where(usable & (offset <= block), 1.0, 0.0)
    far = jnp.where(usable & (offset > block), 1.0, 0.0)
    picked = jnp.concatenate([near, far], axis=0)
    before = jnp.where(
        lax.broadcasted_iota(jnp.int32, (HEAD_DIM, HEAD_DIM), 0)
        < lax.broadcasted_iota(jnp.int32, (HEAD_DIM, HEAD_DIM), 1), 1.0, 0.0,
    ).astype(jnp.bfloat16)
    rank = jnp.dot(picked.astype(jnp.bfloat16), before, preferred_element_type=jnp.float32)
    rank = jnp.where(picked > 0.0, rank, -1.0)
    value = (SPAN - DUMMY) - jnp.concatenate([table, table], axis=0)
    lane = jnp.concatenate([lane, lane], axis=0)
    packed = jnp.where(lane == CAND, jnp.sum(picked, axis=1, keepdims=True), float(DUMMY))
    for slot in range(CAND):
        here = jnp.sum(jnp.where(rank == slot, value, 0.0), axis=1, keepdims=True)
        packed = jnp.where(lane == slot, here + DUMMY, packed)
    return packed.astype(jnp.int32)


def make_work(list_ref, work, unroll):
    def per_block(s, total):
        count = list_ref[s, CAND]
        for i in range(CAND // 4):
            work[total] = s * CAND + i * 4
            total += jnp.where(i * 4 < count, 1, 0)
        return total

    filled = lax.fori_loop(0, CHIP_BLOCKS, per_block, jnp.int32(0))
    spare = work[jnp.maximum(filled - 1, 0)]
    for extra in range(unroll - 1):
        work[filled + extra] = spare
    return filled


def position(core, s):
    return jnp.where(s < ROWS, ROWS * core + s, ROWS * (1 - core) + s - ROWS)


def slot_loop(filled, work, unroll, list_ref, tile_start, keys, queries, slot_max, slot_sum, diagonal):
    lane = lax.broadcasted_iota(jnp.int32, (BLOCK, WIDTH), 1) % BLOCK
    key_row = lax.broadcasted_iota(jnp.int32, (BLOCK, WIDTH), 0)

    @pl.loop(0, (filled + unroll - 1) // unroll)
    def _(step):
        found = []
        for e in range(unroll):
            first = work[step * unroll + e]
            s = first // CAND
            rows = [list_ref[s, first - s * CAND + i] for i in range(4)]
            starts = [pl.multiple_of(tile_start(s, row) * BLOCK, BLOCK) for row in rows]
            if diagonal:
                keep = key_row <= lane + jnp.where(first == s * CAND, 0, BLOCK)
            for g in range(KV_HERE):
                tiles = [
                    keys[pl.ds(start, BLOCK), g * HEAD_DIM:(g + 1) * HEAD_DIM] for start in starts
                ]
                scores = lax.dot_general(
                    jnp.concatenate(tiles, axis=0), queries[s * KV_HERE + g],
                    (((1,), (1,)), ((), ())), preferred_element_type=jnp.float32,
                )
                for i, row in enumerate(rows):
                    part = scores[i * BLOCK:(i + 1) * BLOCK, :]
                    if diagonal and i == 0:
                        part = jnp.where(keep, part, LOW)
                    top = jnp.max(part, axis=0, keepdims=True)
                    total = jnp.sum(
                        jnp.exp2((part - top) * EXP_SCALE), axis=0, keepdims=True
                    )
                    found.append((s * KV_HERE + g, row, top, total))
        for index, row, top, total in found:
            slot_max[index, pl.ds(row, 1), :] = top
            slot_sum[index, pl.ds(row, 1), :] = total


def near_kernel(
    place_ref, offsets_own_ref, counts_own_ref, offsets_other_ref, counts_other_ref,
    q_own_hbm, q_other_hbm, k_own_hbm, k_other_hbm, wq_hbm, wk_hbm,
    queries, slot_max, slot_sum, pooled_query, gate_query, pooled_key, gate_key,
    far_list,
    keys, near_vector, near_list, near_work, q_own_ref, q_other_ref, k_own_ref, k_other_ref,
    wq_ref, wk_ref, sems,
):
    core_ref = place_ref
    core = core_ref[0]
    half = ROWS * BLOCK
    q_copy = pltpu.make_async_copy(
        q_own_hbm.at[:, pl.ds(pl.multiple_of(core * Q_COLS, Q_COLS), Q_COLS)], q_own_ref, sems.at[1]
    )
    wq_copy = pltpu.make_async_copy(
        wq_hbm.at[pl.ds(core * HEADS_HERE, HEADS_HERE)], wq_ref, sems.at[2]
    )
    wk_copy = pltpu.make_async_copy(
        wk_hbm.at[pl.ds(core * KV_HERE, KV_HERE)], wk_ref, sems.at[3]
    )
    q_cols = pl.ds(pl.multiple_of(core * Q_COLS, Q_COLS), Q_COLS)
    k_cols = pl.ds(pl.multiple_of(core * K_COLS, K_COLS), K_COLS)
    q_other_copy = pltpu.make_async_copy(q_other_hbm.at[:, q_cols], q_other_ref, sems.at[4])
    k_own_copy = pltpu.make_async_copy(k_own_hbm.at[:, k_cols], k_own_ref, sems.at[5])
    k_other_copy = pltpu.make_async_copy(k_other_hbm.at[:, k_cols], k_other_ref, sems.at[6])
    k_own_copy.start()
    k_other_copy.start()
    q_other_copy.start()
    q_copy.start()
    wq_copy.start()
    wk_copy.start()
    lists = make_lists(
        core, place_ref[1],
        jnp.concatenate(
            [
                slot_table(offsets_own_ref, counts_own_ref),
                slot_table(offsets_other_ref, counts_other_ref),
            ],
            axis=0,
        ),
    )
    far_list[...] = lists[CHIP_BLOCKS:]
    near_vector[...] = lists[0:CHIP_BLOCKS]
    list_copy = pltpu.make_async_copy(near_vector, near_list, sems.at[0])
    list_copy.start()
    k_own_copy.wait()
    k_other_copy.wait()
    for source, ref in ((core, k_own_ref), (1 - core, k_other_ref)):
        tile = ref[...]
        keys[pl.ds(pl.multiple_of(source * half, half), half), :] = tile
        for g, pooled in enumerate(pool_keys(tile)):
            pooled_key[g, pl.ds(pl.multiple_of(source * ROWS, ROWS), ROWS), :] = pooled

    def prepare(s, q_ref, at):
        for g in range(KV_HERE):
            for r in range(GROUP):
                head = g * GROUP + r
                tile = q_ref[pl.ds(at, BLOCK), head * HEAD_DIM:(head + 1) * HEAD_DIM]
                queries[s * KV_HERE + g, r * BLOCK:(r + 1) * BLOCK, :] = tile
                pooled_query[g, pl.ds(r * CHIP_BLOCKS + s, 1), :] = jnp.sum(
                    tile.astype(jnp.float32), axis=0, keepdims=True
                ) * (1.0 / BLOCK)

    q_other_copy.wait()
    for source in (1, 0):
        q_ref = (q_own_ref, q_other_ref)[source]
        if source == 0:
            q_copy.wait()

        @pl.loop(0, ROWS)
        def _(j):
            prepare(source * ROWS + j, q_ref, pl.multiple_of(j * BLOCK, BLOCK))

    slot_max[...] = jnp.full_like(slot_max, LOW)
    slot_sum[...] = jnp.zeros_like(slot_sum)
    list_copy.wait()
    filled = make_work(near_list, near_work, NEAR_UNROLL)
    slot_loop(
        filled, near_work, NEAR_UNROLL, near_list,
        lambda s, row: position(core, s) + jnp.minimum(row, SPAN) - SPAN,
        keys, queries, slot_max, slot_sum, True,
    )
    wq_copy.wait()
    wk_copy.wait()
    for g in range(KV_HERE):
        gate_key[g] = dot_f32(pooled_key[g], wk_ref[g], ((1,), (0,)))
        for r in range(GROUP):
            picked = slice(r * CHIP_BLOCKS, (r + 1) * CHIP_BLOCKS)
            gate_query[g, picked, :] = dot_f32(
                pooled_query[g, picked, :], wq_ref[g * GROUP + r], ((1,), (0,))
            )


def far_kernel(
    core_ref, far_list,
    k_prev_hbm, k_prev_other_ref, k_far_ref, queries,
    max_ref, sum_ref, pooled_query, gate_query, near_key, near_gate_key, wk_ref,
    out_ref,
    keys, slot_max, slot_sum, pooled_key, shares, hits, far_work,
    k_prev_own_ref, sems,
):
    core = core_ref[0]
    half = ROWS * BLOCK
    k_copy = pltpu.make_async_copy(
        k_prev_hbm.at[:, pl.ds(pl.multiple_of(core * K_COLS, K_COLS), K_COLS)],
        k_prev_own_ref, sems.at[0],
    )
    k_copy.start()
    for place, ref in ((0, k_far_ref), (2 - core, k_prev_other_ref), (1 + core, k_prev_own_ref)):
        if ref is k_prev_own_ref:
            k_copy.wait()
        tile = ref[...]
        at = place * half if isinstance(place, int) else pl.multiple_of(place * half, half)
        row = place * ROWS if isinstance(place, int) else pl.multiple_of(place * ROWS, ROWS)
        keys[pl.ds(at, half), :] = tile
        for g, pooled in enumerate(pool_keys(tile)):
            pooled_key[g, pl.ds(row, ROWS), :] = pooled
    for g in range(KV_HERE):
        pooled_key[g, SPAN:SPAN + CHIP_BLOCKS, :] = near_key[g]
    slot_max[...] = max_ref[...]
    slot_sum[...] = sum_ref[...]
    shares[...] = jnp.zeros_like(shares)
    hits[...] = jnp.zeros_like(hits)
    filled = make_work(far_list, far_work, FAR_UNROLL)
    slot_loop(
        filled, far_work, FAR_UNROLL, far_list,
        lambda s, row: jnp.where(row <= SPAN, position(core, s) + row, 0),
        keys, queries, slot_max, slot_sum, False,
    )

    live = lax.broadcasted_iota(jnp.int32, (SLOT_ROWS, WIDTH), 0) <= SPAN
    spread = jnp.where(
        lax.broadcasted_iota(jnp.int32, (WIDTH, LANES), 0) // BLOCK
        == lax.broadcasted_iota(jnp.int32, (WIDTH, LANES), 1) // CHIP_BLOCKS,
        1.0 / BLOCK, 0.0,
    ).astype(jnp.bfloat16)
    lane_block = lax.broadcasted_iota(jnp.int32, (SLOT_ROWS, LANES), 1) % CHIP_BLOCKS

    @pl.loop(0, CHIP_BLOCKS // 4)
    def _(step):
        found = []
        for e in range(4):
            s = step * 4 + e
            for g in range(KV_HERE):
                tops = jnp.where(live, slot_max[s * KV_HERE + g], LOW)
                top = jnp.max(tops, axis=0, keepdims=True)
                weight = jnp.where(
                    live, slot_sum[s * KV_HERE + g] * jnp.exp2((tops - top) * EXP_SCALE), 0.0
                )
                share = weight / jnp.sum(weight, axis=0, keepdims=True)
                coarse = share.astype(jnp.bfloat16)
                fine = (share - coarse.astype(jnp.float32)).astype(jnp.bfloat16)
                mean = (
                    jnp.dot(coarse, spread, preferred_element_type=jnp.float32)
                    + jnp.dot(fine, spread, preferred_element_type=jnp.float32)
                )
                found.append((shares.at[g], position(core, s), jnp.where(lane_block == s, mean, 0.0)))
                if g == 0:
                    filled = jnp.where(tops > 0.5 * LOW, 1.0, 0.0).astype(jnp.bfloat16)
                    hit = jnp.dot(filled, spread, preferred_element_type=jnp.float32)
                    found.append((hits, position(core, s), jnp.where(lane_block == s, hit, 0.0)))
        for table, block, mine in found:
            table[pl.ds(block, SLOT_ROWS), :] += mine

    scale = 1.0 / math.sqrt(HEAD_DIM)
    window = SPAN + CHIP_BLOCKS
    usable = hits[0:window, :] > 0.5
    divergence = jnp.zeros((1, LANES), jnp.float32)
    key_base = CHIP_BLOCKS + ROWS
    for g in range(KV_HERE):
        far_gate_key = dot_f32(pooled_key[g, 0:SPAN, :], wk_ref[g], ((1,), (0,)))
        gate_key = jnp.concatenate([far_gate_key, near_gate_key[g]], axis=0)
        logits = dot_f32(gate_key, gate_query[g], ((1,), (1,))) * scale
        logits = jnp.where(usable, logits, LOW)
        top = jnp.max(logits, axis=0, keepdims=True)
        weight = jnp.where(usable, jnp.exp(logits - top), 0.0)
        mass = jnp.sum(weight, axis=0, keepdims=True)
        log_gate = jnp.where(usable, logits - top - jnp.log(mass), 0.0)
        target = shares[g, 0:window, :]
        log_target = jnp.log(jnp.where(target > 0.0, target, 1.0))
        terms = jnp.where(usable, target * (log_target - log_gate), 0.0)
        divergence += jnp.sum(terms, axis=0, keepdims=True)
        target = jnp.where(usable, target, 0.0)
        slope = (weight / mass) * jnp.sum(target, axis=0, keepdims=True) - target
        slope = slope * (scale / 32.0)
        d_query = dot_f32(slope, gate_key, ((0,), (0,)))
        d_key = dot_f32(slope, gate_query[g], ((1,), (0,)))
        for r in range(GROUP):
            at = r * CHIP_BLOCKS
            pooled = pooled_query[g, at:at + CHIP_BLOCKS, :]
            for part in range(2):
                share = (g * GROUP + r) * 2 + part
                cols = slice(part * HALF_HEAD, (part + 1) * HALF_HEAD)
                out_ref[share, 0:CHIP_BLOCKS, :] = d_query[at:at + CHIP_BLOCKS, :]
                out_ref[share, CHIP_BLOCKS:key_base, :] = jnp.concatenate(
                    [pooled[0:ROWS, cols], pooled[ROWS:CHIP_BLOCKS, cols]], axis=1
                )
        key_part = dot_f32(pooled_key[g], d_key, ((0,), (0,)))
        for i in range(SHARES // KV_HERE):
            out_ref[g * (SHARES // KV_HERE) + i, key_base:key_base + KEY_ROWS, :] = (
                key_part[i * KEY_ROWS:(i + 1) * KEY_ROWS, :]
            )
    total = jnp.sum(divergence)
    for i in range(SHARES):
        out_ref[i, PART_ROWS - 8:PART_ROWS, :] = jnp.full((8, HEAD_DIM), total, jnp.float32)


def sum_kernel(parts_ref, out_ref):
    parts = parts_ref[...]
    pooled = parts[:, CHIP_BLOCKS:CHIP_BLOCKS + ROWS, :].reshape(SHARES * ROWS, HEAD_DIM)
    early = parts[:, 0:ROWS, :].reshape(SHARES * ROWS, HEAD_DIM)
    late = parts[:, ROWS:CHIP_BLOCKS, :].reshape(SHARES * ROWS, HEAD_DIM)
    out_ref[0:HALF_HEAD, :] = (
        dot_f32(pooled[:, :HALF_HEAD], early, ((0,), (0,)))
        + dot_f32(pooled[:, HALF_HEAD:], late, ((0,), (0,)))
    )
    out_ref[HALF_HEAD:, :] = jnp.sum(parts[:, CHIP_BLOCKS + ROWS:, :], axis=0)


def pack_kernel(got_ref, out_ref, total_ref):
    got = got_ref[...]
    total_ref[...] = got[SUM_ROWS:, :]
    coded = []
    powers = jnp.zeros((TILE, HEAD_DIM), jnp.float32)
    row = lax.broadcasted_iota(jnp.int32, (TILE, HEAD_DIM), 0)
    for tile in range(SUM_ROWS // TILE):
        value = got[tile * TILE:(tile + 1) * TILE, :]
        top = jnp.max(jnp.abs(value), axis=0, keepdims=True)
        power = jnp.clip(jnp.ceil(jnp.log2(jnp.maximum(top, 1e-35))), -110.0, 110.0)
        level = jnp.clip(jnp.round(value * jnp.exp2(-power) * LEVELS), -32767.0, 32767.0)
        coded.append(level.astype(jnp.int32).astype(jnp.int16))
        powers = jnp.where(row == tile, power, powers)
    coded.append(powers.astype(jnp.int32).astype(jnp.int16))
    coded = jnp.concatenate(coded, axis=0)
    for i in range(SHARES):
        out_ref[i] = coded


def unpack_kernel(place_ref, mine_ref, other_ref, query_ref, key_ref):
    core = place_ref[0]
    for source, ref in ((core, mine_ref), (1 - core, other_ref)):
        for share in range(STEP_SHARES):
            powers = ref[share, SUM_ROWS:SUM_ROWS + TILE, :].astype(jnp.int32).astype(jnp.float32)
            scale = jnp.exp2(powers[0:8, :]) * (1.0 / LEVELS)
            for tile in range(SUM_ROWS // TILE):
                coded = ref[share, tile * TILE:(tile + 1) * TILE, :]
                value = coded.astype(jnp.int32).astype(jnp.float32) * scale[tile:tile + 1, :]
                if tile < HALF_HEAD // TILE:
                    query_ref[source, pl.ds(share * HALF_HEAD + tile * TILE, TILE), :] = value
                else:
                    at = share * KEY_ROWS + tile * TILE - HALF_HEAD
                    key_ref[source, pl.ds(at, TILE), :] = value


def pack(*parts):
    return pl.pallas_call(
        pack_kernel,
        out_shape=[
            shaped((SHARES, SUM_ROWS + TILE, HEAD_DIM), jnp.int16), shaped((8, HEAD_DIM)),
        ],
        name="pack",
    )(*parts)


def unpack(place, mine, other):
    rows = HALF_HEAD, KEY_ROWS
    return pl.pallas_call(
        unpack_kernel,
        grid_spec=pltpu.PrefetchScalarGridSpec(
            num_scalar_prefetch=1,
            grid=(SHARES // STEP_SHARES,),
            in_specs=[
                pl.BlockSpec((STEP_SHARES, SUM_ROWS + TILE, HEAD_DIM), lambda i, c: (i, 0, 0))
            ] * 2,
            out_specs=[
                pl.BlockSpec((2, STEP_SHARES * n, HEAD_DIM), lambda i, c: (0, i, 0)) for n in rows
            ],
        ),
        out_shape=[shaped((2, SHARES * n, HEAD_DIM)) for n in rows],
        name="unpack",
    )(place, mine, other)


def swap(x, axis):
    return lax.ppermute(x, axis, [(0, 1), (1, 0)])


def whole(*shape):
    return pl.BlockSpec(shape, lambda i, *_: (0,) * len(shape))


def shaped(shape, dtype=jnp.float32):
    return jax.ShapeDtypeStruct(shape, dtype)


def smem():
    return pl.BlockSpec(memory_space=pltpu.SMEM)


def cut_prev_kernel(place_ref, keys_hbm, after_ref, give_ref, sems):
    cols = pl.ds(pl.multiple_of((1 - place_ref[0]) * K_COLS, K_COLS), K_COLS)
    give = pltpu.make_async_copy(keys_hbm.at[:, cols], give_ref, sems.at[0])
    give.start()
    give.wait()


def cut_prev(place, keys, after):
    half = ROWS * BLOCK
    return pl.pallas_call(
        cut_prev_kernel,
        grid_spec=pltpu.PrefetchScalarGridSpec(
            num_scalar_prefetch=1,
            grid=(1,),
            in_specs=[
                pl.BlockSpec(memory_space=pltpu.HBM),
                pl.BlockSpec(memory_space=pl.ANY),
            ],
            out_specs=whole(half, K_COLS),
            scratch_shapes=[pltpu.SemaphoreType.DMA((1,))],
        ),
        out_shape=shaped((half, K_COLS), jnp.bfloat16),
        compiler_params=pltpu.CompilerParams(vmem_limit_bytes=4 * 1024 * 1024),
        name="cut_prev",
    )(place, keys, after)


def near_call(place, tables, q_own, q_other, k_mine, k_other, wq, wk):
    half = ROWS * BLOCK
    outs = [
        shaped((CHIP_BLOCKS * KV_HERE, WIDTH, HEAD_DIM), jnp.bfloat16),
        shaped((CHIP_BLOCKS * KV_HERE, SLOT_ROWS, WIDTH)),
        shaped((CHIP_BLOCKS * KV_HERE, SLOT_ROWS, WIDTH)),
        shaped((KV_HERE, LANES, HEAD_DIM)),
        shaped((KV_HERE, LANES, HEAD_DIM)),
        shaped((KV_HERE, CHIP_BLOCKS, POOL)),
        shaped((KV_HERE, CHIP_BLOCKS, HEAD_DIM)),
        shaped((CHIP_BLOCKS, HEAD_DIM), jnp.int32),
    ]
    return pl.pallas_call(
        near_kernel,
        grid_spec=pltpu.PrefetchScalarGridSpec(
            num_scalar_prefetch=1,
            grid=(1,),
            in_specs=[whole(ROWS, CAND), smem()] * 2 + [pl.BlockSpec(memory_space=pltpu.HBM)] * 6,
            out_specs=[whole(*o.shape) for o in outs],
            scratch_shapes=[
                pltpu.VMEM((CHIP_BLOCKS * BLOCK, K_COLS), jnp.bfloat16),
                pltpu.VMEM((CHIP_BLOCKS, HEAD_DIM), jnp.int32),
                pltpu.SMEM((CHIP_BLOCKS, HEAD_DIM), jnp.int32),
                pltpu.SMEM((WORK_SIZE,), jnp.int32),
                pltpu.VMEM((half, Q_COLS), jnp.bfloat16),
                pltpu.VMEM((half, Q_COLS), jnp.bfloat16),
                pltpu.VMEM((half, K_COLS), jnp.bfloat16),
                pltpu.VMEM((half, K_COLS), jnp.bfloat16),
                pltpu.VMEM((HEADS_HERE, HEAD_DIM, HEAD_DIM), jnp.float32),
                pltpu.VMEM((KV_HERE, POOL, HEAD_DIM), jnp.float32),
                pltpu.SemaphoreType.DMA((7,)),
            ],
        ),
        out_shape=outs,
        compiler_params=pltpu.CompilerParams(vmem_limit_bytes=VMEM_BYTES),
        cost_estimate=pl.CostEstimate(
            flops=2_000_000_000, bytes_accessed=8_000_000, transcendentals=8_000_000
        ),
        name="near",
    )(place, *tables, q_own, q_other, k_mine, k_other, wq, wk)


def far_call(place, k_prev_own, k_prev_other, k_far, near, wk):
    half = ROWS * BLOCK
    args = (k_prev_own, k_prev_other, k_far, *near[:-1])
    return pl.pallas_call(
        far_kernel,
        grid_spec=pltpu.PrefetchScalarGridSpec(
            num_scalar_prefetch=1,
            grid=(1,),
            in_specs=[smem(), pl.BlockSpec(memory_space=pltpu.HBM)]
            + [whole(*a.shape) for a in args[1:]] + [
                pl.BlockSpec((KV_HERE, POOL, HEAD_DIM), lambda i, c: (c[0], 0, 0)),
            ],
            out_specs=whole(SHARES, PART_ROWS, HEAD_DIM),
            scratch_shapes=[
                pltpu.VMEM((SPAN * BLOCK, K_COLS), jnp.bfloat16),
                pltpu.VMEM((CHIP_BLOCKS * KV_HERE, SLOT_ROWS, WIDTH), jnp.float32),
                pltpu.VMEM((CHIP_BLOCKS * KV_HERE, SLOT_ROWS, WIDTH), jnp.float32),
                pltpu.VMEM((KV_HERE, SPAN + CHIP_BLOCKS, POOL), jnp.float32),
                pltpu.VMEM((KV_HERE, PADDED, LANES), jnp.float32),
                pltpu.VMEM((PADDED, LANES), jnp.float32),
                pltpu.SMEM((WORK_SIZE,), jnp.int32),
                pltpu.VMEM((half, K_COLS), jnp.bfloat16),
                pltpu.SemaphoreType.DMA((1,)),
            ],
        ),
        out_shape=shaped((SHARES, PART_ROWS, HEAD_DIM)),
        compiler_params=pltpu.CompilerParams(vmem_limit_bytes=VMEM_BYTES),
        cost_estimate=pl.CostEstimate(
            flops=2_000_000_000, bytes_accessed=8_000_000, transcendentals=8_000_000
        ),
        name="far",
    )(place, near[-1], *args, wk)


def body(
    teacher_queries, teacher_keys, query_projection, key_projection, block_offsets, valid_counts
):
    chips = ("za", "zb", "yh", "x")
    places = chips + ("core",)
    count = lax.axis_size(places)
    core = lax.axis_index("core")
    place = jnp.stack([core, lax.axis_index(chips)]).astype(jnp.int32)

    columns = lambda x, which: lax.dynamic_slice_in_dim(x, which * K_COLS, K_COLS, 1)
    k_prev = lax.ppermute(teacher_keys, places, [(i, i + 2) for i in range(count - 2)])
    k_other = swap(teacher_keys, "core")
    q_other = swap(teacher_queries, "core")
    tables = (block_offsets, valid_counts, swap(block_offsets, "core"), swap(valid_counts, "core"))
    k_far = lax.ppermute(
        jnp.where(core == 1, columns(teacher_keys, core), columns(k_other, core)),
        places, [(i, i + 4) for i in range(count - 4)],
    )
    near = near_call(
        place, tables, teacher_queries, q_other, teacher_keys, k_other,
        query_projection, key_projection,
    )
    k_prev_other = swap(cut_prev(place, k_prev, near[-1]), "core")
    parts = far_call(place, k_prev, k_prev_other, k_far, near, key_projection)

    group = ("zb", "yh", "x")
    got = lax.all_to_all(parts, group, 0, 0)
    got = pl.pallas_call(sum_kernel, out_shape=shaped((SUM_ROWS + 8, HEAD_DIM)), name="sum")(got)
    one, two, three = (
        lax.ppermute(got, "za", [(i, i ^ step) for i in range(4)]) for step in (1, 2, 3)
    )
    coded, total = pack((got + one) + (two + three))
    total = total + swap(total, "head")
    total = total + swap(total, "core")
    mine = lax.all_to_all(coded, group, 0, 0)
    query_gradient, key_gradient = unpack(place, mine, swap(mine, "core"))
    return (
        query_gradient.reshape(2 * HEADS_HERE, HEAD_DIM, HEAD_DIM),
        key_gradient.reshape(2 * KV_HERE, POOL, HEAD_DIM),
        total[0, 0] / (1024 * HEADS),
    )


def solution(mesh):
    split = Mesh(mesh.devices.reshape(4, 2, 2, 4, 2, 2), ("za", "zb", "yh", "x", "core", "head"))
    ctx = ("za", "zb", "yh", "x", "core")
    placed = (
        P(ctx, "head"),
        P(ctx, "head"),
        P("head", None, None),
        P("head", None, None),
        P(ctx, None),
        P(ctx),
    )
    return jax.shard_map(
        body,
        mesh=split,
        in_specs=placed,
        out_specs=(P("head", None, None), P("head", None, None), P()),
        check_vma=False,
    )
```

```python
import math

import jax
import jax.numpy as jnp
from jax import lax
from jax.experimental import pallas as pl
from jax.experimental.pallas import tpu as pltpu
from jax.sharding import Mesh, PartitionSpec as P

HEADS = 32
KV_HEADS = 8
HEAD_DIM = 128
BLOCK = 64
CAND = 24
REACH = 4

ROWS = 8
SPAN = 24
CHIP_BLOCKS = 2 * ROWS
PADDED = 48
KV_HERE = 2
GROUP = HEADS // KV_HEADS
HEADS_HERE = KV_HERE * GROUP
Q_COLS = HEADS_HERE * HEAD_DIM
K_COLS = KV_HERE * HEAD_DIM
POOL = 3 * HEAD_DIM
WIDTH = GROUP * BLOCK
DUMMY = 31
SLOT_ROWS = 32
LANES = GROUP * CHIP_BLOCKS
SHARES = 16
KEY_ROWS = KV_HERE * POOL // SHARES
HALF_HEAD = HEAD_DIM // 2
PART_ROWS = CHIP_BLOCKS + ROWS + KEY_ROWS + 8
SUM_ROWS = HALF_HEAD + KEY_ROWS
VMEM_BYTES = 40 * 1024 * 1024
NEAR_UNROLL = 4
FAR_UNROLL = 6
TILE = 16
STEP_SHARES = 16
LEVELS = 32760.0
WORK_SIZE = CHIP_BLOCKS * CAND // 4 + 16
LOW = -1e30
EXP_SCALE = math.log2(math.e) / math.sqrt(HEAD_DIM)


def dot_f32(a, b, dims):
    def one(x, y):
        return lax.dot_general(x, y, (dims, ((), ())), preferred_element_type=jnp.float32)

    a_top = a.astype(jnp.bfloat16)
    b_top = b.astype(jnp.bfloat16)
    a_low = (a - a_top.astype(jnp.float32)).astype(jnp.bfloat16)
    b_low = (b - b_top.astype(jnp.float32)).astype(jnp.bfloat16)
    return one(a_top, b_top) + (one(a_top, b_low) + one(a_low, b_top))


def pool_keys(tile):
    wide = tile.astype(jnp.float32).reshape(ROWS, BLOCK, K_COLS)
    top = jnp.max(wide, axis=1)
    low = jnp.min(wide, axis=1)
    mean = jnp.sum(wide, axis=1) * (1.0 / BLOCK)
    return [
        jnp.concatenate(
            [v[:, g * HEAD_DIM:(g + 1) * HEAD_DIM] for v in (top, low, mean)], axis=1
        )
        for g in range(KV_HERE)
    ]


def slot_table(offsets_ref, counts_ref):
    table = jnp.concatenate(
        [offsets_ref[...], jnp.zeros((ROWS, HEAD_DIM - CAND), jnp.int32)], axis=1
    )
    row = lax.broadcasted_iota(jnp.int32, (ROWS, HEAD_DIM), 0)
    lane = lax.broadcasted_iota(jnp.int32, (ROWS, HEAD_DIM), 1)
    for j in range(ROWS):
        table = jnp.where((lane == CAND) & (row == j), counts_ref[j], table)
    return table.astype(jnp.float32)


def make_lists(core, chip, table):
    shape = (CHIP_BLOCKS, HEAD_DIM)
    lane = lax.broadcasted_iota(jnp.int32, shape, 1)
    row = lax.broadcasted_iota(jnp.int32, shape, 0)
    block = position(core, row)
    offset = table.astype(jnp.int32)
    count = jnp.sum(jnp.where(lane == CAND, table, 0.0), axis=1, keepdims=True).astype(jnp.int32)
    usable = (lane < count) & (offset <= chip * CHIP_BLOCKS + block)
    near = jnp.where(usable & (offset <= block), 1.0, 0.0)
    far = jnp.where(usable & (offset > block), 1.0, 0.0)
    picked = jnp.concatenate([near, far], axis=0)
    before = jnp.where(
        lax.broadcasted_iota(jnp.int32, (HEAD_DIM, HEAD_DIM), 0)
        < lax.broadcasted_iota(jnp.int32, (HEAD_DIM, HEAD_DIM), 1), 1.0, 0.0,
    ).astype(jnp.bfloat16)
    rank = jnp.dot(picked.astype(jnp.bfloat16), before, preferred_element_type=jnp.float32)
    rank = jnp.where(picked > 0.0, rank, -1.0)
    value = (SPAN - DUMMY) - jnp.concatenate([table, table], axis=0)
    lane = jnp.concatenate([lane, lane], axis=0)
    packed = jnp.where(lane == CAND, jnp.sum(picked, axis=1, keepdims=True), float(DUMMY))
    for slot in range(CAND):
        here = jnp.sum(jnp.where(rank == slot, value, 0.0), axis=1, keepdims=True)
        packed = jnp.where(lane == slot, here + DUMMY, packed)
    return packed.astype(jnp.int32)


def make_work(list_ref, work, unroll):
    def per_block(s, total):
        count = list_ref[s, CAND]
        for i in range(CAND // 4):
            work[total] = s * CAND + i * 4
            total += jnp.where(i * 4 < count, 1, 0)
        return total

    filled = lax.fori_loop(0, CHIP_BLOCKS, per_block, jnp.int32(0))
    spare = work[jnp.maximum(filled - 1, 0)]
    for extra in range(unroll - 1):
        work[filled + extra] = spare
    return filled


def position(core, s):
    return jnp.where(s < ROWS, ROWS * core + s, ROWS * (1 - core) + s - ROWS)


def slot_loop(filled, work, unroll, list_ref, tile_start, keys, queries, slot_max, slot_sum, diagonal):
    lane = lax.broadcasted_iota(jnp.int32, (BLOCK, WIDTH), 1) % BLOCK
    key_row = lax.broadcasted_iota(jnp.int32, (BLOCK, WIDTH), 0)

    @pl.loop(0, (filled + unroll - 1) // unroll)
    def _(step):
        found = []
        for e in range(unroll):
            first = work[step * unroll + e]
            s = first // CAND
            rows = [list_ref[s, first - s * CAND + i] for i in range(4)]
            starts = [pl.multiple_of(tile_start(s, row) * BLOCK, BLOCK) for row in rows]
            if diagonal:
                keep = key_row <= lane + jnp.where(first == s * CAND, 0, BLOCK)
            for g in range(KV_HERE):
                tiles = [
                    keys[pl.ds(start, BLOCK), g * HEAD_DIM:(g + 1) * HEAD_DIM] for start in starts
                ]
                scores = lax.dot_general(
                    jnp.concatenate(tiles, axis=0), queries[s * KV_HERE + g],
                    (((1,), (1,)), ((), ())), preferred_element_type=jnp.float32,
                )
                for i, row in enumerate(rows):
                    part = scores[i * BLOCK:(i + 1) * BLOCK, :]
                    if diagonal and i == 0:
                        part = jnp.where(keep, part, LOW)
                    top = jnp.max(part, axis=0, keepdims=True)
                    total = jnp.sum(
                        jnp.exp2((part - top) * EXP_SCALE), axis=0, keepdims=True
                    )
                    found.append((s * KV_HERE + g, row, top, total))
        for index, row, top, total in found:
            slot_max[index, pl.ds(row, 1), :] = top
            slot_sum[index, pl.ds(row, 1), :] = total


def near_kernel(
    place_ref, offsets_own_ref, counts_own_ref, offsets_other_ref, counts_other_ref,
    q_own_hbm, q_other_hbm, k_own_hbm, k_other_hbm, wq_hbm, wk_hbm,
    queries, slot_max, slot_sum, pooled_query, gate_query, pooled_key, gate_key,
    far_list,
    keys, near_vector, near_list, near_work, q_own_ref, q_other_ref, k_own_ref, k_other_ref,
    wq_ref, wk_ref, sems,
):
    core_ref = place_ref
    core = core_ref[0]
    half = ROWS * BLOCK
    q_copy = pltpu.make_async_copy(
        q_own_hbm.at[:, pl.ds(pl.multiple_of(core * Q_COLS, Q_COLS), Q_COLS)], q_own_ref, sems.at[1]
    )
    wq_copy = pltpu.make_async_copy(
        wq_hbm.at[pl.ds(core * HEADS_HERE, HEADS_HERE)], wq_ref, sems.at[2]
    )
    wk_copy = pltpu.make_async_copy(
        wk_hbm.at[pl.ds(core * KV_HERE, KV_HERE)], wk_ref, sems.at[3]
    )
    q_cols = pl.ds(pl.multiple_of(core * Q_COLS, Q_COLS), Q_COLS)
    k_cols = pl.ds(pl.multiple_of(core * K_COLS, K_COLS), K_COLS)
    q_other_copy = pltpu.make_async_copy(q_other_hbm.at[:, q_cols], q_other_ref, sems.at[4])
    k_own_copy = pltpu.make_async_copy(k_own_hbm.at[:, k_cols], k_own_ref, sems.at[5])
    k_other_copy = pltpu.make_async_copy(k_other_hbm.at[:, k_cols], k_other_ref, sems.at[6])
    k_own_copy.start()
    k_other_copy.start()
    q_other_copy.start()
    q_copy.start()
    wq_copy.start()
    wk_copy.start()
    lists = make_lists(
        core, place_ref[1],
        jnp.concatenate(
            [
                slot_table(offsets_own_ref, counts_own_ref),
                slot_table(offsets_other_ref, counts_other_ref),
            ],
            axis=0,
        ),
    )
    far_list[...] = lists[CHIP_BLOCKS:]
    near_vector[...] = lists[0:CHIP_BLOCKS]
    list_copy = pltpu.make_async_copy(near_vector, near_list, sems.at[0])
    list_copy.start()
    k_own_copy.wait()
    k_other_copy.wait()
    for source, ref in ((core, k_own_ref), (1 - core, k_other_ref)):
        tile = ref[...]
        keys[pl.ds(pl.multiple_of(source * half, half), half), :] = tile
        for g, pooled in enumerate(pool_keys(tile)):
            pooled_key[g, pl.ds(pl.multiple_of(source * ROWS, ROWS), ROWS), :] = pooled

    def prepare(s, q_ref, at):
        for g in range(KV_HERE):
            for r in range(GROUP):
                head = g * GROUP + r
                tile = q_ref[pl.ds(at, BLOCK), head * HEAD_DIM:(head + 1) * HEAD_DIM]
                queries[s * KV_HERE + g, r * BLOCK:(r + 1) * BLOCK, :] = tile
                pooled_query[g, pl.ds(r * CHIP_BLOCKS + s, 1), :] = jnp.sum(
                    tile.astype(jnp.float32), axis=0, keepdims=True
                ) * (1.0 / BLOCK)

    q_other_copy.wait()
    for source in (1, 0):
        q_ref = (q_own_ref, q_other_ref)[source]
        if source == 0:
            q_copy.wait()

        @pl.loop(0, ROWS)
        def _(j):
            prepare(source * ROWS + j, q_ref, pl.multiple_of(j * BLOCK, BLOCK))

    slot_max[...] = jnp.full_like(slot_max, LOW)
    slot_sum[...] = jnp.zeros_like(slot_sum)
    list_copy.wait()
    filled = make_work(near_list, near_work, NEAR_UNROLL)
    slot_loop(
        filled, near_work, NEAR_UNROLL, near_list,
        lambda s, row: position(core, s) + jnp.minimum(row, SPAN) - SPAN,
        keys, queries, slot_max, slot_sum, True,
    )
    wq_copy.wait()
    wk_copy.wait()
    for g in range(KV_HERE):
        gate_key[g] = dot_f32(pooled_key[g], wk_ref[g], ((1,), (0,)))
        for r in range(GROUP):
            picked = slice(r * CHIP_BLOCKS, (r + 1) * CHIP_BLOCKS)
            gate_query[g, picked, :] = dot_f32(
                pooled_query[g, picked, :], wq_ref[g * GROUP + r], ((1,), (0,))
            )


def far_kernel(
    core_ref, far_list,
    k_prev_hbm, k_prev_other_ref, k_far_ref, queries,
    max_ref, sum_ref, pooled_query, gate_query, near_key, near_gate_key, wk_ref,
    out_ref,
    keys, slot_max, slot_sum, pooled_key, shares, hits, far_work,
    k_prev_own_ref, sems,
):
    core = core_ref[0]
    half = ROWS * BLOCK
    k_copy = pltpu.make_async_copy(
        k_prev_hbm.at[:, pl.ds(pl.multiple_of(core * K_COLS, K_COLS), K_COLS)],
        k_prev_own_ref, sems.at[0],
    )
    k_copy.start()
    for place, ref in ((0, k_far_ref), (2 - core, k_prev_other_ref), (1 + core, k_prev_own_ref)):
        if ref is k_prev_own_ref:
            k_copy.wait()
        tile = ref[...]
        at = place * half if isinstance(place, int) else pl.multiple_of(place * half, half)
        row = place * ROWS if isinstance(place, int) else pl.multiple_of(place * ROWS, ROWS)
        keys[pl.ds(at, half), :] = tile
        for g, pooled in enumerate(pool_keys(tile)):
            pooled_key[g, pl.ds(row, ROWS), :] = pooled
    for g in range(KV_HERE):
        pooled_key[g, SPAN:SPAN + CHIP_BLOCKS, :] = near_key[g]
    slot_max[...] = max_ref[...]
    slot_sum[...] = sum_ref[...]
    shares[...] = jnp.zeros_like(shares)
    hits[...] = jnp.zeros_like(hits)
    filled = make_work(far_list, far_work, FAR_UNROLL)
    slot_loop(
        filled, far_work, FAR_UNROLL, far_list,
        lambda s, row: jnp.where(row <= SPAN, position(core, s) + row, 0),
        keys, queries, slot_max, slot_sum, False,
    )

    live = lax.broadcasted_iota(jnp.int32, (SLOT_ROWS, WIDTH), 0) <= SPAN
    spread = jnp.where(
        lax.broadcasted_iota(jnp.int32, (WIDTH, LANES), 0) // BLOCK
        == lax.broadcasted_iota(jnp.int32, (WIDTH, LANES), 1) // CHIP_BLOCKS,
        1.0 / BLOCK, 0.0,
    ).astype(jnp.bfloat16)
    lane_block = lax.broadcasted_iota(jnp.int32, (SLOT_ROWS, LANES), 1) % CHIP_BLOCKS

    @pl.loop(0, CHIP_BLOCKS // 4)
    def _(step):
        found = []
        for e in range(4):
            s = step * 4 + e
            for g in range(KV_HERE):
                tops = jnp.where(live, slot_max[s * KV_HERE + g], LOW)
                top = jnp.max(tops, axis=0, keepdims=True)
                weight = jnp.where(
                    live, slot_sum[s * KV_HERE + g] * jnp.exp2((tops - top) * EXP_SCALE), 0.0
                )
                share = weight / jnp.sum(weight, axis=0, keepdims=True)
                coarse = share.astype(jnp.bfloat16)
                fine = (share - coarse.astype(jnp.float32)).astype(jnp.bfloat16)
                mean = (
                    jnp.dot(coarse, spread, preferred_element_type=jnp.float32)
                    + jnp.dot(fine, spread, preferred_element_type=jnp.float32)
                )
                found.append((shares.at[g], position(core, s), jnp.where(lane_block == s, mean, 0.0)))
                if g == 0:
                    filled = jnp.where(tops > 0.5 * LOW, 1.0, 0.0).astype(jnp.bfloat16)
                    hit = jnp.dot(filled, spread, preferred_element_type=jnp.float32)
                    found.append((hits, position(core, s), jnp.where(lane_block == s, hit, 0.0)))
        for table, block, mine in found:
            table[pl.ds(block, SLOT_ROWS), :] += mine

    scale = 1.0 / math.sqrt(HEAD_DIM)
    window = SPAN + CHIP_BLOCKS
    usable = hits[0:window, :] > 0.5
    divergence = jnp.zeros((1, LANES), jnp.float32)
    key_base = CHIP_BLOCKS + ROWS
    for g in range(KV_HERE):
        far_gate_key = dot_f32(pooled_key[g, 0:SPAN, :], wk_ref[g], ((1,), (0,)))
        gate_key = jnp.concatenate([far_gate_key, near_gate_key[g]], axis=0)
        logits = dot_f32(gate_key, gate_query[g], ((1,), (1,))) * scale
        logits = jnp.where(usable, logits, LOW)
        top = jnp.max(logits, axis=0, keepdims=True)
        weight = jnp.where(usable, jnp.exp(logits - top), 0.0)
        mass = jnp.sum(weight, axis=0, keepdims=True)
        log_gate = jnp.where(usable, logits - top - jnp.log(mass), 0.0)
        target = shares[g, 0:window, :]
        log_target = jnp.log(jnp.where(target > 0.0, target, 1.0))
        terms = jnp.where(usable, target * (log_target - log_gate), 0.0)
        divergence += jnp.sum(terms, axis=0, keepdims=True)
        target = jnp.where(usable, target, 0.0)
        slope = (weight / mass) * jnp.sum(target, axis=0, keepdims=True) - target
        slope = slope * (scale / 32.0)
        d_query = dot_f32(slope, gate_key, ((0,), (0,)))
        d_key = dot_f32(slope, gate_query[g], ((1,), (0,)))
        for r in range(GROUP):
            at = r * CHIP_BLOCKS
            pooled = pooled_query[g, at:at + CHIP_BLOCKS, :]
            for part in range(2):
                share = (g * GROUP + r) * 2 + part
                cols = slice(part * HALF_HEAD, (part + 1) * HALF_HEAD)
                out_ref[share, 0:CHIP_BLOCKS, :] = d_query[at:at + CHIP_BLOCKS, :]
                out_ref[share, CHIP_BLOCKS:key_base, :] = jnp.concatenate(
                    [pooled[0:ROWS, cols], pooled[ROWS:CHIP_BLOCKS, cols]], axis=1
                )
        key_part = dot_f32(pooled_key[g], d_key, ((0,), (0,)))
        for i in range(SHARES // KV_HERE):
            out_ref[g * (SHARES // KV_HERE) + i, key_base:key_base + KEY_ROWS, :] = (
                key_part[i * KEY_ROWS:(i + 1) * KEY_ROWS, :]
            )
    total = jnp.sum(divergence)
    for i in range(SHARES):
        out_ref[i, PART_ROWS - 8:PART_ROWS, :] = jnp.full((8, HEAD_DIM), total, jnp.float32)


def sum_kernel(parts_ref, out_ref):
    parts = parts_ref[...]
    pooled = parts[:, CHIP_BLOCKS:CHIP_BLOCKS + ROWS, :].reshape(SHARES * ROWS, HEAD_DIM)
    early = parts[:, 0:ROWS, :].reshape(SHARES * ROWS, HEAD_DIM)
    late = parts[:, ROWS:CHIP_BLOCKS, :].reshape(SHARES * ROWS, HEAD_DIM)
    out_ref[0:HALF_HEAD, :] = (
        dot_f32(pooled[:, :HALF_HEAD], early, ((0,), (0,)))
        + dot_f32(pooled[:, HALF_HEAD:], late, ((0,), (0,)))
    )
    out_ref[HALF_HEAD:, :] = jnp.sum(parts[:, CHIP_BLOCKS + ROWS:, :], axis=0)


def pack_kernel(own_ref, one_ref, two_ref, three_ref, out_ref, total_ref):
    got = (own_ref[...] + one_ref[...]) + (two_ref[...] + three_ref[...])
    total_ref[...] = got[SUM_ROWS:, :]
    coded = []
    powers = jnp.zeros((TILE, HEAD_DIM), jnp.float32)
    row = lax.broadcasted_iota(jnp.int32, (TILE, HEAD_DIM), 0)
    for tile in range(SUM_ROWS // TILE):
        value = got[tile * TILE:(tile + 1) * TILE, :]
        top = jnp.max(jnp.abs(value), axis=0, keepdims=True)
        power = jnp.clip(jnp.ceil(jnp.log2(jnp.maximum(top, 1e-35))), -110.0, 110.0)
        level = jnp.clip(jnp.round(value * jnp.exp2(-power) * LEVELS), -32767.0, 32767.0)
        coded.append(level.astype(jnp.int32).astype(jnp.int16))
        powers = jnp.where(row == tile, power, powers)
    coded.append(powers.astype(jnp.int32).astype(jnp.int16))
    coded = jnp.concatenate(coded, axis=0)
    for i in range(SHARES):
        out_ref[i] = coded


def unpack_kernel(place_ref, mine_ref, other_ref, query_ref, key_ref):
    core = place_ref[0]
    for source, ref in ((core, mine_ref), (1 - core, other_ref)):
        for share in range(STEP_SHARES):
            powers = ref[share, SUM_ROWS:SUM_ROWS + TILE, :].astype(jnp.int32).astype(jnp.float32)
            scale = jnp.exp2(powers[0:8, :]) * (1.0 / LEVELS)
            for tile in range(SUM_ROWS // TILE):
                coded = ref[share, tile * TILE:(tile + 1) * TILE, :]
                value = coded.astype(jnp.int32).astype(jnp.float32) * scale[tile:tile + 1, :]
                if tile < HALF_HEAD // TILE:
                    query_ref[source, pl.ds(share * HALF_HEAD + tile * TILE, TILE), :] = value
                else:
                    at = share * KEY_ROWS + tile * TILE - HALF_HEAD
                    key_ref[source, pl.ds(at, TILE), :] = value


def pack(*parts):
    return pl.pallas_call(
        pack_kernel,
        out_shape=[
            shaped((SHARES, SUM_ROWS + TILE, HEAD_DIM), jnp.int16), shaped((8, HEAD_DIM)),
        ],
        name="pack",
    )(*parts)


def unpack(place, mine, other):
    rows = HALF_HEAD, KEY_ROWS
    return pl.pallas_call(
        unpack_kernel,
        grid_spec=pltpu.PrefetchScalarGridSpec(
            num_scalar_prefetch=1,
            grid=(SHARES // STEP_SHARES,),
            in_specs=[
                pl.BlockSpec((STEP_SHARES, SUM_ROWS + TILE, HEAD_DIM), lambda i, c: (i, 0, 0))
            ] * 2,
            out_specs=[
                pl.BlockSpec((2, STEP_SHARES * n, HEAD_DIM), lambda i, c: (0, i, 0)) for n in rows
            ],
        ),
        out_shape=[shaped((2, SHARES * n, HEAD_DIM)) for n in rows],
        name="unpack",
    )(place, mine, other)


def swap(x, axis):
    return lax.ppermute(x, axis, [(0, 1), (1, 0)])


def whole(*shape):
    return pl.BlockSpec(shape, lambda i, *_: (0,) * len(shape))


def shaped(shape, dtype=jnp.float32):
    return jax.ShapeDtypeStruct(shape, dtype)


def smem():
    return pl.BlockSpec(memory_space=pltpu.SMEM)


def cut_prev_kernel(place_ref, keys_hbm, after_ref, give_ref, sems):
    cols = pl.ds(pl.multiple_of((1 - place_ref[0]) * K_COLS, K_COLS), K_COLS)
    give = pltpu.make_async_copy(keys_hbm.at[:, cols], give_ref, sems.at[0])
    give.start()
    give.wait()


def cut_prev(place, keys, after):
    half = ROWS * BLOCK
    return pl.pallas_call(
        cut_prev_kernel,
        grid_spec=pltpu.PrefetchScalarGridSpec(
            num_scalar_prefetch=1,
            grid=(1,),
            in_specs=[
                pl.BlockSpec(memory_space=pltpu.HBM),
                pl.BlockSpec(memory_space=pl.ANY),
            ],
            out_specs=whole(half, K_COLS),
            scratch_shapes=[pltpu.SemaphoreType.DMA((1,))],
        ),
        out_shape=shaped((half, K_COLS), jnp.bfloat16),
        compiler_params=pltpu.CompilerParams(vmem_limit_bytes=4 * 1024 * 1024),
        name="cut_prev",
    )(place, keys, after)


def near_call(place, tables, q_own, q_other, k_mine, k_other, wq, wk):
    half = ROWS * BLOCK
    outs = [
        shaped((CHIP_BLOCKS * KV_HERE, WIDTH, HEAD_DIM), jnp.bfloat16),
        shaped((CHIP_BLOCKS * KV_HERE, SLOT_ROWS, WIDTH)),
        shaped((CHIP_BLOCKS * KV_HERE, SLOT_ROWS, WIDTH)),
        shaped((KV_HERE, LANES, HEAD_DIM)),
        shaped((KV_HERE, LANES, HEAD_DIM)),
        shaped((KV_HERE, CHIP_BLOCKS, POOL)),
        shaped((KV_HERE, CHIP_BLOCKS, HEAD_DIM)),
        shaped((CHIP_BLOCKS, HEAD_DIM), jnp.int32),
    ]
    return pl.pallas_call(
        near_kernel,
        grid_spec=pltpu.PrefetchScalarGridSpec(
            num_scalar_prefetch=1,
            grid=(1,),
            in_specs=[whole(ROWS, CAND), smem()] * 2 + [pl.BlockSpec(memory_space=pltpu.HBM)] * 6,
            out_specs=[whole(*o.shape) for o in outs],
            scratch_shapes=[
                pltpu.VMEM((CHIP_BLOCKS * BLOCK, K_COLS), jnp.bfloat16),
                pltpu.VMEM((CHIP_BLOCKS, HEAD_DIM), jnp.int32),
                pltpu.SMEM((CHIP_BLOCKS, HEAD_DIM), jnp.int32),
                pltpu.SMEM((WORK_SIZE,), jnp.int32),
                pltpu.VMEM((half, Q_COLS), jnp.bfloat16),
                pltpu.VMEM((half, Q_COLS), jnp.bfloat16),
                pltpu.VMEM((half, K_COLS), jnp.bfloat16),
                pltpu.VMEM((half, K_COLS), jnp.bfloat16),
                pltpu.VMEM((HEADS_HERE, HEAD_DIM, HEAD_DIM), jnp.float32),
                pltpu.VMEM((KV_HERE, POOL, HEAD_DIM), jnp.float32),
                pltpu.SemaphoreType.DMA((7,)),
            ],
        ),
        out_shape=outs,
        compiler_params=pltpu.CompilerParams(vmem_limit_bytes=VMEM_BYTES),
        cost_estimate=pl.CostEstimate(
            flops=2_000_000_000, bytes_accessed=8_000_000, transcendentals=8_000_000
        ),
        name="near",
    )(place, *tables, q_own, q_other, k_mine, k_other, wq, wk)


def far_call(place, k_prev_own, k_prev_other, k_far, near, wk):
    half = ROWS * BLOCK
    args = (k_prev_own, k_prev_other, k_far, *near[:-1])
    return pl.pallas_call(
        far_kernel,
        grid_spec=pltpu.PrefetchScalarGridSpec(
            num_scalar_prefetch=1,
            grid=(1,),
            in_specs=[smem(), pl.BlockSpec(memory_space=pltpu.HBM)]
            + [whole(*a.shape) for a in args[1:]] + [
                pl.BlockSpec((KV_HERE, POOL, HEAD_DIM), lambda i, c: (c[0], 0, 0)),
            ],
            out_specs=whole(SHARES, PART_ROWS, HEAD_DIM),
            scratch_shapes=[
                pltpu.VMEM((SPAN * BLOCK, K_COLS), jnp.bfloat16),
                pltpu.VMEM((CHIP_BLOCKS * KV_HERE, SLOT_ROWS, WIDTH), jnp.float32),
                pltpu.VMEM((CHIP_BLOCKS * KV_HERE, SLOT_ROWS, WIDTH), jnp.float32),
                pltpu.VMEM((KV_HERE, SPAN + CHIP_BLOCKS, POOL), jnp.float32),
                pltpu.VMEM((KV_HERE, PADDED, LANES), jnp.float32),
                pltpu.VMEM((PADDED, LANES), jnp.float32),
                pltpu.SMEM((WORK_SIZE,), jnp.int32),
                pltpu.VMEM((half, K_COLS), jnp.bfloat16),
                pltpu.SemaphoreType.DMA((1,)),
            ],
        ),
        out_shape=shaped((SHARES, PART_ROWS, HEAD_DIM)),
        compiler_params=pltpu.CompilerParams(vmem_limit_bytes=VMEM_BYTES),
        cost_estimate=pl.CostEstimate(
            flops=2_000_000_000, bytes_accessed=8_000_000, transcendentals=8_000_000
        ),
        name="far",
    )(place, near[-1], *args, wk)


def body(
    teacher_queries, teacher_keys, query_projection, key_projection, block_offsets, valid_counts
):
    chips = ("za", "zb", "yh", "x")
    places = chips + ("core",)
    count = lax.axis_size(places)
    core = lax.axis_index("core")
    place = jnp.stack([core, lax.axis_index(chips)]).astype(jnp.int32)

    columns = lambda x, which: lax.dynamic_slice_in_dim(x, which * K_COLS, K_COLS, 1)
    k_prev = lax.ppermute(teacher_keys, places, [(i, i + 2) for i in range(count - 2)])
    k_other = swap(teacher_keys, "core")
    q_other = swap(teacher_queries, "core")
    tables = (block_offsets, valid_counts, swap(block_offsets, "core"), swap(valid_counts, "core"))
    k_far = lax.ppermute(
        jnp.where(core == 1, columns(teacher_keys, core), columns(k_other, core)),
        places, [(i, i + 4) for i in range(count - 4)],
    )
    near = near_call(
        place, tables, teacher_queries, q_other, teacher_keys, k_other,
        query_projection, key_projection,
    )
    k_prev_other = swap(cut_prev(place, k_prev, near[-1]), "core")
    parts = far_call(place, k_prev, k_prev_other, k_far, near, key_projection)

    group = ("zb", "yh", "x")
    got = lax.all_to_all(parts, group, 0, 0)
    got = pl.pallas_call(sum_kernel, out_shape=shaped((SUM_ROWS + 8, HEAD_DIM)), name="sum")(got)
    one, two, three = (
        lax.ppermute(got, "za", [(i, i ^ step) for i in range(4)]) for step in (1, 2, 3)
    )
    coded, total = pack(got, one, two, three)
    across = lax.ppermute(total, ("core", "head"), [(i, 3 - i) for i in range(4)])
    total = (total + swap(total, "head")) + (swap(total, "core") + across)
    mine = lax.all_to_all(coded, group, 0, 0)
    query_gradient, key_gradient = unpack(place, mine, swap(mine, "core"))
    return (
        query_gradient.reshape(2 * HEADS_HERE, HEAD_DIM, HEAD_DIM),
        key_gradient.reshape(2 * KV_HERE, POOL, HEAD_DIM),
        total[0, 0] / (1024 * HEADS),
    )


def solution(mesh):
    split = Mesh(mesh.devices.reshape(4, 2, 2, 4, 2, 2), ("za", "zb", "yh", "x", "core", "head"))
    ctx = ("za", "zb", "yh", "x", "core")
    placed = (
        P(ctx, "head"),
        P(ctx, "head"),
        P("head", None, None),
        P("head", None, None),
        P(ctx, None),
        P(ctx),
    )
    return jax.shard_map(
        body,
        mesh=split,
        in_specs=placed,
        out_specs=(P("head", None, None), P("head", None, None), P()),
        check_vma=False,
    )
```
